128 devices in a mesh: seq: 8 (over z_hi, x), exp: 16 (over z_lo, y, core).
Axes of the slice: x: 4, y: 4, z: 4 (z_hi: 2, z_lo: 2; z = z_hi * 2 + z_lo), core: 2. Of those that a mesh axis runs over, the one named last changes fastest.
Arguments:
- tokens: bfloat16 [16, 2048, 768], P('exp', 'seq'), may hold values from -6 to 6
- cotangent: bfloat16 [16, 2048, 768], P('exp', 'seq'), may hold values from -6 to 6
- gain_first: float32 [768], replicated, may hold values from 0.1 to 1.9
- w_qkv: bfloat16 [768, 2304], replicated, may hold values from -0.21875 to 0.21875
- w_o: bfloat16 [768, 768], replicated, may hold values from -1.75 to 1.75
- gain_second: float32 [768], replicated, may hold values from 0.1 to 1.9
- w_gate: bfloat16 [768, 32], replicated, may hold values from -0.15625 to 0.15625
- w_in: bfloat16 [32, 768, 3072], P('exp', None, 'seq'), may hold values from -0.21875 to 0.21875
- w_out: bfloat16 [32, 3072, 768], P('exp', 'seq'), may hold values from -0.109375 to 0.109375
- routes: int32 [16, 2048, 2], P('exp', 'seq'), may hold values from 0 to 31, all different within a row; in each aligned block of 256 rows (0 to 255, 256 to 511, ..., all dimensions but the last counted through in order) at most 32 rows name the same one
- frozen: int32 [32], replicated, may hold values from 0 to 1, as said below
Outputs:
- out: bfloat16 [16, 2048, 768], P('exp', 'seq')
- tokens_grad: float32 [16, 2048, 768], P('exp', 'seq')
- gain_first_grad: float32 [768], replicated
- qkv_grad: float32 [768, 2304], replicated
- o_grad: float32 [768, 768], replicated
- gain_second_grad: float32 [768], replicated
- gate_grad: float32 [768, 32], replicated
- w_in_grad: float32 [32, 768, 3072], P('exp', None, 'seq')
- w_out_grad: float32 [32, 3072, 768], P('exp', 'seq')
The draws below stay inside these ranges and needn't reach their ends.
Inputs may be any that keep to these rules, and one draw needn't show every extreme that they name: `routes`: A token's two experts differ. In each aligned block of 256 positions of a sequence no expert is named more than 32 times, and in some block some expert exactly 32 times; every expert is named somewhere. Half of the 32 experts are frozen.
All inputs are finite; a program needn't handle non-finite values.
Results may differ from the reference program's by a relative error of at most 0.015.
Values may be sent and summed in bfloat16 or wider, within the bound.
A program may use at most 256 MiB of HBM per device.

```python
import math
import jax
import jax.numpy as jnp
import numpy as np
from jax import lax

D = 768
HEADS = 12
HEAD_DIM = 64
FF = 3072
EXPERTS = 32
LEN_DEV = 256
CAP = 32
LEN = 2048
SEQS = 16


def draw_frozen(key, part):
    key = jax.random.fold_in(key, 7)
    order = jax.random.permutation(key, EXPERTS)
    return (order < EXPERTS // 2).astype(jnp.int32)


def block_levels(stream_key, dims, shards, least, top_value):
    level = 1.0
    for dim, blocks in shards:
        draws = jax.random.uniform(jax.random.fold_in(jax.random.fold_in(stream_key, 6), dim), (blocks,), jnp.float32, least / len(shards), top_value / len(shards))
        level = level * jnp.repeat(jnp.exp(draws), dims[dim] // blocks).reshape((-1,) + (1,) * (len(dims) - 1 - dim))
    return level


def deal_out(own_key, own, number, rows, count, top, bound, lean):
    order = jax.random.permutation(own_key, count)
    heavy_load, common = portions_of(count, rows * top, bound, lean, True), portions_of(count, rows * top, bound, lean, False)
    places = jnp.arange(count)

    def named(sizes, rotation):
        used = int((sizes > 0).sum())
        fixed = max(1, used // 4)
        moved = fixed + (places - fixed + rotation * (used - fixed)) % max(1, count - fixed)
        return jnp.zeros((count,), jnp.int32).at[order[jnp.where(places < fixed, places, moved)]].set(jnp.asarray(sizes, jnp.int32))

    sizes = jnp.where(number % 4 == 0, named(heavy_load, number // 4), named(common, number - number // 4 - 1))
    mixed = jax.random.permutation(jax.random.fold_in(own, 3), count)
    donor, receiver = mixed[0:count // 2 * 2:2], mixed[1:count // 2 * 2:2]
    slack = jnp.minimum(sizes[donor] - 1, bound - sizes[receiver]) // 2
    slack = jnp.where((donor == order[0]) | (receiver == order[0]) | (sizes[receiver] == 0), 0, jnp.maximum(slack, 0))
    moved = jax.random.randint(jax.random.fold_in(own, 4), (count // 2,), 0, 1 << 20) % (slack + 1)
    sizes = sizes.at[donor].add(-moved).at[receiver].add(moved)
    members = jnp.searchsorted(jnp.cumsum(sizes), jnp.arange(rows * top), side="right").astype(jnp.int32)
    table = members.reshape(top, rows).T
    table = table[jax.random.permutation(jax.random.fold_in(own, 1), rows)]
    rotation = jax.random.randint(jax.random.fold_in(own, 2), (rows, 1), 0, top)
    return jnp.take_along_axis(table, (jnp.arange(top)[None, :] + rotation) % top, axis=1)


def portions_of(count, total, bound, skew, full):
    loads = [(1 << 20) // math.isqrt(rank ** skew) + 1 for rank in range(1, count + 1)]
    largest = bound if full else min(bound, max(-(-total // count), total * loads[0] // sum(loads)))
    least = 1 if total - largest >= count - 1 else 0
    holding, surplus = [largest] + [least] * (count - 1), total - largest - least * (count - 1)
    while surplus > 0:
        candidates = [i for i in range(1, count) if holding[i] < largest] or [i for i in range(1, count) if holding[i] < bound]
        whole, budget = sum([loads[i] for i in candidates]), surplus
        for i in candidates:
            more = min(bound - holding[i], max(1, budget * loads[i] // whole), surplus)
            holding[i] = holding[i] + more
            surplus = surplus - more
    return np.array(holding)


def bell_draw(stream_key, extent, scale, limit, cuts=(), kind=jnp.bfloat16):
    values = jax.random.normal(stream_key, extent, jnp.float32) * scale
    if len(cuts) > 0:
        values = block_levels(stream_key, extent, cuts, -0.22, 0.18) * values
    return jnp.clip(values, min=-limit, max=limit).astype(kind)


def setup_inputs(seed: int = 0) -> dict:
    keys = jax.random.split(jax.random.key(seed), 12)
    tokens = bell_draw(keys[0], (SEQS, LEN, D), 1.0, 6.0, ((0, 16), (1, 8)))
    cotangent = bell_draw(keys[1], (SEQS, LEN, D), 1.0, 6.0, ((0, 16), (1, 8)))
    gain_first = jnp.clip(1.0 + 0.18 * jax.random.normal(keys[2], (D,), jnp.float32), 0.1, 1.9)
    w_qkv = bell_draw(keys[3], (D, 3 * D), D ** -0.5, 0.21875)
    w_o = bell_draw(keys[4], (D, D), (D // 64) ** -0.5, 1.75)
    gain_second = jnp.clip(1.0 + 0.18 * jax.random.normal(keys[5], (D,), jnp.float32), 0.1, 1.9)
    w_gate = bell_draw(keys[6], (D, EXPERTS), (2 * D) ** -0.5, 0.15625)
    w_in = bell_draw(keys[7], (EXPERTS, D, FF), D ** -0.5, 0.21875, ((0, 16), (2, 8)))
    w_out = bell_draw(keys[8], (EXPERTS, FF, D), FF ** -0.5, 0.109375, ((0, 16), (1, 8)))
    routes_keys = jax.random.split(jax.random.fold_in(keys[9], 1), SEQS * LEN // LEN_DEV)
    routes_turns = jax.random.permutation(jax.random.fold_in(keys[9], 3), SEQS * LEN // LEN_DEV)
    routes = jax.vmap(lambda own, number: deal_out(jax.random.fold_in(keys[9], 2), own, number, LEN_DEV, EXPERTS, 2, CAP, 2))(routes_keys, routes_turns).reshape((SEQS, LEN, 2))
    frozen = draw_frozen(jax.random.fold_in(keys[11], 71), 0)
    return dict(tokens=tokens, cotangent=cotangent, gain_first=gain_first, w_qkv=w_qkv, w_o=w_o, gain_second=gain_second, w_gate=w_gate, w_in=w_in, w_out=w_out, routes=routes, frozen=frozen)


exact_mode = lax.Precision.HIGHEST

@jax.custom_vjp
def low(v):
    return lax.optimization_barrier(v.astype(jnp.bfloat16)).astype(jnp.float32)

@jax.custom_vjp
def low_back(v):
    return v

def low_keep(v):
    return (low(v), None)

def low_pass(kept, grad):
    return (grad,)

def back_keep(v):
    return (v, None)

def back_low(kept, grad):
    return (low(grad),)
low.defvjp(low_keep, low_pass)
low_back.defvjp(back_keep, back_low)

def round_both(values):
    return low_back(low(values))

def layer_norm(values, gain_vec):
    centred = values - lax.optimization_barrier(jnp.mean(values, axis=-1, keepdims=True))
    return centred * lax.rsqrt(lax.optimization_barrier(jnp.mean(centred * centred, axis=-1, keepdims=True)) + 1e-05) * gain_vec

def attend_heads(operands):
    asking_token_vectors, key_matrix_rows, value_matrix_rows = operands
    length = asking_token_vectors.shape[0]
    scores = jnp.einsum('qhd,khd->hqk', asking_token_vectors, key_matrix_rows, precision=exact_mode) * HEAD_DIM ** (-0.5)
    scores = low_back(scores)
    position = jnp.arange(length, dtype=jnp.int32)
    allowed = position[:, None] >= position[None, :]
    scores = jnp.where(allowed[None], scores, -1e+30)
    weight_params = low(jax.nn.softmax(scores, axis=-1))
    return jnp.einsum('hqk,khd->qhd', weight_params, value_matrix_rows, precision=exact_mode)

def expert_rows(operands):
    rows_in, first_weight, second_weight = operands
    pre_act = low_back(jnp.dot(rows_in, first_weight, precision=exact_mode, preferred_element_type=jnp.float32))
    hidden = low(jax.nn.gelu(pre_act, approximate=False))
    return jnp.dot(hidden, second_weight, precision=exact_mode, preferred_element_type=jnp.float32)

def slot_places(routes):
    blocks = routes.reshape(-1, LEN_DEV * 2)
    matches = (blocks[..., None] == jnp.arange(EXPERTS, dtype=jnp.int32)).astype(jnp.int32)
    earlier = jnp.cumsum(matches, axis=1) - matches
    slot_number = lax.optimization_barrier(jnp.sum(earlier * matches, axis=-1))
    block_ids = jnp.arange(blocks.shape[0], dtype=jnp.int32)[:, None]
    slot_rows = (block_ids * CAP + slot_number).astype(jnp.int32)
    return (blocks.reshape(-1), slot_rows.reshape(-1))

def reference(tokens, cotangent, gain_first, w_qkv, w_o, gain_second, w_gate, w_in, w_out, routes, frozen):
    expert_ids, slot_rows = slot_places(routes)
    block_count = routes.shape[0] * routes.shape[1] // LEN_DEV

    def forward_pass(inputs, gain_one, qkv_weight, out_weight, gain_two, gate_weight, first_weights, second_weights):
        seq_count, length, model_width = inputs.shape
        acts_one = low(layer_norm(inputs, gain_one))
        joined = jnp.einsum('bld,de->ble', acts_one, qkv_weight, precision=exact_mode)

        def to_heads(section):
            return round_both(section).reshape(seq_count, length, HEADS, HEAD_DIM)
        asking_token_vectors = to_heads(joined[..., :model_width])
        key_matrix_rows = to_heads(joined[..., model_width:2 * model_width])
        value_matrix_rows = to_heads(joined[..., 2 * model_width:])
        attended = lax.map(jax.checkpoint(attend_heads), (asking_token_vectors, key_matrix_rows, value_matrix_rows))
        attended = round_both(attended.reshape(seq_count, length, model_width))
        mid = inputs + low_back(jnp.einsum('bld,de->ble', attended, out_weight, precision=exact_mode))
        acts_two = low(layer_norm(mid, gain_two))
        logits = jnp.einsum('bld,de->ble', acts_two, gate_weight, precision=exact_mode)
        gates = jax.nn.softmax(jnp.take_along_axis(logits, routes, axis=-1), axis=-1)
        duplicated_copies = jnp.broadcast_to(acts_two[:, :, None, :], (seq_count, length, 2, model_width)).reshape(-1, model_width)
        buffer = jnp.zeros((EXPERTS, block_count * CAP, model_width), jnp.float32)
        buffer = low_back(buffer.at[expert_ids, slot_rows].set(duplicated_copies))
        produced = round_both(lax.map(jax.checkpoint(expert_rows), (buffer, first_weights, second_weights)))
        picked = produced[expert_ids, slot_rows].reshape(seq_count, length, 2, model_width)
        return mid + lax.optimization_barrier(jnp.sum(gates[..., None] * picked, axis=2))
    result, pullback = jax.vjp(forward_pass, tokens.astype(jnp.float32), gain_first, w_qkv.astype(jnp.float32), w_o.astype(jnp.float32), gain_second, w_gate.astype(jnp.float32), w_in.astype(jnp.float32), w_out.astype(jnp.float32))
    grads = pullback(cotangent.astype(jnp.float32))
    keep_mask = (1 - frozen).astype(jnp.float32)
    return (result.astype(jnp.bfloat16), grads[0], grads[1], grads[2], grads[3], grads[4], grads[5] * keep_mask[None, :], grads[6] * keep_mask[:, None, None], grads[7] * keep_mask[:, None, None])
```

```python
import functools
import math

import jax
import jax.numpy as jnp
from jax import lax
from jax.experimental import pallas as pl
from jax.experimental.pallas import tpu as pltpu
from jax.sharding import Mesh
from jax.sharding import PartitionSpec as P

D = 768
HEADS = 12
HEAD_DIM = 64
EXPERTS = 32
CAP = 32
ROWS = 256
BLOCKS = 8
FF = 3072
SLOTS = EXPERTS * CAP
EXTRA = 128
EPS = 1e-5
SCALE = HEAD_DIM ** -0.5
LOG2E = math.log2(math.e)
BF16 = jnp.bfloat16
F32 = jnp.float32
NEG = -1e30

SEQ = ("zh", "x")
GROUP = ("zh", "zl", "y", "c")
ALL = ("zh", "x", "zl", "y", "c")


def dot(a, b, ca=1, cb=0):
    return lax.dot_general(a, b, (((ca,), (cb,)), ((), ())), preferred_element_type=F32)


def params(mb=56):
    return pltpu.CompilerParams(vmem_limit_bytes=mb * 2**20)


def vspec(n):
    return [pl.BlockSpec(memory_space=pltpu.VMEM)] * n


def call(body, outs, n_in, scratch=(), **kw):
    return pl.pallas_call(
        body,
        out_shape=[jax.ShapeDtypeStruct(s, t) for s, t in outs],
        in_specs=vspec(n_in),
        out_specs=vspec(len(outs)),
        scratch_shapes=list(scratch),
        compiler_params=params(),
        **kw,
    )


def norm(v):
    mean = jnp.mean(v, axis=-1, keepdims=True)
    centred = v - mean
    inv = lax.rsqrt(jnp.mean(centred * centred, axis=-1, keepdims=True) + EPS)
    return centred * inv, inv


def norm_back(grad, gain, unit, inv):
    t = grad * gain
    m1 = jnp.mean(t, axis=-1, keepdims=True)
    m2 = jnp.mean(t * unit, axis=-1, keepdims=True)
    return inv * (t - m1 - unit * m2)


def lane_low():
    return lax.broadcasted_iota(jnp.int32, (1, 128), 1) < 64


def pair_up(wide, s):
    low = wide[:, 128 * (s // 2) : 128 * (s // 2) + 128]
    if s % 2:
        low = pltpu.roll(low, 64, 1)
    high = wide[:, 512 + 128 * (s // 4) : 640 + 128 * (s // 4)]
    if (s // 2) % 2 == 0:
        high = pltpu.roll(high, 64, 1)
    return jnp.where(lane_low(), low, high)


def unpair(tiles):
    out = []
    for t in range(4):
        out.append(
            jnp.where(lane_low(), tiles[2 * t], pltpu.roll(tiles[2 * t + 1], 64, 1))
        )
    for t in range(2):
        a = tiles[4 * t] + tiles[4 * t + 1]
        b = tiles[4 * t + 2] + tiles[4 * t + 3]
        out.append(jnp.where(lane_low(), pltpu.roll(a, 64, 1), b))
    return out


def project_body(tok_ref, gain_ref, w_ref, send_ref):
    unit, _ = norm(tok_ref[...].astype(F32))
    a1 = (unit * gain_ref[...]).astype(BF16)
    for part in range(3):
        wide = dot(a1, w_ref[:, part * D : part * D + D])
        for s in range(BLOCKS):
            send_ref[s, :, part * 128 : part * 128 + 128] = pair_up(wide, s).astype(
                BF16
            )


def unit_list(half):
    units = [(0, i, i + 1, i, i) for i in range(BLOCKS)]
    firsts = [(0, 1), (3, 2), (4, 5), (7, 6)]
    for t, (a, b) in enumerate(firsts):
        units.append((1, a + half * (b - a), 2 * t + 2, 2 * t, BLOCKS + t))
    return units


def masked_scores(k, q, block, first, count):
    s = dot(k, q, 1, 1)
    start = first * ROWS
    tail = (count - first) * ROWS
    keys = lax.broadcasted_iota(jnp.int32, (tail, ROWS), 0) + start
    queries = lax.broadcasted_iota(jnp.int32, (tail, ROWS), 1) + block * ROWS
    end = jnp.where(keys <= queries, s[start:], NEG)
    return end if start == 0 else jnp.concatenate([s[:start], end], axis=0)


def head_mask(h):
    low = lane_low()
    return (low if h == 0 else jnp.logical_not(low)).astype(F32).astype(BF16)


def attend_forward(half, qkv_ref, o_ref, ot_ref, lse_ref, vt_ref):
    c = SCALE * LOG2E
    for b in range(BLOCKS):
        vt_ref[:, b * ROWS : (b + 1) * ROWS] = qkv_ref[b, :, 256:384].T
        o_ref[b] = jnp.zeros((ROWS, 128), BF16)
    for h, block, count, first, u in unit_list(half):
        q = qkv_ref[block, :, 0:128] * head_mask(h)
        k = qkv_ref[0:count, :, 128:256].reshape(count * ROWS, 128)
        s = masked_scores(k, q, block, first, count)
        top = jnp.max(s, axis=0, keepdims=True)
        p = jnp.exp2((s - top) * c)
        total = jnp.sum(p, axis=0, keepdims=True)
        ot = dot(vt_ref[64 * h : 64 * h + 64, 0 : count * ROWS], p.astype(BF16))
        ot = ot / total
        ot_ref[u] = ot
        lse_ref[u] = jnp.broadcast_to(top * c + jnp.log2(total), (8, ROWS))
        wide = jnp.concatenate([ot, jnp.zeros_like(ot)] if h == 0 else [jnp.zeros_like(ot), ot], axis=0)
        o_ref[block] = (o_ref[block].astype(F32) + wide.T).astype(BF16)


def attend_backward(half, qkv_ref, do_ref, ot_ref, lse_ref, out_ref, kt_ref, dk_ref, dv_ref):
    c = SCALE * LOG2E
    for b in range(BLOCKS):
        kt_ref[:, b * ROWS : (b + 1) * ROWS] = qkv_ref[b, :, 128:256].T
        out_ref[b, :, 0:128] = jnp.zeros((ROWS, 128), BF16)
    dk_ref[...] = jnp.zeros_like(dk_ref)
    dv_ref[...] = jnp.zeros_like(dv_ref)
    for h, block, count, first, u in unit_list(half):
        rows = count * ROWS
        q = qkv_ref[block, :, 0:128] * head_mask(h)
        do = do_ref[block] * head_mask(h)
        dot_rows = do.astype(F32).T[64 * h : 64 * h + 64]
        delta = jnp.sum(dot_rows * ot_ref[u], axis=0, keepdims=True)
        lse = lse_ref[u][0:1]
        k = qkv_ref[0:count, :, 128:256].reshape(rows, 128)
        v = qkv_ref[0:count, :, 256:384].reshape(rows, 128)
        s = masked_scores(k, q, block, first, count)
        p = jnp.exp2(s * c - lse)
        dp = dot(v, do, 1, 1)
        ds = (p * (dp - delta)).astype(BF16)
        dv_ref[0:rows] += dot(p.astype(BF16), do)
        dk_ref[0:rows] += dot(ds, q)
        dqt = dot(kt_ref[64 * h : 64 * h + 64, 0:rows], ds) * SCALE
        wide = jnp.concatenate([dqt, jnp.zeros_like(dqt)] if h == 0 else [jnp.zeros_like(dqt), dqt], axis=0)
        out_ref[block, :, 0:128] = (
            out_ref[block, :, 0:128].astype(F32) + wide.T
        ).astype(BF16)
    for b in range(BLOCKS):
        at = slice(b * ROWS, (b + 1) * ROWS)
        out_ref[b, :, 128:256] = (dk_ref[at] * SCALE).astype(BF16)
        out_ref[b, :, 256:384] = dv_ref[at].astype(BF16)


def half_of(index):
    return (index + index // 2) % 2


def choices(routes):
    ids = lax.broadcasted_iota(jnp.int32, (ROWS, EXPERTS), 1)
    e1, e2 = routes[:, 0:1], routes[:, 1:2]
    m1, m2 = (e1 == ids).astype(F32), (e2 == ids).astype(F32)
    r = lax.broadcasted_iota(jnp.int32, (ROWS, ROWS), 0)
    k = lax.broadcasted_iota(jnp.int32, (ROWS, ROWS), 1)
    lower = (k < r).astype(F32).astype(BF16)
    earlier = dot(lower, (m1 + m2).astype(BF16))
    s1 = jnp.sum(earlier * m1, axis=1, keepdims=True)
    s2 = jnp.sum(earlier * m2, axis=1, keepdims=True)

    def column(e, s):
        place = (e % 2) * (EXPERTS // 2) + e // 2
        return (place * CAP).astype(F32) + s

    return m1, m2, column(e1, s1), column(e2, s2)


def chosen(col):
    at = lax.broadcasted_iota(jnp.int32, (ROWS, SLOTS), 1).astype(F32)
    return (at == col).astype(F32).astype(BF16)


def chosen_t(col):
    row = jnp.broadcast_to(col, (ROWS, 128)).T[0:1]
    at = lax.broadcasted_iota(jnp.int32, (SLOTS, ROWS), 0).astype(F32)
    return (at == row).astype(F32).astype(BF16)


def two_parts(v):
    lane = lax.broadcasted_iota(jnp.int32, (v.shape[0], EXTRA), 1)
    high = v.astype(BF16).astype(F32)
    return jnp.where(lane == 0, high, jnp.where(lane == 1, v - high, 0.0)).astype(BF16)


def from_parts(v):
    lane = lax.broadcasted_iota(jnp.int32, v.shape, 1)
    return jnp.sum(jnp.where(lane < 2, v.astype(F32), 0.0), axis=1, keepdims=True)


def deal_body(cot_ref, routes_ref, send_ref):
    _, _, c1, c2 = choices(routes_ref[...])
    either = chosen_t(c1) + chosen_t(c2)
    send_ref[...] = dot(either, cot_ref[...]).astype(BF16)


def middle_body(o_ref, tok_ref, w_o_ref, gain_ref, gate_ref, routes_ref, mid_ref, att_ref, send_ref, gates_ref):
    tiles = unpair([o_ref[s].astype(F32) for s in range(BLOCKS)])
    o = jnp.concatenate([t.astype(BF16) for t in tiles], axis=1)
    att_ref[...] = o
    mid = tok_ref[...].astype(F32) + dot(o, w_o_ref[...])
    mid_ref[...] = mid
    unit, _ = norm(mid)
    a2 = (unit * gain_ref[...]).astype(BF16)
    logits = dot(a2, gate_ref[...])
    m1, m2, c1, c2 = choices(routes_ref[...])
    l1 = jnp.sum(logits * m1, axis=1, keepdims=True)
    l2 = jnp.sum(logits * m2, axis=1, keepdims=True)
    top = jnp.maximum(l1, l2)
    x1, x2 = jnp.exp(l1 - top), jnp.exp(l2 - top)
    g1, g2 = x1 / (x1 + x2), x2 / (x1 + x2)
    lane = lax.broadcasted_iota(jnp.int32, (ROWS, 128), 1)
    gates_ref[...] = jnp.where(lane == 0, g1, g2)
    t1, t2 = chosen_t(c1), chosen_t(c2)
    send_ref[:, 0:D] = dot(t1 + t2, a2).astype(BF16)
    send_ref[:, D:] = (dot(t1, two_parts(g1)) + dot(t2, two_parts(g2))).astype(BF16)


def erf_parts(h):
    x = jnp.abs(h) * (0.5**0.5)
    t = 1.0 / (1.0 + 0.3275911 * x)
    e = jnp.exp(-0.5 * h * h)
    poly = t * (
        0.254829592
        + t * (-0.284496736 + t * (1.421413741 + t * (-1.453152027 + t * 1.061405429)))
    )
    tail = 0.5 * poly * e
    return jnp.where(h >= 0, 1.0 - tail, tail), e * (1.0 / math.sqrt(2.0 * math.pi))


STEP = 256


def expert_body(x_ref, c_ref, win_ref, wout_ref, ret_ref, y_ref, dwin_ref, dwout_ref, g_ref, dh_ref, dx_ref, ya_ref, dg_ref, xg_ref, cg_ref):
    i = pl.program_id(0)
    n = pl.num_programs(0)

    @pl.when(i == 0)
    def _():
        dx_ref[...] = jnp.zeros_like(dx_ref)
        ya_ref[...] = jnp.zeros_like(ya_ref)
        dg_ref[...] = jnp.zeros_like(dg_ref)

    w_in, w_out = win_ref[0], wout_ref[0]

    def rows(r, carry):
        at = pl.ds(pl.multiple_of(r * STEP, STEP), STEP)
        gate = from_parts(x_ref[at, D:])
        x, c = x_ref[at, 0:D], c_ref[at, :]

        @pl.when(i == 0)
        def _():
            xg_ref[at, :] = x
            cg_ref[at, :] = (gate * c.astype(F32)).astype(BF16)

        h = dot(x, w_in)
        cw = dot(cg_ref[at, :], w_out, 1, 1)
        phi, density = erf_parts(h)
        g = (h * phi).astype(BF16)
        dh = ((phi + h * density) * cw).astype(BF16)
        g_ref[at, :] = g
        dh_ref[at, :] = dh
        back = dot(dh, w_in, 1, 1)
        out = dot(g, w_out)
        dx_ref[at, :] += back
        ya_ref[at, :] += out
        return carry

    lax.fori_loop(0, SLOTS // STEP, rows, 0)
    dwin_ref[0] = dot(xg_ref[...], dh_ref[...], 0, 0).astype(BF16)
    dwout_ref[0] = dot(g_ref[...], cg_ref[...], 0, 0).astype(BF16)

    @pl.when(i == n - 1)
    def _():
        def finish(r, carry):
            at = pl.ds(pl.multiple_of(r * STEP, STEP), STEP)
            y = ya_ref[at, :].astype(BF16)
            y_ref[at, :] = y
            dgate = jnp.sum(
                c_ref[at, :].astype(F32) * y.astype(F32), axis=1, keepdims=True
            )
            ret_ref[at, 0:D] = dx_ref[at, :].astype(BF16)
            ret_ref[at, D:] = two_parts(dgate)
            return carry

        lax.fori_loop(0, SLOTS // STEP, finish, 0)


def experts(x, c, w_in, w_out):
    n, _, width = w_in.shape
    whole = lambda shape: pl.BlockSpec(shape, lambda i: (0,) * len(shape))
    return pl.pallas_call(
        expert_body,
        grid=(n,),
        out_shape=[
            jax.ShapeDtypeStruct((SLOTS, D + EXTRA), BF16),
            jax.ShapeDtypeStruct((SLOTS, D), BF16),
            jax.ShapeDtypeStruct((n, D, width), BF16),
            jax.ShapeDtypeStruct((n, width, D), BF16),
        ],
        in_specs=[
            whole((SLOTS, D + EXTRA)),
            whole((SLOTS, D)),
            pl.BlockSpec((1, D, width), lambda i: (i, 0, 0)),
            pl.BlockSpec((1, width, D), lambda i: (i, 0, 0)),
        ],
        out_specs=[
            whole((SLOTS, D + EXTRA)),
            whole((SLOTS, D)),
            pl.BlockSpec((1, D, width), lambda i: (i, 0, 0)),
            pl.BlockSpec((1, width, D), lambda i: (i, 0, 0)),
        ],
        scratch_shapes=[
            pltpu.VMEM((SLOTS, width), BF16),
            pltpu.VMEM((SLOTS, width), BF16),
            pltpu.VMEM((SLOTS, D), F32),
            pltpu.VMEM((SLOTS, D), F32),
            pltpu.VMEM((SLOTS, 128), F32),
            pltpu.VMEM((SLOTS, D), BF16),
            pltpu.VMEM((SLOTS, D), BF16),
        ],
        compiler_params=params(60),
    )(x, c, w_in, w_out)


def back_body(ret_ref, cot_ref, routes_ref, gates_ref, mid_ref, att_ref, gain_ref, gate_w_ref, w_o_ref,
              send_ref, dmid_ref, o_grad_ref, gate_grad_ref, gain_grad_ref):
    m1, m2, c1, c2 = choices(routes_ref[...])
    s1, s2 = chosen(c1), chosen(c2)
    g1, g2 = gates_ref[:, 0:1], gates_ref[:, 1:2]
    extra = ret_ref[:, D:]
    d1, d2 = from_parts(dot(s1, extra)), from_parts(dot(s2, extra))
    dl = g1 * g2 * (d1 - d2)
    dlogits = (m1 - m2) * dl
    unit, inv = norm(mid_ref[...])
    a2 = (unit * gain_ref[...]).astype(BF16)
    high = dlogits.astype(BF16)
    low = (dlogits - high.astype(F32)).astype(BF16)
    gate_grad_ref[...] = dot(a2, high, 0, 0) + dot(a2, low, 0, 0)
    gate_w = gate_w_ref[...]
    da2 = dot(s1 + s2, ret_ref[:, 0:D]) + dot(high, gate_w, 1, 1) + dot(low, gate_w, 1, 1)
    gain_grad_ref[...] = jnp.sum(da2 * unit, axis=0, keepdims=True)
    dmid = cot_ref[...].astype(F32) + norm_back(da2, gain_ref[...], unit, inv)
    dmid_ref[...] = dmid
    datt = dmid.astype(BF16)
    o_grad_ref[...] = dot(att_ref[...], datt, 0, 0)
    do = dot(datt, w_o_ref[...], 1, 1)
    for s in range(BLOCKS):
        send_ref[s] = pair_up(do, s).astype(BF16)


def out_body(y_ref, mid_ref, gates_ref, routes_ref, out_ref):
    _, _, c1, c2 = choices(routes_ref[...])
    y = y_ref[...]
    mix = gates_ref[:, 0:1] * dot(chosen(c1), y) + gates_ref[:, 1:2] * dot(chosen(c2), y)
    out_ref[...] = (mid_ref[...] + mix).astype(BF16)


def finish_body(dqkv_ref, tok_ref, gain_ref, w_ref, dmid_ref, tok_grad_ref, qkv_grad_ref, gain_grad_ref):
    unit, inv = norm(tok_ref[...].astype(F32))
    a1 = (unit * gain_ref[...]).astype(BF16)
    da1 = jnp.zeros((ROWS, D), F32)
    for part in range(3):
        tiles = unpair(
            [dqkv_ref[s, :, part * 128 : part * 128 + 128].astype(F32) for s in range(BLOCKS)]
        )
        d = jnp.concatenate([t.astype(BF16) for t in tiles], axis=1)
        at = slice(part * D, part * D + D)
        qkv_grad_ref[:, at] = dot(a1, d, 0, 0)
        da1 = da1 + dot(d, w_ref[:, at], 1, 1)
    gain_grad_ref[...] = jnp.sum(da1 * unit, axis=0, keepdims=True)
    tok_grad_ref[...] = dmid_ref[...] + norm_back(da1, gain_ref[...], unit, inv)


def on_device(tokens, cotangent, gain_first, w_qkv, w_o, gain_second, w_gate, w_in, w_out, routes, frozen):
    zh = lax.axis_index("zh")
    s = zh * 4 + lax.axis_index("x")
    e = (lax.axis_index("zl") * 4 + lax.axis_index("y")) * 2 + lax.axis_index("c")
    half = s % 2
    tok, cot, routes = tokens[0], cotangent[0], routes[0]
    gain1, gain2 = gain_first.reshape(1, D), gain_second.reshape(1, D)

    swap = [(0, 1), (1, 0)]

    def gather(w, axis):
        own = lax.dynamic_index_in_dim(w, zh, 0, keepdims=False)
        other = lax.dynamic_index_in_dim(w, 1 - zh, 0, keepdims=False)
        got = lax.ppermute(other, "zh", swap)
        return lax.all_gather(jnp.concatenate([own, got], axis=axis), "x")

    w_in_full = gather(w_in, 1)
    w_out_full = gather(w_out, 0)

    c_send = call(deal_body, [((SLOTS, D), BF16)], 2)(cot, routes)[0]
    c_rows = lax.all_to_all(c_send.reshape(32, CAP, D), GROUP, 0, 0, tiled=True)

    qkv_send = call(project_body, [((BLOCKS, ROWS, 384), BF16)], 3)(tok, gain1, w_qkv)[0]
    qkv = lax.all_to_all(qkv_send, SEQ, 0, 0, tiled=True)

    def fwd(*refs):
        attend_forward(lax.axis_index("x") % 2, *refs)

    o_send, ot, lse = call(
        fwd,
        [((BLOCKS, ROWS, 128), BF16), ((12, 64, ROWS), F32), ((12, 8, ROWS), F32)],
        1,
        [pltpu.VMEM((128, BLOCKS * ROWS), BF16)],
    )(qkv)
    o = lax.all_to_all(o_send, SEQ, 0, 0, tiled=True)
    mid, att, x_send, gates = call(
        middle_body,
        [((ROWS, D), F32), ((ROWS, D), BF16), ((SLOTS, D + EXTRA), BF16), ((ROWS, 128), F32)],
        6,
    )(o, tok, w_o, gain2, w_gate, routes)
    x_rows = lax.all_to_all(x_send.reshape(32, CAP, D + EXTRA), GROUP, 0, 0, tiled=True)
    ret, y, dw_in, dw_out = experts(
        x_rows.reshape(SLOTS, D + EXTRA), c_rows.reshape(SLOTS, D), w_in_full, w_out_full
    )
    ret = lax.all_to_all(ret.reshape(32, CAP, D + EXTRA), GROUP, 0, 0, tiled=True).reshape(SLOTS, D + EXTRA)
    y = lax.all_to_all(y.reshape(32, CAP, D), GROUP, 0, 0, tiled=True).reshape(SLOTS, D)

    keep = (1 - lax.dynamic_slice_in_dim(frozen, 2 * e, 2)).astype(F32)

    def scatter(dw, axis):
        mine = lax.psum_scatter(dw, "x", scatter_dimension=0, tiled=False)
        own, other = jnp.split(mine, 2, axis=axis)
        got = lax.ppermute(other, "zh", swap)
        first = jnp.where(zh == 0, own, got).astype(F32)
        second = jnp.where(zh == 0, got, own).astype(F32)
        return jnp.stack([first, second]) * keep[:, None, None]

    w_in_grad = scatter(dw_in, 1)
    w_out_grad = scatter(dw_out, 0)

    do_send, dmid, o_grad, gate_grad, gain2_grad = call(
        back_body,
        [((BLOCKS, ROWS, 128), BF16), ((ROWS, D), F32), ((D, D), F32), ((D, EXPERTS), F32), ((1, D), F32)],
        9,
    )(ret, cot, routes, gates, mid, att, gain2, w_gate, w_o)
    do = lax.all_to_all(do_send, SEQ, 0, 0, tiled=True)

    def bwd(*refs):
        attend_backward(lax.axis_index("x") % 2, *refs)

    dqkv_send = call(
        bwd,
        [((BLOCKS, ROWS, 384), BF16)],
        4,
        [
            pltpu.VMEM((128, BLOCKS * ROWS), BF16),
            pltpu.VMEM((BLOCKS * ROWS, 128), F32),
            pltpu.VMEM((BLOCKS * ROWS, 128), F32),
        ],
    )(qkv, do, ot, lse)[0]
    dqkv = lax.all_to_all(dqkv_send, SEQ, 0, 0, tiled=True)
    out = call(out_body, [((ROWS, D), BF16)], 4)(y, mid, gates, routes)[0]
    tok_grad, qkv_grad, gain1_grad = call(
        finish_body, [((ROWS, D), F32), ((D, 3 * D), F32), ((1, D), F32)], 5
    )(dqkv, tok, gain1, w_qkv, dmid)
    qkv_grad, o_grad, gate_grad, gain1_grad, gain2_grad = lax.psum(
        (qkv_grad, o_grad, gate_grad, gain1_grad, gain2_grad), ALL
    )
    return (
        out[None],
        tok_grad[None],
        gain1_grad.reshape(D),
        qkv_grad,
        o_grad,
        gain2_grad.reshape(D),
        gate_grad * (1 - frozen).astype(F32)[None, :],
        w_in_grad,
        w_out_grad,
    )


def solution(mesh):
    fine = Mesh(mesh.devices.reshape(2, 4, 2, 4, 2), ALL)
    seq, exp = ("zh", "x"), ("zl", "y", "c")
    in_specs = (
        P(exp, seq, None),
        P(exp, seq, None),
        P(),
        P(),
        P(),
        P(),
        P(),
        P(exp, None, seq),
        P(exp, seq, None),
        P(exp, seq, None),
        P(),
    )
    out_specs = (
        P(exp, seq, None),
        P(exp, seq, None),
        P(),
        P(),
        P(),
        P(),
        P(),
        P(exp, None, seq),
        P(exp, seq, None),
    )
    return jax.shard_map(on_device, mesh=fine, in_specs=in_specs, out_specs=out_specs, check_vma=False)
```

```python
import functools
import math

import jax
import jax.numpy as jnp
from jax import lax
from jax.experimental import pallas as pl
from jax.experimental.pallas import tpu as pltpu
from jax.sharding import Mesh
from jax.sharding import PartitionSpec as P

D = 768
HEADS = 12
HEAD_DIM = 64
EXPERTS = 32
CAP = 32
ROWS = 256
BLOCKS = 8
FF = 3072
SLOTS = EXPERTS * CAP
EXTRA = 128
EPS = 1e-5
SCALE = HEAD_DIM ** -0.5
LOG2E = math.log2(math.e)
BF16 = jnp.bfloat16
F32 = jnp.float32
NEG = -1e30

SEQ = ("zh", "x")
MESH = pl.DeviceIdType.MESH
ALL = ("zh", "x", "zl", "y", "c")


def dot(a, b, ca=1, cb=0):
    return lax.dot_general(a, b, (((ca,), (cb,)), ((), ())), preferred_element_type=F32)


def params(mb=56):
    return pltpu.CompilerParams(vmem_limit_bytes=mb * 2**20)


def vspec(n):
    return [pl.BlockSpec(memory_space=pltpu.VMEM)] * n


def call(body, outs, n_in, scratch=(), **kw):
    return pl.pallas_call(
        body,
        out_shape=[jax.ShapeDtypeStruct(s, t) for s, t in outs],
        in_specs=vspec(n_in),
        out_specs=vspec(len(outs)),
        scratch_shapes=list(scratch),
        compiler_params=params(),
        **kw,
    )


def norm(v):
    mean = jnp.mean(v, axis=-1, keepdims=True)
    centred = v - mean
    inv = lax.rsqrt(jnp.mean(centred * centred, axis=-1, keepdims=True) + EPS)
    return centred * inv, inv


def norm_back(grad, gain, unit, inv):
    t = grad * gain
    m1 = jnp.mean(t, axis=-1, keepdims=True)
    m2 = jnp.mean(t * unit, axis=-1, keepdims=True)
    return inv * (t - m1 - unit * m2)


def lane_low():
    return lax.broadcasted_iota(jnp.int32, (1, 128), 1) < 64


def pair_up(wide, s):
    low = wide[:, 128 * (s // 2) : 128 * (s // 2) + 128]
    if s % 2:
        low = pltpu.roll(low, 64, 1)
    high = wide[:, 512 + 128 * (s // 4) : 640 + 128 * (s // 4)]
    if (s // 2) % 2 == 0:
        high = pltpu.roll(high, 64, 1)
    return jnp.where(lane_low(), low, high)


def unpair(tiles):
    out = []
    for t in range(4):
        out.append(
            jnp.where(lane_low(), tiles[2 * t], pltpu.roll(tiles[2 * t + 1], 64, 1))
        )
    for t in range(2):
        a = tiles[4 * t] + tiles[4 * t + 1]
        b = tiles[4 * t + 2] + tiles[4 * t + 3]
        out.append(jnp.where(lane_low(), pltpu.roll(a, 64, 1), b))
    return out


def project_body(tok_ref, gain_ref, w_ref, send_ref):
    unit, _ = norm(tok_ref[...].astype(F32))
    a1 = (unit * gain_ref[...]).astype(BF16)
    for part in range(3):
        wide = dot(a1, w_ref[:, part * D : part * D + D])
        for s in range(BLOCKS):
            send_ref[s, :, part * 128 : part * 128 + 128] = pair_up(wide, s).astype(
                BF16
            )


def unit_list(half):
    units = [(0, i, i + 1, i, i) for i in range(BLOCKS)]
    firsts = [(0, 1), (3, 2), (4, 5), (7, 6)]
    for t, (a, b) in enumerate(firsts):
        units.append((1, a + half * (b - a), 2 * t + 2, 2 * t, BLOCKS + t))
    return units


def masked_scores(k, q, block, first, count):
    s = dot(k, q, 1, 1)
    start = first * ROWS
    tail = (count - first) * ROWS
    keys = lax.broadcasted_iota(jnp.int32, (tail, ROWS), 0) + start
    queries = lax.broadcasted_iota(jnp.int32, (tail, ROWS), 1) + block * ROWS
    end = jnp.where(keys <= queries, s[start:], NEG)
    return end if start == 0 else jnp.concatenate([s[:start], end], axis=0)


def head_mask(h):
    low = lane_low()
    return (low if h == 0 else jnp.logical_not(low)).astype(F32).astype(BF16)


def attend_forward(half, qkv_ref, o_ref, ot_ref, lse_ref, vt_ref):
    c = SCALE * LOG2E
    for b in range(BLOCKS):
        vt_ref[:, b * ROWS : (b + 1) * ROWS] = qkv_ref[b, :, 256:384].T
        o_ref[b] = jnp.zeros((ROWS, 128), BF16)
    for h, block, count, first, u in unit_list(half):
        q = qkv_ref[block, :, 0:128] * head_mask(h)
        k = qkv_ref[0:count, :, 128:256].reshape(count * ROWS, 128)
        s = masked_scores(k, q, block, first, count)
        top = jnp.max(s, axis=0, keepdims=True)
        p = jnp.exp2((s - top) * c)
        total = jnp.sum(p, axis=0, keepdims=True)
        ot = dot(vt_ref[64 * h : 64 * h + 64, 0 : count * ROWS], p.astype(BF16))
        ot = ot / total
        ot_ref[u] = ot
        lse_ref[u] = jnp.broadcast_to(top * c + jnp.log2(total), (8, ROWS))
        wide = jnp.concatenate([ot, jnp.zeros_like(ot)] if h == 0 else [jnp.zeros_like(ot), ot], axis=0)
        o_ref[block] = (o_ref[block].astype(F32) + wide.T).astype(BF16)


def attend_backward(half, qkv_ref, do_ref, ot_ref, lse_ref, out_ref, kt_ref, dk_ref, dv_ref):
    c = SCALE * LOG2E
    for b in range(BLOCKS):
        kt_ref[:, b * ROWS : (b + 1) * ROWS] = qkv_ref[b, :, 128:256].T
        out_ref[b, :, 0:128] = jnp.zeros((ROWS, 128), BF16)
    dk_ref[...] = jnp.zeros_like(dk_ref)
    dv_ref[...] = jnp.zeros_like(dv_ref)
    for h, block, count, first, u in unit_list(half):
        rows = count * ROWS
        q = qkv_ref[block, :, 0:128] * head_mask(h)
        do = do_ref[block] * head_mask(h)
        dot_rows = do.astype(F32).T[64 * h : 64 * h + 64]
        delta = jnp.sum(dot_rows * ot_ref[u], axis=0, keepdims=True)
        lse = lse_ref[u][0:1]
        k = qkv_ref[0:count, :, 128:256].reshape(rows, 128)
        v = qkv_ref[0:count, :, 256:384].reshape(rows, 128)
        s = masked_scores(k, q, block, first, count)
        p = jnp.exp2(s * c - lse)
        dp = dot(v, do, 1, 1)
        ds = (p * (dp - delta)).astype(BF16)
        dv_ref[0:rows] += dot(p.astype(BF16), do)
        dk_ref[0:rows] += dot(ds, q)
        dqt = dot(kt_ref[64 * h : 64 * h + 64, 0:rows], ds) * SCALE
        wide = jnp.concatenate([dqt, jnp.zeros_like(dqt)] if h == 0 else [jnp.zeros_like(dqt), dqt], axis=0)
        out_ref[block, :, 0:128] = (
            out_ref[block, :, 0:128].astype(F32) + wide.T
        ).astype(BF16)
    for b in range(BLOCKS):
        at = slice(b * ROWS, (b + 1) * ROWS)
        out_ref[b, :, 128:256] = (dk_ref[at] * SCALE).astype(BF16)
        out_ref[b, :, 256:384] = dv_ref[at].astype(BF16)


def half_of(index):
    return (index + index // 2) % 2


def choices(routes):
    ids = lax.broadcasted_iota(jnp.int32, (ROWS, EXPERTS), 1)
    e1, e2 = routes[:, 0:1], routes[:, 1:2]
    m1, m2 = (e1 == ids).astype(F32), (e2 == ids).astype(F32)
    r = lax.broadcasted_iota(jnp.int32, (ROWS, ROWS), 0)
    k = lax.broadcasted_iota(jnp.int32, (ROWS, ROWS), 1)
    lower = (k < r).astype(F32).astype(BF16)
    earlier = dot(lower, (m1 + m2).astype(BF16))
    s1 = jnp.sum(earlier * m1, axis=1, keepdims=True)
    s2 = jnp.sum(earlier * m2, axis=1, keepdims=True)

    return m1, m2, (e1 * CAP).astype(F32) + s1, (e2 * CAP).astype(F32) + s2


def chosen(col):
    at = lax.broadcasted_iota(jnp.int32, (ROWS, SLOTS), 1).astype(F32)
    return (at == col).astype(F32).astype(BF16)


def chosen_t(col):
    row = jnp.broadcast_to(col, (ROWS, 128)).T[0:1]
    at = lax.broadcasted_iota(jnp.int32, (SLOTS, ROWS), 0).astype(F32)
    return (at == row).astype(F32).astype(BF16)


def two_parts(v):
    lane = lax.broadcasted_iota(jnp.int32, (v.shape[0], EXTRA), 1)
    high = v.astype(BF16).astype(F32)
    return jnp.where(lane == 0, high, jnp.where(lane == 1, v - high, 0.0)).astype(BF16)


def from_parts(v):
    lane = lax.broadcasted_iota(jnp.int32, v.shape, 1)
    return jnp.sum(jnp.where(lane < 2, v.astype(F32), 0.0), axis=1, keepdims=True)


def deal_body(cot_ref, routes_ref, send_ref):
    _, _, c1, c2 = choices(routes_ref[...])
    either = chosen_t(c1) + chosen_t(c2)
    send_ref[...] = dot(either, cot_ref[...]).astype(BF16)


def middle_body(o_ref, tok_ref, w_o_ref, gain_ref, gate_ref, routes_ref, mid_ref, att_ref, send_ref, gates_ref):
    tiles = unpair([o_ref[s].astype(F32) for s in range(BLOCKS)])
    o = jnp.concatenate([t.astype(BF16) for t in tiles], axis=1)
    att_ref[...] = o
    mid = tok_ref[...].astype(F32) + dot(o, w_o_ref[...])
    mid_ref[...] = mid
    unit, _ = norm(mid)
    a2 = (unit * gain_ref[...]).astype(BF16)
    logits = dot(a2, gate_ref[...])
    m1, m2, c1, c2 = choices(routes_ref[...])
    l1 = jnp.sum(logits * m1, axis=1, keepdims=True)
    l2 = jnp.sum(logits * m2, axis=1, keepdims=True)
    top = jnp.maximum(l1, l2)
    x1, x2 = jnp.exp(l1 - top), jnp.exp(l2 - top)
    g1, g2 = x1 / (x1 + x2), x2 / (x1 + x2)
    lane = lax.broadcasted_iota(jnp.int32, (ROWS, 128), 1)
    gates_ref[...] = jnp.where(lane == 0, g1, g2)
    t1, t2 = chosen_t(c1), chosen_t(c2)
    send_ref[:, 0:D] = dot(t1 + t2, a2).astype(BF16)
    send_ref[:, D:] = (dot(t1, two_parts(g1)) + dot(t2, two_parts(g2))).astype(BF16)


def erf_parts(h):
    x = jnp.abs(h) * (0.5**0.5)
    t = 1.0 / (1.0 + 0.3275911 * x)
    e = jnp.exp(-0.5 * h * h)
    poly = t * (
        0.254829592
        + t * (-0.284496736 + t * (1.421413741 + t * (-1.453152027 + t * 1.061405429)))
    )
    tail = 0.5 * poly * e
    return jnp.where(h >= 0, 1.0 - tail, tail), e * (1.0 / math.sqrt(2.0 * math.pi))


def div(a, b):
    return lax.div(a, jnp.int32(b))


def rem(a, b):
    return lax.rem(a, jnp.int32(b))


def coords():
    return tuple(lax.axis_index(a) for a in ALL)


def near(x, pair):
    return x + rem(div(x, 2) + pair, 2) * (3 - 2 * x)


def neighbour(x):
    return x + 1 - 2 * rem(x, 2)


def expert_of(zh, x, zl, y):
    return 4 * (4 * zl + y) + 2 * div(x, 2) + zh


def remote(src, dst, send, recv, device):
    return pltpu.make_async_remote_copy(
        src_ref=src,
        dst_ref=dst,
        send_sem=send,
        recv_sem=recv,
        device_id=device,
        device_id_type=MESH,
    )


def await_bytes(ref, sem):
    pltpu.make_async_copy(ref, ref, sem).wait()


def chip_partner(me, k):
    zh, x, zl, y, c = me
    return (
        rem(zh + div(k, 8), 2),
        rem(x + rem(div(k, 2), 4), 4),
        zl,
        y,
        rem(c + rem(k, 2), 2),
    )


def row_partner(me, k):
    zh, x, zl, y, c = me
    return (
        rem(zh + rem(div(k, 8), 2), 2),
        x + div(k, 16) * (3 - 2 * x),
        rem(zl + rem(div(k, 4), 2), 2),
        rem(y + rem(k, 4), 4),
        c,
    )


def head_partner(me, k):
    zh, x, zl, y, c = me
    t = rem(zh * 4 + x + k, 8)
    return t, (div(t, 4), rem(t, 4), zl, y, c)


def greet(me, partner, count):
    barrier = pltpu.get_barrier_semaphore()

    def one(k, carry):
        pl.semaphore_signal(
            barrier, inc=1, device_id=partner(me, k), device_id_type=MESH
        )
        return carry

    lax.fori_loop(1, count, one, 0)
    return count - 1


def greet_all(*groups):
    me = coords()
    total = sum(greet(me, partner, count) for partner, count in groups)
    pl.semaphore_wait(pltpu.get_barrier_semaphore(), total)
    return me


class HeadSwap:
    def __init__(self, me, send, recv, sems):
        self.me, self.send, self.recv, self.sems = me, send, recv, sems
        self.place = me[0] * 4 + me[1]

    def local(self):
        s = self.place
        return pltpu.make_async_copy(
            self.send.at[s], self.recv.at[s], self.sems.at[0, 0]
        )

    def copy(self, k):
        t, device = head_partner(self.me, k)
        return remote(
            self.send.at[t],
            self.recv.at[self.place],
            self.sems.at[0, k],
            self.sems.at[1, k],
            device,
        )

    def start(self):
        self.local().start()
        for k in range(1, 8):
            self.copy(jnp.int32(k)).start()

    def wait(self):
        self.local().wait()
        for k in range(1, 8):
            self.copy(jnp.int32(k)).wait()


class RowSwap:
    def __init__(self, me, send, recv, sems, back=False):
        self.me, self.send, self.recv, self.sems = me, send, recv, sems
        self.back = back

    def ends(self, k):
        zh, x, zl, y, c = self.me
        device = row_partner(self.me, k)
        mirrored = 16 * div(k, 16)
        if self.back:
            src = mirrored + 8 * device[0] + 4 * device[2] + device[3]
            dst = expert_of(zh, x, zl, y)
        else:
            src = expert_of(*device[:4])
            dst = mirrored + 8 * zh + 4 * zl + y
        rows = lambda n: pl.ds(pl.multiple_of(n * CAP, CAP), CAP)
        return self.send.at[rows(src)], self.recv.at[rows(dst)], device

    def start(self):
        src, dst, _ = self.ends(jnp.int32(0))
        pltpu.make_async_copy(src, dst, self.sems.at[1]).start()

        def one(k, carry):
            src, dst, device = self.ends(k)
            remote(src, dst, self.sems.at[0], self.sems.at[1], device).start()
            return carry

        lax.fori_loop(1, 32, one, 0)

    def wait_recv(self):
        await_bytes(self.recv, self.sems.at[1])

    def wait_send(self):
        await_bytes(self.send.at[pl.ds(0, 31 * CAP)], self.sems.at[0])

    def wait(self):
        self.wait_recv()
        self.wait_send()


def remote_params(n, mb=60):
    return pltpu.CompilerParams(
        vmem_limit_bytes=mb * 2**20, collective_id=n, has_side_effects=True
    )


VMEM = pl.BlockSpec(memory_space=pltpu.VMEM)
ANY = pl.BlockSpec(memory_space=pl.ANY)
DMA = pltpu.SemaphoreType.DMA


class Weights:
    def __init__(self, me, w_in, w_out, full_in, full_out, sems):
        self.me, self.refs, self.full, self.sems = me, (w_in, w_out), (full_in, full_out), sems

    def place(self, i, x, zh):
        at = pl.ds(pl.multiple_of(zh * 384, 128), 384)
        return self.full[0].at[x, :, at] if i == 0 else self.full[1].at[x, at, :]

    def first(self, i, b):
        zh, x, zl, y, c = self.me
        device = (jnp.int32(b), near(x, c), zl, y, zh)
        copy = remote(
            self.refs[i].at[b], self.place(i, x, zh), self.sems.at[0, i, b], self.sems.at[1, i, x], device
        )
        local = pltpu.make_async_copy(
            self.refs[i].at[b], self.place(i, x, zh), self.sems.at[1, i, x]
        )
        own = jnp.logical_and(
            jnp.logical_and(zh == b, div(x, 2) == c), zh == c
        )
        return copy, local, own

    def start(self, i):
        for b in range(2):
            copy, local, own = self.first(i, b)
            pl.when(own)(local.start)
            pl.when(jnp.logical_not(own))(copy.start)

    def forward(self, i, x, step):
        zh, me_x, zl, y, c = self.me
        piece = self.place(i, x, c)
        device = (zh, neighbour(me_x), zl, y, c) if step == 2 else (zh, me_x, zl, y, 1 - c)
        return remote(piece, piece, self.sems.at[2 * step - 2, i, x], self.sems.at[2 * step - 1, i, x], device)

    def sources(self, step):
        x = self.me[1]
        if step == 1:
            return x, 3 - x
        return neighbour(x), 3 - neighbour(x)

    def second(self, i):
        for x in self.sources(1):
            await_bytes(self.place(i, x, self.me[4]), self.sems.at[1, i, x])
            self.forward(i, x, 2).start()
            self.forward(i, x, 3).start()

    def third(self, i):
        for x in self.sources(2):
            self.forward(i, x, 2).wait_recv()
            self.forward(i, x, 3).start()

    def finish(self, i):
        for b in range(2):
            copy, _, own = self.first(i, b)
            pl.when(jnp.logical_not(own))(copy.wait_send)
        for x in self.sources(1):
            self.forward(i, x, 2).wait_send()
        for x in range(4):
            self.forward(i, jnp.int32(x), 3).wait()


def front_body(tok_ref, cot_ref, gain1_ref, w_qkv_ref, w_o_ref, gain2_ref, gate_ref, routes_ref, w_in_ref, w_out_ref,
               qkv_ref, x_ref, c_ref, full_in_ref, full_out_ref, mid_ref, att_ref, gates_ref, ot_ref, lse_ref,
               qkv_send, o_send, o_recv, x_send, c_send, vt_ref, head_sems, row_sems, weight_sems):
    me = greet_all((chip_partner, 16), (row_partner, 32))
    weights = Weights(me, w_in_ref, w_out_ref, full_in_ref, full_out_ref, weight_sems)
    heads = HeadSwap(me, qkv_send, qkv_ref, head_sems.at[0])
    heads_back = HeadSwap(me, o_send, o_recv, head_sems.at[1])
    rows_c = RowSwap(me, c_send, c_ref, row_sems.at[0])
    rows_x = RowSwap(me, x_send, x_ref, row_sems.at[1])
    weights.start(0)
    project_body(tok_ref, gain1_ref, w_qkv_ref, qkv_send)
    heads.start()
    deal_body(cot_ref, routes_ref, c_send)
    weights.start(1)
    heads.wait()
    rows_c.start()
    weights.second(0)
    attend_forward(rem(me[1], 2), qkv_ref, o_send, ot_ref, lse_ref, vt_ref)
    heads_back.start()
    weights.second(1)
    weights.third(0)
    heads_back.wait()
    middle_body(o_recv, tok_ref, w_o_ref, gain2_ref, gate_ref, routes_ref, mid_ref, att_ref, x_send, gates_ref)
    rows_x.start()
    weights.third(1)
    rows_c.wait()
    weights.finish(0)
    weights.finish(1)
    rows_x.wait()


def front(tok, cot, gain1, w_qkv, w_o, gain2, gate, routes, w_in, w_out):
    outs = [
        ((BLOCKS, ROWS, 384), BF16, VMEM),
        ((SLOTS, D + EXTRA), BF16, VMEM),
        ((SLOTS, D), BF16, VMEM),
        ((4, D, D), BF16, ANY),
        ((4, D, D), BF16, ANY),
        ((ROWS, D), F32, VMEM),
        ((ROWS, D), BF16, VMEM),
        ((ROWS, 128), F32, VMEM),
        ((12, 64, ROWS), F32, VMEM),
        ((12, 8, ROWS), F32, VMEM),
    ]
    return pl.pallas_call(
        front_body,
        out_shape=[jax.ShapeDtypeStruct(s, t) for s, t, _ in outs],
        in_specs=[VMEM] * 8 + [ANY] * 2,
        out_specs=[m for _, _, m in outs],
        scratch_shapes=[
            pltpu.VMEM((BLOCKS, ROWS, 384), BF16),
            pltpu.VMEM((BLOCKS, ROWS, 128), BF16),
            pltpu.VMEM((BLOCKS, ROWS, 128), BF16),
            pltpu.VMEM((SLOTS, D + EXTRA), BF16),
            pltpu.VMEM((SLOTS, D), BF16),
            pltpu.VMEM((128, BLOCKS * ROWS), BF16),
            DMA((2, 2, 8)),
            DMA((2, 2)),
            DMA((6, 2, 4)),
        ],
        compiler_params=remote_params(0),
    )(tok, cot, gain1, w_qkv, w_o, gain2, gate, routes, w_in, w_out)


STEP = 256
CHUNKS = 4
TILES = SLOTS // STEP


def row_block(r):
    return pl.ds(pl.multiple_of(r * STEP, STEP), STEP)


def expert_body(x_ref, c_ref, win_ref, wout_ref, ret_ref, y_ref, dwin_ref, dwout_ref,
                g_ref, dh_ref, dx_ref, dg_ref, xg_ref, cg_ref, ret_send, y_send, sems):
    me = greet_all((row_partner, 32))
    rows_ret = RowSwap(me, ret_send, ret_ref, sems.at[0], back=True)
    rows_y = RowSwap(me, y_send, y_ref, sems.at[1], back=True)
    dx_ref[...] = jnp.zeros_like(dx_ref)
    dg_ref[...] = jnp.zeros_like(dg_ref)

    def hidden(n, carry):
        j, r = div(n, TILES), rem(n, TILES)
        at = row_block(r)
        h = dot(x_ref[at, 0:D], win_ref[j])
        cw = dot(c_ref[at, :], wout_ref[j], 1, 1)
        phi, density = erf_parts(h)
        g = h * phi
        dh = ((phi + h * density) * cw).astype(BF16)
        g_ref[j, at, :] = g.astype(BF16)
        dh_ref[j, at, :] = dh
        prod = g * cw
        part = prod[:, 0:128]
        for t in range(1, D // 128):
            part = part + prod[:, 128 * t : 128 * t + 128]
        dg_ref[at, :] += part
        dx_ref[at, :] += dot(dh, win_ref[j], 1, 1)
        return carry

    lax.fori_loop(0, CHUNKS * TILES, hidden, 0)

    def scale(r, carry):
        at = row_block(r)
        gate = from_parts(x_ref[at, D:])
        ret_send[at, 0:D] = (dx_ref[at, :] * gate).astype(BF16)
        ret_send[at, D:] = two_parts(jnp.sum(dg_ref[at, :], axis=1, keepdims=True))
        return carry

    lax.fori_loop(0, TILES, scale, 0)
    rows_ret.start()

    def produce(r, carry):
        at = row_block(r)
        gate = from_parts(x_ref[at, D:])
        xg_ref[at, :] = (x_ref[at, 0:D].astype(F32) * gate).astype(BF16)
        cg_ref[at, :] = (c_ref[at, :].astype(F32) * gate).astype(BF16)
        y = dot(g_ref[0, at, :], wout_ref[0])
        for j in range(1, CHUNKS):
            y = y + dot(g_ref[j, at, :], wout_ref[j])
        y_send[at, :] = y.astype(BF16)
        return carry

    lax.fori_loop(0, TILES, produce, 0)
    rows_y.start()

    def grads(j, carry):
        dwin_ref[j] = dot(xg_ref[...], dh_ref[j], 0, 0).astype(BF16)
        dwout_ref[j] = dot(g_ref[j], cg_ref[...], 0, 0).astype(BF16)
        return carry

    lax.fori_loop(0, CHUNKS, grads, 0)
    rows_ret.wait()
    rows_y.wait()


def experts(x, c, w_in, w_out):
    return pl.pallas_call(
        expert_body,
        out_shape=[
            jax.ShapeDtypeStruct((SLOTS, D + EXTRA), BF16),
            jax.ShapeDtypeStruct((SLOTS, D), BF16),
            jax.ShapeDtypeStruct((CHUNKS, D, D), BF16),
            jax.ShapeDtypeStruct((CHUNKS, D, D), BF16),
        ],
        in_specs=[VMEM] * 4,
        out_specs=[VMEM] * 4,
        scratch_shapes=[
            pltpu.VMEM((CHUNKS, SLOTS, D), BF16),
            pltpu.VMEM((CHUNKS, SLOTS, D), BF16),
            pltpu.VMEM((SLOTS, D), F32),
            pltpu.VMEM((SLOTS, 128), F32),
            pltpu.VMEM((SLOTS, D), BF16),
            pltpu.VMEM((SLOTS, D), BF16),
            pltpu.VMEM((SLOTS, D + EXTRA), BF16),
            pltpu.VMEM((SLOTS, D), BF16),
            DMA((2, 2)),
        ],
        compiler_params=remote_params(1),
    )(x, c, w_in, w_out)


def back_body(ret_ref, cot_ref, routes_ref, gates_ref, mid_ref, att_ref, gain_ref, gate_w_ref, w_o_ref,
              send_ref, dmid_ref, o_grad_ref, gate_grad_ref, gain_grad_ref):
    m1, m2, c1, c2 = choices(routes_ref[...])
    s1, s2 = chosen(c1), chosen(c2)
    g1, g2 = gates_ref[:, 0:1], gates_ref[:, 1:2]
    extra = ret_ref[:, D:]
    d1, d2 = from_parts(dot(s1, extra)), from_parts(dot(s2, extra))
    dl = g1 * g2 * (d1 - d2)
    dlogits = (m1 - m2) * dl
    unit, inv = norm(mid_ref[...])
    a2 = (unit * gain_ref[...]).astype(BF16)
    high = dlogits.astype(BF16)
    low = (dlogits - high.astype(F32)).astype(BF16)
    gate_grad_ref[...] = dot(high, a2, 0, 0) + dot(low, a2, 0, 0)
    gate_w = gate_w_ref[...]
    da2 = dot(s1 + s2, ret_ref[:, 0:D]) + dot(high, gate_w, 1, 1) + dot(low, gate_w, 1, 1)
    gain_grad_ref[...] = jnp.sum(da2 * unit, axis=0, keepdims=True)
    dmid = cot_ref[...].astype(F32) + norm_back(da2, gain_ref[...], unit, inv)
    dmid_ref[...] = dmid
    datt = dmid.astype(BF16)
    o_grad_ref[...] = dot(att_ref[...], datt, 0, 0)
    do = dot(datt, w_o_ref[...], 1, 1)
    for s in range(BLOCKS):
        send_ref[s] = pair_up(do, s).astype(BF16)


def out_body(y_ref, mid_ref, gates_ref, routes_ref, out_ref):
    _, _, c1, c2 = choices(routes_ref[...])
    y = y_ref[...]
    mix = gates_ref[:, 0:1] * dot(chosen(c1), y) + gates_ref[:, 1:2] * dot(chosen(c2), y)
    out_ref[...] = (mid_ref[...] + mix).astype(BF16)


def finish_body(dqkv_ref, tok_ref, gain_ref, w_ref, dmid_ref, tok_grad_ref, qkv_grad_ref, gain_grad_ref):
    unit, inv = norm(tok_ref[...].astype(F32))
    a1 = (unit * gain_ref[...]).astype(BF16)
    da1 = jnp.zeros((ROWS, D), F32)
    for part in range(3):
        tiles = unpair(
            [dqkv_ref[s, :, part * 128 : part * 128 + 128].astype(F32) for s in range(BLOCKS)]
        )
        d = jnp.concatenate([t.astype(BF16) for t in tiles], axis=1)
        at = slice(part * D, part * D + D)
        qkv_grad_ref[:, at] = dot(a1, d, 0, 0)
        da1 = da1 + dot(d, w_ref[:, at], 1, 1)
    gain_grad_ref[...] = jnp.sum(da1 * unit, axis=0, keepdims=True)
    tok_grad_ref[...] = dmid_ref[...] + norm_back(da1, gain_ref[...], unit, inv)


def rear_body(ret_ref, cot_ref, routes_ref, gates_ref, mid_ref, att_ref, gain2_ref, gate_w_ref, w_o_ref,
              qkv_ref, ot_ref, lse_ref, tok_ref, gain1_ref, w_qkv_ref,
              tok_grad_ref, grads_ref, small_ref,
              dmid_ref, do_send, do_recv, dqkv_send, dqkv_recv, kt_ref, dk_ref, dv_ref, sems):
    me = greet_all((lambda m, k: head_partner(m, k)[1], 8))
    heads = HeadSwap(me, do_send, do_recv, sems.at[0])
    heads_back = HeadSwap(me, dqkv_send, dqkv_recv, sems.at[1])
    small_ref[...] = jnp.zeros_like(small_ref)
    back_body(ret_ref, cot_ref, routes_ref, gates_ref, mid_ref, att_ref, gain2_ref, gate_w_ref, w_o_ref,
              do_send, dmid_ref, grads_ref.at[:, 3 * D : 4 * D], small_ref.at[0:32], small_ref.at[32:33])
    heads.start()
    heads.wait()
    attend_backward(rem(me[1], 2), qkv_ref, do_recv, ot_ref, lse_ref, dqkv_send, kt_ref, dk_ref, dv_ref)
    heads_back.start()
    heads_back.wait()
    finish_body(dqkv_recv, tok_ref, gain1_ref, w_qkv_ref, dmid_ref, tok_grad_ref,
                grads_ref.at[:, 0 : 3 * D], small_ref.at[40:41])


def rear(*args):
    return pl.pallas_call(
        rear_body,
        out_shape=[
            jax.ShapeDtypeStruct((ROWS, D), F32),
            jax.ShapeDtypeStruct((D, 4 * D), F32),
            jax.ShapeDtypeStruct((48, D), F32),
        ],
        in_specs=[VMEM] * len(args),
        out_specs=[VMEM] * 3,
        scratch_shapes=[
            pltpu.VMEM((ROWS, D), F32),
            pltpu.VMEM((BLOCKS, ROWS, 128), BF16),
            pltpu.VMEM((BLOCKS, ROWS, 128), BF16),
            pltpu.VMEM((BLOCKS, ROWS, 384), BF16),
            pltpu.VMEM((BLOCKS, ROWS, 384), BF16),
            pltpu.VMEM((128, BLOCKS * ROWS), BF16),
            pltpu.VMEM((BLOCKS * ROWS, 128), F32),
            pltpu.VMEM((BLOCKS * ROWS, 128), F32),
            DMA((2, 2, 8)),
        ],
        compiler_params=remote_params(2),
    )(*args)


def collect_body(dwin_ref, dwout_ref, fin_in, fin_out, got1_in, got1_out, sum_in, sum_out, send_in, send_out, got2_in, got2_out, sems):
    me = greet_all((chip_partner, 16))
    zh, x, zl, y, c = me
    dw, got1, total = (dwin_ref, dwout_ref), (got1_in, got1_out), (sum_in, sum_out)
    send, got2, fin = (send_in, send_out), (got2_in, got2_out), (fin_in, fin_out)

    def half(i, n, xs):
        at = pl.ds(pl.multiple_of(n * 384, 128), 384)
        return dw[i].at[xs, :, at] if i == 0 else dw[i].at[xs, at, :]

    def first(i, xs):
        return remote(half(i, 1 - c, xs), got1[i].at[xs], sems.at[0, i, xs], sems.at[1, i, xs], (zh, x, zl, y, 1 - c))

    def second(i, j):
        return remote(send[i].at[j], got2[i].at[j], sems.at[2, i, j], sems.at[3, i, j], (zh, neighbour(x), zl, y, c))

    xs3 = (x, 3 - x)

    def third(i, j):
        pair = div(x, 2)
        copy = remote(total[i].at[j], fin[i].at[zh], sems.at[4, i, j], sems.at[5, i, zh], (c, xs3[j], zl, y, pair))
        local = pltpu.make_async_copy(total[i].at[j], fin[i].at[zh], sems.at[5, i, zh])
        own = jnp.logical_and(jnp.logical_and(zh == c, pair == c), j == 0)
        return copy, local, own

    for i in range(2):
        for xs in (neighbour(x), 3 - neighbour(x), x, 3 - x):
            first(i, xs).start()
    for i in range(2):
        for j, xs in enumerate((neighbour(x), 3 - neighbour(x))):
            first(i, xs).wait_recv()
            send[i][j] = (half(i, c, xs)[...].astype(F32) + got1[i][xs].astype(F32)).astype(BF16)
            second(i, j).start()
    for i in range(2):
        for j, xs in enumerate(xs3):
            first(i, xs).wait_recv()
            second(i, j).wait_recv()
            total[i][j] = (half(i, c, xs)[...].astype(F32) + got1[i][xs].astype(F32) + got2[i][j].astype(F32)).astype(BF16)
            copy, local, own = third(i, j)
            pl.when(own)(local.start)
            pl.when(jnp.logical_not(own))(copy.start)
    for i in range(2):
        for xs in range(4):
            first(i, jnp.int32(xs)).wait_send()
        for j in range(2):
            second(i, j).wait_send()
            copy, _, own = third(i, j)
            pl.when(jnp.logical_not(own))(copy.wait_send)
        for b in range(2):
            await_bytes(fin[i].at[b], sems.at[5, i, b])


def collect(dw_in, dw_out):
    shapes = [(D, 384), (384, D)]
    buf = lambda n: [pltpu.VMEM((n,) + s, BF16) for s in shapes]
    return pl.pallas_call(
        collect_body,
        out_shape=[jax.ShapeDtypeStruct((2,) + s, BF16) for s in shapes],
        in_specs=[VMEM] * 2,
        out_specs=[VMEM] * 2,
        scratch_shapes=buf(4) + buf(2) + buf(2) + buf(2) + [DMA((6, 2, 4))],
        compiler_params=remote_params(3),
    )(dw_in, dw_out)


AXES = (1, 3, 2)


def axis_place(me, a):
    zh, x, zl, y, c = me
    return (x, y, 2 * zh + zl)[a]


def axis_peer(me, a, k):
    zh, x, zl, y, c = me
    p = rem(axis_place(me, a) + k, 4)
    if a == 0:
        return p, (zh, p, zl, y, c)
    if a == 1:
        return p, (zh, x, zl, p, c)
    return p, (div(p, 2), x, rem(p, 2), y, c)


def total_body(grads_ref, small_ref, out_ref, small_out,
               s0, r0, a0, s1, r1, a1, s2, r2, a2, r3, sa, sr, sems, small_sems):
    me = coords()
    zh, x, zl, y, c = me
    sibling = (zh, x, zl, y, 1 - c)
    barrier = pltpu.get_barrier_semaphore()
    pl.semaphore_signal(barrier, inc=1, device_id=sibling, device_id_type=MESH)
    for a in range(3):
        for k in range(1, 4):
            pl.semaphore_signal(barrier, inc=1, device_id=axis_peer(me, a, jnp.int32(k))[1], device_id_type=MESH)
    pl.semaphore_wait(barrier, 10)

    def lanes(n, w, base=0):
        return pl.ds(pl.multiple_of(base + n * w, 128), w)

    def rows(n, w, base=0):
        return pl.ds(pl.multiple_of(base + n * w, 16), w)

    place = [[axis_place(me, (g + t) % 3) for t in range(3)] for g in range(3)]

    def swap0(g):
        return remote(s0.at[g], r0.at[g], sems.at[0, g, 0], sems.at[1, g, 0], sibling)

    def small0():
        return remote(small_ref, sr.at[0], small_sems.at[0, 0], small_sems.at[1, 0], sibling)

    for g in range(3):
        s0[g] = grads_ref[:, lanes(1 - c, 512, 1024 * g)].astype(BF16)
        swap0(g).start()
    small0().start()

    def scatter(stage, g, k, src, dst):
        p, device = axis_peer(me, (g + stage - 1) % 3, k)
        n = 2 * stage
        return remote(src(p), dst.at[g, k - 1], sems.at[n, g, k], sems.at[n + 1, g, k], device)

    ks = range(1, 4)

    def scatter1(g, k):
        return scatter(1, g, k, lambda p: s1.at[g, rows(p, 192)], r1)

    def scatter2(g, k):
        return scatter(2, g, k, lambda p: s2.at[g, :, lanes(p, 128)], r2)

    def scatter3(g, k):
        return scatter(3, g, k, lambda p: a2.at[g, rows(p, 48)], r3)

    def small_step(a, k):
        n = 3 * a + k
        return remote(sa.at[a], sr.at[1 + 4 * a + axis_place(me, a)], small_sems.at[0, n], small_sems.at[1, n],
                      axis_peer(me, a, jnp.int32(k))[1])

    def small_sum(a):
        for k in ks:
            small_step(a, k).wait_recv()
        sr[1 + 4 * a + axis_place(me, a)] = sa[a]
        return (sr[1 + 4 * a] + sr[2 + 4 * a]) + (sr[3 + 4 * a] + sr[4 + 4 * a])

    for g in range(3):
        swap0(g).wait_recv()
        a0[g] = grads_ref[:, lanes(c, 512, 1024 * g)] + r0[g].astype(F32)
        s1[g] = a0[g].astype(BF16)
        for k in ks:
            scatter1(g, jnp.int32(k)).start()
    small0().wait_recv()
    sa[0] = small_ref[...] + sr[0]
    for k in ks:
        small_step(0, k).start()
    for g in range(3):
        for k in ks:
            scatter1(g, jnp.int32(k)).wait_recv()
        mine = a0[g, rows(place[g][0], 192), :]
        for k in ks:
            mine = mine + r1[g, k - 1].astype(F32)
        a1[g] = mine
        s2[g] = mine.astype(BF16)
        for k in ks:
            scatter2(g, jnp.int32(k)).start()
    sa[1] = small_sum(0)
    for k in ks:
        small_step(1, k).start()
    for g in range(3):
        for k in ks:
            scatter2(g, jnp.int32(k)).wait_recv()
        mine = a1[g, :, lanes(place[g][1], 128)]
        for k in ks:
            mine = mine + r2[g, k - 1].astype(F32)
        a2[g] = mine
        for k in ks:
            scatter3(g, jnp.int32(k)).start()
    sa[2] = small_sum(1)
    for k in ks:
        small_step(2, k).start()

    def block(g, stage):
        i, j, k = place[g]
        if stage == 3:
            return out_ref.at[rows(4 * i + k, 48), lanes(j, 128, 1024 * g + 512 * c)]
        if stage == 2:
            return out_ref.at[rows(i, 192), lanes(j, 128, 1024 * g + 512 * c)]
        if stage == 1:
            return out_ref.at[rows(i, 192), lanes(c, 512, 1024 * g)]
        return out_ref.at[:, lanes(c, 512, 1024 * g)]

    def gather(g, stage, k):
        n = 8 + 2 * stage
        if stage == 0:
            device = sibling
        else:
            device = axis_peer(me, (g + stage - 1) % 3, k)[1]
        return remote(block(g, stage), block(g, stage), sems.at[n, g, k], sems.at[n + 1, g, k], device)

    for g in range(3):
        for k in ks:
            scatter3(g, jnp.int32(k)).wait_recv()
        mine = a2[g, rows(place[g][2], 48), :]
        for k in ks:
            mine = mine + r3[g, k - 1]
        block(g, 3)[...] = mine.astype(BF16)
        for k in ks:
            gather(g, 3, jnp.int32(k)).start()
    for stage in (2, 1, 0):
        for g in range(3):
            for k in ks:
                gather(g, stage + 1, jnp.int32(k)).wait()
            for k in ks if stage else (0,):
                gather(g, stage, jnp.int32(k)).start()
    small_out[...] = small_sum(2)
    small0().wait_send()
    for k in ks:
        for a in range(3):
            small_step(a, k).wait_send()
    for g in range(3):
        swap0(g).wait_send()
        for k in ks:
            scatter1(g, jnp.int32(k)).wait_send()
            scatter2(g, jnp.int32(k)).wait_send()
            scatter3(g, jnp.int32(k)).wait_send()
        gather(g, 0, jnp.int32(0)).wait()


def totals(grads, small):
    return pl.pallas_call(
        total_body,
        out_shape=[jax.ShapeDtypeStruct((D, 4 * D), BF16), jax.ShapeDtypeStruct((48, D), F32)],
        in_specs=[VMEM] * 2,
        out_specs=[VMEM] * 2,
        scratch_shapes=[
            pltpu.VMEM((3, D, 512), BF16),
            pltpu.VMEM((3, D, 512), BF16),
            pltpu.VMEM((3, D, 512), F32),
            pltpu.VMEM((3, D, 512), BF16),
            pltpu.VMEM((3, 3, 192, 512), BF16),
            pltpu.VMEM((3, 192, 512), F32),
            pltpu.VMEM((3, 192, 512), BF16),
            pltpu.VMEM((3, 3, 192, 128), BF16),
            pltpu.VMEM((3, 192, 128), F32),
            pltpu.VMEM((3, 3, 48, 128), F32),
            pltpu.VMEM((3, 48, D), F32),
            pltpu.VMEM((13, 48, D), F32),
            DMA((16, 3, 4)),
            DMA((2, 10)),
        ],
        compiler_params=remote_params(4),
    )(grads, small)


def on_device(tokens, cotangent, gain_first, w_qkv, w_o, gain_second, w_gate, w_in, w_out, routes, frozen):
    e = (lax.axis_index("zl") * 4 + lax.axis_index("y")) * 2 + lax.axis_index("c")
    tok, cot, routes = tokens[0], cotangent[0], routes[0]
    gain1, gain2 = gain_first.reshape(1, D), gain_second.reshape(1, D)
    qkv, x_rows, c_rows, w_in_full, w_out_full, mid, att, gates, ot, lse = front(
        tok, cot, gain1, w_qkv, w_o, gain2, w_gate, routes, w_in, w_out
    )
    ret, y, dw_in, dw_out = experts(x_rows, c_rows, w_in_full, w_out_full)
    keep = (1 - lax.dynamic_slice_in_dim(frozen, 2 * e, 2)).astype(F32)
    tok_grad, grads, small = rear(
        ret, cot, routes, gates, mid, att, gain2, w_gate, w_o, qkv, ot, lse, tok, gain1, w_qkv
    )
    w_in_grad, w_out_grad = collect(dw_in, dw_out)
    out = call(out_body, [((ROWS, D), BF16)], 4)(y, mid, gates, routes)[0]
    grads, small = totals(grads, small)
    return (
        out[None],
        tok_grad[None],
        small[40],
        grads[:, : 3 * D].astype(F32),
        grads[:, 3 * D :].astype(F32),
        small[32],
        small[:32].T * (1 - frozen).astype(F32)[None, :],
        w_in_grad.astype(F32) * keep[:, None, None],
        w_out_grad.astype(F32) * keep[:, None, None],
    )


def solution(mesh):
    fine = Mesh(mesh.devices.reshape(2, 4, 2, 4, 2), ALL)
    seq, exp = ("zh", "x"), ("zl", "y", "c")
    rows, rest = P(exp, seq, None), P()
    in_specs = (rows, rows, rest, rest, rest, rest, rest, P(exp, None, seq), rows, rows, rest)
    out_specs = (rows, rows, rest, rest, rest, rest, rest, P(exp, None, seq), rows)
    return jax.shard_map(on_device, mesh=fine, in_specs=in_specs, out_specs=out_specs, check_vma=False)
```

```python
import functools
import math

import jax
import jax.numpy as jnp
from jax import lax
from jax.experimental import pallas as pl
from jax.experimental.pallas import tpu as pltpu
from jax.sharding import Mesh
from jax.sharding import PartitionSpec as P

D = 768
HEADS = 12
HEAD_DIM = 64
EXPERTS = 32
CAP = 32
ROWS = 256
BLOCKS = 8
FF = 3072
SLOTS = EXPERTS * CAP
EXTRA = 128
EPS = 1e-5
SCALE = HEAD_DIM ** -0.5
LOG2E = math.log2(math.e)
BF16 = jnp.bfloat16
F32 = jnp.float32
NEG = -1e30

SEQ = ("zh", "x")
MESH = pl.DeviceIdType.MESH
ALL = ("zh", "x", "zl", "y", "c")


def dot(a, b, ca=1, cb=0):
    return lax.dot_general(a, b, (((ca,), (cb,)), ((), ())), preferred_element_type=F32)


def params(mb=56):
    return pltpu.CompilerParams(vmem_limit_bytes=mb * 2**20)


def vspec(n):
    return [pl.BlockSpec(memory_space=pltpu.VMEM)] * n


def call(body, outs, n_in, scratch=(), **kw):
    return pl.pallas_call(
        body,
        out_shape=[jax.ShapeDtypeStruct(s, t) for s, t in outs],
        in_specs=vspec(n_in),
        out_specs=vspec(len(outs)),
        scratch_shapes=list(scratch),
        compiler_params=params(),
        **kw,
    )


def norm(v):
    mean = jnp.mean(v, axis=-1, keepdims=True)
    centred = v - mean
    inv = lax.rsqrt(jnp.mean(centred * centred, axis=-1, keepdims=True) + EPS)
    return centred * inv, inv


def norm_back(grad, gain, unit, inv):
    t = grad * gain
    m1 = jnp.mean(t, axis=-1, keepdims=True)
    m2 = jnp.mean(t * unit, axis=-1, keepdims=True)
    return inv * (t - m1 - unit * m2)


def lane_low():
    return lax.broadcasted_iota(jnp.int32, (1, 128), 1) < 64


def pair_up(wide, s):
    low = wide[:, 128 * (s // 2) : 128 * (s // 2) + 128]
    if s % 2:
        low = pltpu.roll(low, 64, 1)
    high = wide[:, 512 + 128 * (s // 4) : 640 + 128 * (s // 4)]
    if (s // 2) % 2 == 0:
        high = pltpu.roll(high, 64, 1)
    return jnp.where(lane_low(), low, high)


def unpair(tiles):
    out = []
    for t in range(4):
        out.append(
            jnp.where(lane_low(), tiles[2 * t], pltpu.roll(tiles[2 * t + 1], 64, 1))
        )
    for t in range(2):
        a = tiles[4 * t] + tiles[4 * t + 1]
        b = tiles[4 * t + 2] + tiles[4 * t + 3]
        out.append(jnp.where(lane_low(), pltpu.roll(a, 64, 1), b))
    return out


def project_body(tok_ref, gain_ref, w_ref, send_ref):
    unit, _ = norm(tok_ref[...].astype(F32))
    a1 = (unit * gain_ref[...]).astype(BF16)
    for part in range(3):
        wide = dot(a1, w_ref[:, part * D : part * D + D])
        for s in range(BLOCKS):
            send_ref[s, :, part * 128 : part * 128 + 128] = pair_up(wide, s).astype(
                BF16
            )


def unit_of(half, h, i):
    if h == 0:
        return 0, i, i + 1, i, i
    a, b = ((0, 1), (3, 2), (4, 5), (7, 6))[i]
    return 1, a + half * (b - a), 2 * i + 2, 2 * i, BLOCKS + i


def masked_scores(k, q, block, first, count):
    s = dot(k, q, 1, 1)
    start = first * ROWS
    tail = (count - first) * ROWS
    keys = lax.broadcasted_iota(jnp.int32, (tail, ROWS), 0) + start
    queries = lax.broadcasted_iota(jnp.int32, (tail, ROWS), 1) + block * ROWS
    end = jnp.where(keys <= queries, s[start:], NEG)
    return end if start == 0 else jnp.concatenate([s[:start], end], axis=0)


def head_mask(h):
    low = lane_low()
    return (low if h == 0 else jnp.logical_not(low)).astype(F32).astype(BF16)


def padded(h, t):
    zero = jnp.zeros_like(t)
    return jnp.concatenate([t, zero] if h == 0 else [zero, t], axis=0).T


def attend_forward(half, qkv_ref, o_ref, ot_ref, lse_ref, vt_ref, arrived, leave):
    c = SCALE * LOG2E
    for pair in range(BLOCKS // 2):
        for b in (2 * pair, 2 * pair + 1):
            arrived(b)
            vt_ref[:, b * ROWS : (b + 1) * ROWS] = qkv_ref[b, :, 256:384].T
            o_ref[b] = jnp.zeros((ROWS, 128), BF16)
        for unit in ((1, pair), (0, 2 * pair), (0, 2 * pair + 1)):
            h, block, count, first, u = unit_of(half, *unit)
            q = qkv_ref[block, :, 0:128] * head_mask(h)
            k = qkv_ref[0:count, :, 128:256].reshape(count * ROWS, 128)
            s = masked_scores(k, q, block, first, count)
            top = jnp.max(s, axis=0, keepdims=True)
            p = jnp.exp2((s - top) * c)
            total = jnp.sum(p, axis=0, keepdims=True)
            ot = dot(vt_ref[64 * h : 64 * h + 64, 0 : count * ROWS], p.astype(BF16))
            ot = ot / total
            ot_ref[u] = ot
            lse_ref[u] = jnp.broadcast_to(top * c + jnp.log2(total), (8, ROWS))
            o_ref[block] = (o_ref[block].astype(F32) + padded(h, ot)).astype(BF16)
        leave(2 * pair)
        leave(2 * pair + 1)


def attend_backward(half, qkv_ref, do_ref, ot_ref, lse_ref, out_ref, kt_ref, dk_ref, dv_ref, arrived, leave, beside):
    c = SCALE * LOG2E
    for b in range(BLOCKS):
        kt_ref[:, b * ROWS : (b + 1) * ROWS] = qkv_ref[b, :, 128:256].T
        out_ref[b, :, 0:128] = jnp.zeros((ROWS, 128), BF16)
    dk_ref[...] = jnp.zeros_like(dk_ref)
    dv_ref[...] = jnp.zeros_like(dv_ref)

    def one(h, i):
        h, block, count, first, u = unit_of(half, h, i)
        rows = count * ROWS
        q = qkv_ref[block, :, 0:128] * head_mask(h)
        do = do_ref[block] * head_mask(h)
        dot_rows = do.astype(F32).T[64 * h : 64 * h + 64]
        delta = jnp.sum(dot_rows * ot_ref[u], axis=0, keepdims=True)
        lse = lse_ref[u][0:1]
        k = qkv_ref[0:count, :, 128:256].reshape(rows, 128)
        v = qkv_ref[0:count, :, 256:384].reshape(rows, 128)
        s = masked_scores(k, q, block, first, count)
        p = jnp.exp2(s * c - lse)
        dp = dot(v, do, 1, 1)
        ds = (p * (dp - delta)).astype(BF16)
        dv_ref[0:rows] += dot(p.astype(BF16), do)
        dk_ref[0:rows] += dot(ds, q)
        dqt = dot(kt_ref[64 * h : 64 * h + 64, 0:rows], ds) * SCALE
        out_ref[block, :, 0:128] = (
            out_ref[block, :, 0:128].astype(F32) + padded(h, dqt)
        ).astype(BF16)

    for pair in reversed(range(BLOCKS // 2)):
        b = 2 * pair + 1
        arrived(b)
        arrived(b - 1)
        one(1, pair)
        for b in (b, b - 1):
            one(0, b)
            at = slice(b * ROWS, (b + 1) * ROWS)
            out_ref[b, :, 128:256] = (dk_ref[at] * SCALE).astype(BF16)
            out_ref[b, :, 256:384] = dv_ref[at].astype(BF16)
            leave(b)
        beside(pair)


def choices(routes):
    ids = lax.broadcasted_iota(jnp.int32, (ROWS, EXPERTS), 1)
    e1, e2 = routes[:, 0:1], routes[:, 1:2]
    m1, m2 = (e1 == ids).astype(F32), (e2 == ids).astype(F32)
    r = lax.broadcasted_iota(jnp.int32, (ROWS, ROWS), 0)
    k = lax.broadcasted_iota(jnp.int32, (ROWS, ROWS), 1)
    lower = (k < r).astype(F32).astype(BF16)
    earlier = dot(lower, (m1 + m2).astype(BF16))
    s1 = jnp.sum(earlier * m1, axis=1, keepdims=True)
    s2 = jnp.sum(earlier * m2, axis=1, keepdims=True)

    return m1, m2, (e1 * CAP).astype(F32) + s1, (e2 * CAP).astype(F32) + s2


def chosen(col):
    at = lax.broadcasted_iota(jnp.int32, (ROWS, SLOTS), 1).astype(F32)
    return (at == col).astype(F32).astype(BF16)


def chosen_t(col):
    row = jnp.broadcast_to(col, (ROWS, 128)).T[0:1]
    at = lax.broadcasted_iota(jnp.int32, (SLOTS, ROWS), 0).astype(F32)
    return (at == row).astype(F32).astype(BF16)


def two_parts(v):
    lane = lax.broadcasted_iota(jnp.int32, (v.shape[0], EXTRA), 1)
    high = v.astype(BF16).astype(F32)
    return jnp.where(lane == 0, high, jnp.where(lane == 1, v - high, 0.0)).astype(BF16)


def from_parts(v):
    lane = lax.broadcasted_iota(jnp.int32, v.shape, 1)
    return jnp.sum(jnp.where(lane < 2, v.astype(F32), 0.0), axis=1, keepdims=True)


def deal_body(cot_ref, routes_ref, send_ref):
    _, _, c1, c2 = choices(routes_ref[...])
    either = chosen_t(c1) + chosen_t(c2)
    send_ref[...] = dot(either, cot_ref[...]).astype(BF16)


def middle_body(o_ref, tok_ref, w_o_ref, gain_ref, gate_ref, routes_ref, mid_ref, att_ref, send_ref, gates_ref):
    tiles = unpair([o_ref[s].astype(F32) for s in range(BLOCKS)])
    o = jnp.concatenate([t.astype(BF16) for t in tiles], axis=1)
    att_ref[...] = o
    mid = tok_ref[...].astype(F32) + dot(o, w_o_ref[...])
    mid_ref[...] = mid
    unit, _ = norm(mid)
    a2 = (unit * gain_ref[...]).astype(BF16)
    logits = dot(a2, gate_ref[...])
    m1, m2, c1, c2 = choices(routes_ref[...])
    l1 = jnp.sum(logits * m1, axis=1, keepdims=True)
    l2 = jnp.sum(logits * m2, axis=1, keepdims=True)
    top = jnp.maximum(l1, l2)
    x1, x2 = jnp.exp(l1 - top), jnp.exp(l2 - top)
    g1, g2 = x1 / (x1 + x2), x2 / (x1 + x2)
    lane = lax.broadcasted_iota(jnp.int32, (ROWS, 128), 1)
    gates_ref[...] = jnp.where(lane == 0, g1, g2)
    t1, t2 = chosen_t(c1), chosen_t(c2)
    send_ref[:, 0:D] = dot(t1 + t2, a2).astype(BF16)
    send_ref[:, D:] = (dot(t1, two_parts(g1)) + dot(t2, two_parts(g2))).astype(BF16)


def erf_parts(h):
    x = jnp.abs(h) * (0.5**0.5)
    t = 1.0 / (1.0 + 0.3275911 * x)
    e = jnp.exp(-0.5 * h * h)
    poly = t * (
        0.254829592
        + t * (-0.284496736 + t * (1.421413741 + t * (-1.453152027 + t * 1.061405429)))
    )
    tail = 0.5 * poly * e
    return jnp.where(h >= 0, 1.0 - tail, tail), e * (1.0 / math.sqrt(2.0 * math.pi))


def div(a, b):
    return lax.div(a, jnp.int32(b))


def rem(a, b):
    return lax.rem(a, jnp.int32(b))


def coords():
    return tuple(lax.axis_index(a) for a in ALL)


def near(x, pair):
    return x + rem(div(x, 2) + pair, 2) * (3 - 2 * x)


def neighbour(x):
    return x + 1 - 2 * rem(x, 2)


def expert_of(zh, x, zl, y):
    return 4 * (4 * zl + y) + 2 * div(x, 2) + zh


def remote(src, dst, send, recv, device):
    return pltpu.make_async_remote_copy(
        src_ref=src,
        dst_ref=dst,
        send_sem=send,
        recv_sem=recv,
        device_id=device,
        device_id_type=MESH,
    )


def await_bytes(ref, sem):
    pltpu.make_async_copy(ref, ref, sem).wait()


def chip_partner(me, k):
    zh, x, zl, y, c = me
    return (
        rem(zh + div(k, 8), 2),
        rem(x + rem(div(k, 2), 4), 4),
        zl,
        y,
        rem(c + rem(k, 2), 2),
    )


def core_partner(me, k):
    return me[:4] + (rem(me[4] + k, 2),)


def row_partner(me, k):
    zh, x, zl, y, c = me
    return (
        rem(zh + rem(div(k, 8), 2), 2),
        x + div(k, 16) * (3 - 2 * x),
        rem(zl + rem(div(k, 4), 2), 2),
        rem(y + rem(k, 4), 4),
        c,
    )


def head_partner(me, k):
    zh, x, zl, y, c = me
    t = rem(zh * 4 + x + k, 8)
    return t, (div(t, 4), rem(t, 4), zl, y, c)


def greet(me, partner, count):
    barrier = pltpu.get_barrier_semaphore()

    def one(k, carry):
        pl.semaphore_signal(
            barrier, inc=1, device_id=partner(me, k), device_id_type=MESH
        )
        return carry

    lax.fori_loop(1, count, one, 0)
    return count - 1


def greet_all(*groups):
    me = coords()
    total = sum(greet(me, partner, count) for partner, count in groups)
    pl.semaphore_wait(pltpu.get_barrier_semaphore(), total)
    return me


class HeadSwap:
    def __init__(self, me, send, recv, sems):
        self.me, self.send, self.recv, self.sems = me, send, recv, sems
        self.place = me[0] * 4 + me[1]

    def leave(self, t):
        s = self.place
        zh, x, zl, y, c = self.me
        local = pltpu.make_async_copy(self.send.at[t], self.recv.at[t], self.sems.at[1, t])
        away = remote(
            self.send.at[t], self.recv.at[s], self.sems.at[0, t], self.sems.at[1, s], (t // 4, t % 4, zl, y, c)
        )
        pl.when(s == t)(local.start)
        pl.when(s != t)(away.start)

    def start(self):
        s = self.place
        pltpu.make_async_copy(self.send.at[s], self.recv.at[s], self.sems.at[1, s]).start()
        for k in (2, 4, 6, 1, 3, 5, 7):
            t, device = head_partner(self.me, jnp.int32(k))
            remote(self.send.at[t], self.recv.at[s], self.sems.at[0, t], self.sems.at[1, s], device).start()

    def arrived(self, t):
        await_bytes(self.recv.at[t], self.sems.at[1, t])

    def wait_send(self):
        for k in range(1, 8):
            t, _ = head_partner(self.me, jnp.int32(k))
            await_bytes(self.send.at[t], self.sems.at[0, t])


class RowSwap:
    def __init__(self, me, send, recv, sems, back=False):
        self.me, self.send, self.recv, self.sems = me, send, recv, sems
        self.back = back

    def ends(self, k):
        zh, x, zl, y, c = self.me
        device = row_partner(self.me, k)
        mirrored = 16 * div(k, 16)
        if self.back:
            src = mirrored + 8 * device[0] + 4 * device[2] + device[3]
            dst = expert_of(zh, x, zl, y)
        else:
            src = expert_of(*device[:4])
            dst = mirrored + 8 * zh + 4 * zl + y
        rows = lambda n: pl.ds(pl.multiple_of(n * CAP, CAP), CAP)
        return self.send.at[rows(src)], self.recv.at[rows(dst)], device

    def start(self):
        src, dst, _ = self.ends(jnp.int32(0))
        pltpu.make_async_copy(src, dst, self.sems.at[1]).start()

        def one(k, carry):
            src, dst, device = self.ends(rem(9 * k, 32))
            remote(src, dst, self.sems.at[0], self.sems.at[1], device).start()
            return carry

        lax.fori_loop(1, 32, one, 0)

    def wait_recv(self):
        await_bytes(self.recv, self.sems.at[1])

    def wait_send(self):
        await_bytes(self.send.at[pl.ds(0, 31 * CAP)], self.sems.at[0])

    def wait(self):
        self.wait_recv()
        self.wait_send()


def remote_params(n, mb=60):
    return pltpu.CompilerParams(
        vmem_limit_bytes=mb * 2**20, collective_id=n, has_side_effects=True
    )


VMEM = pl.BlockSpec(memory_space=pltpu.VMEM)
ANY = pl.BlockSpec(memory_space=pl.ANY)
DMA = pltpu.SemaphoreType.DMA


class Weights:
    def __init__(self, me, w_in, w_out, full_in, full_out, sems):
        self.me, self.refs, self.full, self.sems = me, (w_in, w_out), (full_in, full_out), sems

    def place(self, i, x, zh):
        at = pl.ds(pl.multiple_of(zh * 384, 128), 384)
        return self.full[0].at[x, :, at] if i == 0 else self.full[1].at[x, at, :]

    def first(self, i, b):
        zh, x, zl, y, c = self.me
        device = (jnp.int32(b), near(x, c), zl, y, zh)
        copy = remote(
            self.refs[i].at[b], self.place(i, x, zh), self.sems.at[0, i, b], self.sems.at[1, i, x], device
        )
        local = pltpu.make_async_copy(
            self.refs[i].at[b], self.place(i, x, zh), self.sems.at[1, i, x]
        )
        own = jnp.logical_and(
            jnp.logical_and(zh == b, div(x, 2) == c), zh == c
        )
        return copy, local, own

    def start(self, i):
        for b in range(2):
            copy, local, own = self.first(i, b)
            pl.when(own)(local.start)
            pl.when(jnp.logical_not(own))(copy.start)

    def forward(self, i, x, step):
        zh, me_x, zl, y, c = self.me
        piece = self.place(i, x, c)
        device = (zh, neighbour(me_x), zl, y, c) if step == 2 else (zh, me_x, zl, y, 1 - c)
        return remote(piece, piece, self.sems.at[2 * step - 2, i, x], self.sems.at[2 * step - 1, i, x], device)

    def sources(self, step):
        x = self.me[1]
        if step == 1:
            return x, 3 - x
        return neighbour(x), 3 - neighbour(x)

    def second(self, i):
        for x in self.sources(1):
            await_bytes(self.place(i, x, self.me[4]), self.sems.at[1, i, x])
            self.forward(i, x, 2).start()
            self.forward(i, x, 3).start()

    def third(self, i):
        for x in self.sources(2):
            self.forward(i, x, 2).wait_recv()
            self.forward(i, x, 3).start()

    def finish(self, i):
        for b in range(2):
            copy, _, own = self.first(i, b)
            pl.when(jnp.logical_not(own))(copy.wait_send)
        for x in self.sources(1):
            self.forward(i, x, 2).wait_send()
        for x in range(4):
            self.forward(i, jnp.int32(x), 3).wait()


def front_body(tok_ref, cot_ref, gain1_ref, w_qkv_ref, w_o_ref, gain2_ref, gate_ref, routes_ref, w_in_ref, w_out_ref,
               qkv_ref, x_ref, c_ref, full_in_ref, full_out_ref, mid_ref, att_ref, gates_ref, ot_ref, lse_ref,
               qkv_send, o_send, o_recv, x_send, c_send, vt_ref, head_sems, row_sems, weight_sems):
    me = greet_all((chip_partner, 16), (row_partner, 32))
    weights = Weights(me, w_in_ref, w_out_ref, full_in_ref, full_out_ref, weight_sems)
    heads = HeadSwap(me, qkv_send, qkv_ref, head_sems.at[0])
    heads_back = HeadSwap(me, o_send, o_recv, head_sems.at[1])
    rows_c = RowSwap(me, c_send, c_ref, row_sems.at[0])
    rows_x = RowSwap(me, x_send, x_ref, row_sems.at[1])
    weights.start(0)
    project_body(tok_ref, gain1_ref, w_qkv_ref, qkv_send)
    heads.start()
    deal_body(cot_ref, routes_ref, c_send)
    weights.start(1)
    weights.second(0)
    attend_forward(rem(me[1], 2), qkv_ref, o_send, ot_ref, lse_ref, vt_ref, heads.arrived, heads_back.leave)
    rows_c.start()
    weights.second(1)
    weights.third(0)
    for t in range(BLOCKS):
        heads_back.arrived(t)
    middle_body(o_recv, tok_ref, w_o_ref, gain2_ref, gate_ref, routes_ref, mid_ref, att_ref, x_send, gates_ref)
    rows_x.start()
    weights.third(1)
    rows_c.wait()
    heads.wait_send()
    heads_back.wait_send()
    weights.finish(0)
    weights.finish(1)
    rows_x.wait()


def front(tok, cot, gain1, w_qkv, w_o, gain2, gate, routes, w_in, w_out):
    outs = [
        ((BLOCKS, ROWS, 384), BF16, VMEM),
        ((SLOTS, D + EXTRA), BF16, VMEM),
        ((SLOTS, D), BF16, VMEM),
        ((4, D, D), BF16, ANY),
        ((4, D, D), BF16, ANY),
        ((ROWS, D), F32, VMEM),
        ((ROWS, D), BF16, VMEM),
        ((ROWS, 128), F32, VMEM),
        ((12, 64, ROWS), F32, VMEM),
        ((12, 8, ROWS), F32, VMEM),
    ]
    return pl.pallas_call(
        front_body,
        out_shape=[jax.ShapeDtypeStruct(s, t) for s, t, _ in outs],
        in_specs=[VMEM] * 8 + [ANY] * 2,
        out_specs=[m for _, _, m in outs],
        scratch_shapes=[
            pltpu.VMEM((BLOCKS, ROWS, 384), BF16),
            pltpu.VMEM((BLOCKS, ROWS, 128), BF16),
            pltpu.VMEM((BLOCKS, ROWS, 128), BF16),
            pltpu.VMEM((SLOTS, D + EXTRA), BF16),
            pltpu.VMEM((SLOTS, D), BF16),
            pltpu.VMEM((128, BLOCKS * ROWS), BF16),
            DMA((2, 2, 8)),
            DMA((2, 2)),
            DMA((6, 2, 4)),
        ],
        compiler_params=remote_params(0),
    )(tok, cot, gain1, w_qkv, w_o, gain2, gate, routes, w_in, w_out)


STEP = 256
CHUNKS = 4
TILES = SLOTS // STEP


def row_block(r):
    return pl.ds(pl.multiple_of(r * STEP, STEP), STEP)


def expert_body(x_ref, c_ref, win_ref, wout_ref, ret_ref, y_ref, dwin_ref, dwout_ref,
                g_ref, dh_ref, dx_ref, dg_ref, xg_ref, cg_ref, ret_send, out_in, out_out, got_in, got_out, sems, core_sems):
    me = greet_all((row_partner, 32), (core_partner, 2))
    c = me[4]
    sibling = core_partner(me, 1)
    rows_ret = RowSwap(me, ret_send, ret_ref, sems.at[0], back=True)
    dx_ref[...] = jnp.zeros_like(dx_ref)
    dg_ref[...] = jnp.zeros_like(dg_ref)

    def hidden(n, carry):
        j, r = div(n, TILES), rem(n, TILES)
        at = row_block(r)
        h = dot(x_ref[at, 0:D], win_ref[j])
        cw = dot(c_ref[at, :], wout_ref[j], 1, 1)
        phi, density = erf_parts(h)
        g = h * phi
        dh = ((phi + h * density) * cw).astype(BF16)
        g_ref[j, at, :] = g.astype(BF16)
        dh_ref[j, at, :] = dh
        prod = g * cw
        part = prod[:, 0:128]
        for t in range(1, D // 128):
            part = part + prod[:, 128 * t : 128 * t + 128]
        dg_ref[at, :] += part
        dx_ref[at, :] += dot(dh, win_ref[j], 1, 1)
        return carry

    lax.fori_loop(0, CHUNKS * TILES, hidden, 0)

    def scale(r, carry):
        at = row_block(r)
        gate = from_parts(x_ref[at, D:])
        ret_send[at, 0:D] = (dx_ref[at, :] * gate).astype(BF16)
        ret_send[at, D:] = two_parts(jnp.sum(dg_ref[at, :], axis=1, keepdims=True))
        return carry

    lax.fori_loop(0, TILES, scale, 0)
    rows_ret.start()

    def produce(r, carry):
        at = row_block(r)
        gate = from_parts(x_ref[at, D:])
        xg_ref[at, :] = (x_ref[at, 0:D].astype(F32) * gate).astype(BF16)
        cg_ref[at, :] = (c_ref[at, :].astype(F32) * gate).astype(BF16)
        y = dot(g_ref[0, at, :], wout_ref[0])
        for j in range(1, CHUNKS):
            y = y + dot(g_ref[j, at, :], wout_ref[j])
        y_ref[at, :] = y.astype(BF16)
        return carry

    lax.fori_loop(0, TILES, produce, 0)

    def over(i, j):
        pair = (out_in, got_in) if i == 0 else (out_out, got_out)
        return remote(pair[0].at[j], pair[1].at[j], core_sems.at[0, i, j], core_sems.at[1, i, j], sibling)

    def grads(j, carry):
        part = dot(xg_ref[...], dh_ref[j], 0, 0)
        out_in[j] = jnp.where(c == 0, part[:, 384:], part[:, :384]).astype(BF16)
        dwin_ref[j] = jnp.where(c == 0, part[:, :384], part[:, 384:]).astype(BF16)
        over(0, j).start()
        part = dot(g_ref[j], cg_ref[...], 0, 0)
        out_out[j] = jnp.where(c == 0, part[384:], part[:384]).astype(BF16)
        dwout_ref[j] = jnp.where(c == 0, part[:384], part[384:]).astype(BF16)
        over(1, j).start()
        return carry

    lax.fori_loop(0, CHUNKS, grads, 0)

    def add(j, carry):
        over(0, j).wait()
        dwin_ref[j] = (dwin_ref[j].astype(F32) + got_in[j].astype(F32)).astype(BF16)
        over(1, j).wait()
        dwout_ref[j] = (dwout_ref[j].astype(F32) + got_out[j].astype(F32)).astype(BF16)
        return carry

    lax.fori_loop(0, CHUNKS, add, 0)
    rows_ret.wait()


def experts(x, c, w_in, w_out):
    return pl.pallas_call(
        expert_body,
        out_shape=[
            jax.ShapeDtypeStruct((SLOTS, D + EXTRA), BF16),
            jax.ShapeDtypeStruct((SLOTS, D), BF16),
            jax.ShapeDtypeStruct((CHUNKS, D, 384), BF16),
            jax.ShapeDtypeStruct((CHUNKS, 384, D), BF16),
        ],
        in_specs=[VMEM] * 4,
        out_specs=[VMEM] * 4,
        scratch_shapes=[
            pltpu.VMEM((CHUNKS, SLOTS, D), BF16),
            pltpu.VMEM((CHUNKS, SLOTS, D), BF16),
            pltpu.VMEM((SLOTS, D), F32),
            pltpu.VMEM((SLOTS, 128), F32),
            pltpu.VMEM((SLOTS, D), BF16),
            pltpu.VMEM((SLOTS, D), BF16),
            pltpu.VMEM((SLOTS, D + EXTRA), BF16),
            pltpu.VMEM((CHUNKS, D, 384), BF16),
            pltpu.VMEM((CHUNKS, 384, D), BF16),
            pltpu.VMEM((CHUNKS, D, 384), BF16),
            pltpu.VMEM((CHUNKS, 384, D), BF16),
            DMA((2, 2)),
            DMA((2, 2, CHUNKS)),
        ],
        compiler_params=remote_params(1),
    )(x, c, w_in, w_out)


def back_body(ret_ref, cot_ref, routes_ref, gates_ref, mid_ref, gain_ref, gate_w_ref, w_o_ref,
              send_ref, dmid_ref, gate_grad_ref, gain_grad_ref):
    m1, m2, c1, c2 = choices(routes_ref[...])
    s1, s2 = chosen(c1), chosen(c2)
    g1, g2 = gates_ref[:, 0:1], gates_ref[:, 1:2]
    extra = ret_ref[:, D:]
    d1, d2 = from_parts(dot(s1, extra)), from_parts(dot(s2, extra))
    dl = g1 * g2 * (d1 - d2)
    dlogits = (m1 - m2) * dl
    unit, inv = norm(mid_ref[...])
    high = dlogits.astype(BF16)
    low = (dlogits - high.astype(F32)).astype(BF16)
    gate_w = gate_w_ref[...]
    da2 = dot(s1 + s2, ret_ref[:, 0:D]) + dot(high, gate_w, 1, 1) + dot(low, gate_w, 1, 1)
    dmid = cot_ref[...].astype(F32) + norm_back(da2, gain_ref[...], unit, inv)
    dmid_ref[...] = dmid
    do = dot(dmid.astype(BF16), w_o_ref[...], 1, 1)
    for s in range(BLOCKS):
        send_ref[s] = pair_up(do, s).astype(BF16)

    def later():
        a2 = (unit * gain_ref[...]).astype(BF16)
        gate_grad_ref[...] = dot(high, a2, 0, 0) + dot(low, a2, 0, 0)
        gain_grad_ref[...] = jnp.sum(da2 * unit, axis=0, keepdims=True)

    return later


def axis_place(me, a):
    zh, x, zl, y, c = me
    return (x, y, 2 * zh + zl)[a]


def axis_peer(me, a, k):
    zh, x, zl, y, c = me
    p = rem(axis_place(me, a) + k, 4)
    if a == 0:
        return p, (zh, p, zl, y, c)
    if a == 1:
        return p, (zh, x, zl, p, c)
    return p, (div(p, 2), x, rem(p, 2), y, c)


def multiple(n, w):
    return pl.ds(pl.multiple_of(n * w, w), w)


PEERS = (1, 2, 3)


class GroupSum:
    def __init__(self, me, g, axes, out, bufs, sems):
        self.me, self.g, self.axes, self.out, self.sems = me, g, axes, out, sems.at[g]
        self.s0, self.r0, self.a0, self.r1, self.a1, self.s2, self.r2, self.r3 = [b.at[g] for b in bufs]
        self.place = [axis_place(me, a) for a in axes]
        self.c = me[4]

    def copy(self, stage, k, src, dst):
        if stage in (0, 6):
            device = core_partner(self.me, 1)
        else:
            device = axis_peer(self.me, self.axes[(0, 0, 1, 2, 1, 0)[stage]], jnp.int32(k))[1]
        return remote(src, dst, self.sems.at[stage, 0, k], self.sems.at[stage, 1, k], device)

    def peer(self, t, k):
        return axis_peer(self.me, self.axes[t], jnp.int32(k))[0]

    def swap(self):
        return self.copy(0, 0, self.s0, self.r0)

    def scatter1(self, k):
        return self.copy(1, k, self.s0.at[multiple(self.peer(0, k), 192)], self.r1.at[k - 1])

    def scatter2(self, k):
        return self.copy(2, k, self.s2.at[multiple(self.peer(1, k), 48)], self.r2.at[k - 1])

    def share(self, k):
        mine = self.r3.at[self.place[2]]
        return self.copy(3, k, mine, mine)

    def block(self, rows):
        base = self.g * D + self.c * 384
        lanes = pl.ds(pl.multiple_of(base, 128), 384)
        i, j = self.place[0], self.place[1]
        if rows == 48:
            return self.out.at[multiple(4 * i + j, 48), lanes]
        if rows == 192:
            return self.out.at[multiple(i, 192), lanes]
        return self.out.at[:, lanes]

    def gather(self, stage, k):
        ref = self.block((48, 192, 768)[stage - 4])
        return self.copy(stage, k, ref, ref)

    def begin(self, grad):
        self.s0[...] = grad(1 - self.c).astype(BF16)
        self.swap().start()
        self.a0[...] = grad(self.c)

    def step1(self):
        self.swap().wait()
        self.a0[...] += self.r0[...].astype(F32)
        self.s0[...] = self.a0[...].astype(BF16)
        for k in PEERS:
            self.scatter1(k).start()

    def step2(self):
        for k in PEERS:
            self.scatter1(k).wait_recv()
        mine = self.a0[multiple(self.place[0], 192), :]
        for k in PEERS:
            mine = mine + self.r1[k - 1].astype(F32)
        self.a1[...] = mine
        self.s2[...] = mine.astype(BF16)
        for k in PEERS:
            self.scatter2(k).start()

    def step3(self):
        for k in PEERS:
            self.scatter2(k).wait_recv()
        mine = self.a1[multiple(self.place[1], 48), :]
        for k in PEERS:
            mine = mine + self.r2[k - 1].astype(F32)
        self.r3[self.place[2]] = mine.astype(BF16)
        for k in PEERS:
            self.share(k).start()

    def step4(self):
        for k in PEERS:
            p = axis_peer(self.me, self.axes[2], jnp.int32(k))[0]
            self.copy(3, 4 - k, self.r3.at[p], self.r3.at[p]).wait_recv()
        total = (self.r3[0].astype(F32) + self.r3[1].astype(F32)) + (
            self.r3[2].astype(F32) + self.r3[3].astype(F32)
        )
        self.block(48)[...] = total.astype(BF16)
        for k in PEERS:
            self.gather(4, k).start()

    def step5(self):
        for k in PEERS:
            self.gather(4, k).wait_recv()
        for k in PEERS:
            self.gather(5, k).start()

    def step6(self):
        for k in PEERS:
            self.gather(5, k).wait_recv()
        self.gather(6, 0).start()

    def finish(self):
        self.gather(6, 0).wait()
        for k in PEERS:
            self.scatter1(k).wait_send()
            self.scatter2(k).wait_send()
            self.share(k).wait_send()
            self.gather(4, k).wait_send()
            self.gather(5, k).wait_send()


class SmallSum:
    def __init__(self, me, mine, slots, sems):
        self.me, self.mine, self.slots, self.sems = me, mine, slots, sems

    def swap(self):
        return remote(self.mine.at[0], self.slots.at[0], self.sems.at[0, 0], self.sems.at[1, 0], core_partner(self.me, 1))

    def share(self, a, k):
        n = 3 * a + k
        return remote(self.mine.at[a + 1], self.slots.at[1 + 4 * a + axis_place(self.me, a)], self.sems.at[0, n],
                      self.sems.at[1, n], axis_peer(self.me, a, jnp.int32(k))[1])

    def begin(self):
        self.swap().start()

    def step(self, a):
        if a == 0:
            self.swap().wait_recv()
            total = self.mine[0] + self.slots[0]
        else:
            total = self.total(a - 1)
        if a < 3:
            self.mine[a + 1] = total
            for k in PEERS:
                self.share(a, k).start()
        return total

    def total(self, a):
        for k in PEERS:
            self.share(a, k).wait_recv()
        s, n = self.slots, 1 + 4 * a
        s[n + axis_place(self.me, a)] = self.mine[a + 1]
        return (s[n] + s[n + 1]) + (s[n + 2] + s[n + 3])

    def finish(self):
        self.swap().wait_send()
        for a in range(3):
            for k in PEERS:
                self.share(a, k).wait_send()


class Collect:
    def __init__(self, me, dw, got, fin, sems):
        self.me, self.dw, self.got, self.fin, self.sems = me, dw, got, fin, sems
        x = me[1]
        self.keep, self.pass_on = (x, 3 - x), (neighbour(x), 3 - neighbour(x))

    def second(self, i, j):
        zh, x, zl, y, c = self.me
        return remote(self.dw[i].at[self.pass_on[j]], self.got[i].at[j], self.sems.at[0, i, j], self.sems.at[1, i, j],
                      (zh, neighbour(x), zl, y, c))

    def third(self, i, j):
        zh, x, zl, y, c = self.me
        pair = div(x, 2)
        copy = remote(self.got[i].at[j], self.fin[i].at[zh], self.sems.at[2, i, j], self.sems.at[3, i, zh],
                      (c, self.keep[j], zl, y, pair))
        local = pltpu.make_async_copy(self.got[i].at[j], self.fin[i].at[zh], self.sems.at[3, i, zh])
        if j == 1:
            return copy, None, None
        return copy, local, jnp.logical_and(zh == c, pair == c)

    def begin(self):
        for i in range(2):
            for j in range(2):
                self.second(i, j).start()

    def go_on(self, i):
        for j in range(2):
            self.second(i, j).wait_recv()
            self.got[i][j] = (self.dw[i][self.keep[j]].astype(F32) + self.got[i][j].astype(F32)).astype(BF16)
            copy, local, own = self.third(i, j)
            if j == 1:
                copy.start()
            else:
                pl.when(own)(local.start)
                pl.when(jnp.logical_not(own))(copy.start)

    def finish(self):
        for i in range(2):
            for j in range(2):
                self.second(i, j).wait_send()
                copy, _, own = self.third(i, j)
                if j == 1:
                    copy.wait_send()
                else:
                    pl.when(jnp.logical_not(own))(copy.wait_send)
            for b in range(2):
                await_bytes(self.fin[i].at[b], self.sems.at[3, i, b])


def rear_body(ret_ref, cot_ref, routes_ref, gates_ref, mid_ref, att_ref, gain2_ref, gate_w_ref, w_o_ref,
              qkv_ref, ot_ref, lse_ref, tok_ref, gain1_ref, w_qkv_ref, y_ref, dw_in_ref, dw_out_ref,
              tok_grad_ref, grads_ref, early_ref, late_ref, out_ref, fin_in, fin_out,
              dmid_ref, do_send, do_recv, dqkv_send, dqkv_recv, kt_ref, dk_ref, dv_ref, y_recv, d_ref, datt_ref,
              got_in, got_out,
              s0, r0, a0, r1, a1, s2, r2, r3, early, early_slots, late, late_slots,
              head_sems, row_sems, collect_sems, group_sems, small_sems):
    me = greet_all((chip_partner, 16), (row_partner, 32))
    heads = HeadSwap(me, do_send, do_recv, head_sems.at[0])
    heads_back = HeadSwap(me, dqkv_send, dqkv_recv, head_sems.at[1])
    rows_y = RowSwap(me, y_ref, y_recv, row_sems, back=True)
    collect = Collect(me, (dw_in_ref, dw_out_ref), (got_in, got_out), (fin_in, fin_out), collect_sems)
    bufs = (s0, r0, a0, r1, a1, s2, r2, r3)
    orders = ((0, 1, 2), (1, 2, 0), (2, 0, 1), (1, 0, 2))
    groups = [GroupSum(me, g, orders[g], grads_ref, bufs, group_sems) for g in range(4)]
    qkv_groups, o_group = groups[:3], groups[3]
    small = SmallSum(me, early, early_slots, small_sems.at[0])
    small_late = SmallSum(me, late, late_slots, small_sems.at[1])
    early[...] = jnp.zeros_like(early)
    late[...] = jnp.zeros_like(late)

    collect.begin()
    later = back_body(ret_ref, cot_ref, routes_ref, gates_ref, mid_ref, gain2_ref, gate_w_ref, w_o_ref,
                      do_send, dmid_ref, early.at[0, 0:32], early.at[0, 32:33])
    heads.start()
    rows_y.start()
    later()
    small.begin()
    datt_ref[...] = dmid_ref[...].astype(BF16)
    o_group.begin(lambda n: dot(att_ref[...], datt_ref[:, pl.ds(pl.multiple_of(n * 384, 128), 384)], 0, 0))

    def beside(pair):
        if pair == 3:
            o_group.step1()
            small.step(0)
        elif pair == 2:
            o_group.step2()
            small.step(1)
        elif pair == 1:
            o_group.step3()
            small.step(2)
        else:
            o_group.step4()
            early_ref[...] = small.step(3)

    attend_backward(rem(me[1], 2), qkv_ref, do_recv, ot_ref, lse_ref, dqkv_send, kt_ref, dk_ref, dv_ref,
                    heads.arrived, heads_back.leave, beside)
    rows_y.wait_recv()
    _, _, c1, c2 = choices(routes_ref[...])
    y = y_recv[...]
    mix = gates_ref[:, 0:1] * dot(chosen(c1), y) + gates_ref[:, 1:2] * dot(chosen(c2), y)
    out_ref[...] = (mid_ref[...] + mix).astype(BF16)
    o_group.step5()
    unit, inv = norm(tok_ref[...].astype(F32))
    a1_rows = (unit * gain1_ref[...]).astype(BF16)
    for t in range(BLOCKS):
        heads_back.arrived(t)
    for part in range(3):
        tiles = unpair(
            [dqkv_recv[s, :, part * 128 : part * 128 + 128].astype(F32) for s in range(BLOCKS)]
        )
        for t in range(6):
            d_ref[part, :, 128 * t : 128 * t + 128] = tiles[t].astype(BF16)
        qkv_groups[part].begin(
            lambda n: dot(a1_rows, d_ref[part, :, pl.ds(pl.multiple_of(n * 384, 128), 384)], 0, 0)
        )
    da1 = dot(d_ref[0], w_qkv_ref[:, 0:D], 1, 1)
    for part in (1, 2):
        da1 = da1 + dot(d_ref[part], w_qkv_ref[:, part * D : part * D + D], 1, 1)
    late[0, 0:1] = jnp.sum(da1 * unit, axis=0, keepdims=True)
    small_late.begin()
    for g in qkv_groups:
        g.step1()
    tok_grad_ref[...] = dmid_ref[...] + norm_back(da1, gain1_ref[...], unit, inv)
    small_late.step(0)
    for i in range(2):
        collect.go_on(i)
    for g in qkv_groups:
        g.step2()
    small_late.step(1)
    for g in qkv_groups:
        g.step3()
    small_late.step(2)
    for g in qkv_groups:
        g.step4()
    late_ref[...] = small_late.step(3)
    o_group.step6()
    for g in qkv_groups:
        g.step5()
    for g in qkv_groups:
        g.step6()
    small.finish()
    small_late.finish()
    heads.wait_send()
    heads_back.wait_send()
    rows_y.wait_send()
    collect.finish()
    for g in groups:
        g.finish()


def rear(*args):
    buf = lambda *s: pltpu.VMEM(s, BF16)
    f32 = lambda *s: pltpu.VMEM(s, F32)
    return pl.pallas_call(
        rear_body,
        out_shape=[
            jax.ShapeDtypeStruct((ROWS, D), F32),
            jax.ShapeDtypeStruct((D, 4 * D), BF16),
            jax.ShapeDtypeStruct((40, D), F32),
            jax.ShapeDtypeStruct((8, D), F32),
            jax.ShapeDtypeStruct((ROWS, D), BF16),
            jax.ShapeDtypeStruct((2, D, 384), BF16),
            jax.ShapeDtypeStruct((2, 384, D), BF16),
        ],
        in_specs=[VMEM] * len(args),
        out_specs=[VMEM] * 7,
        scratch_shapes=[
            f32(ROWS, D),
            buf(BLOCKS, ROWS, 128),
            buf(BLOCKS, ROWS, 128),
            buf(BLOCKS, ROWS, 384),
            buf(BLOCKS, ROWS, 384),
            buf(128, BLOCKS * ROWS),
            f32(BLOCKS * ROWS, 128),
            f32(BLOCKS * ROWS, 128),
            buf(SLOTS, D),
            buf(3, ROWS, D),
            buf(ROWS, D),
            buf(2, D, 384),
            buf(2, 384, D),
            buf(4, D, 384),
            buf(4, D, 384),
            f32(4, D, 384),
            buf(4, 3, 192, 384),
            f32(4, 192, 384),
            buf(4, 192, 384),
            buf(4, 3, 48, 384),
            buf(4, 4, 48, 384),
            f32(4, 40, D),
            f32(13, 40, D),
            f32(4, 8, D),
            f32(13, 8, D),
            DMA((2, 2, 8)),
            DMA((2,)),
            DMA((4, 2, 2)),
            DMA((4, 7, 2, 4)),
            DMA((2, 2, 10)),
        ],
        compiler_params=remote_params(2),
    )(*args)


def on_device(tokens, cotangent, gain_first, w_qkv, w_o, gain_second, w_gate, w_in, w_out, routes, frozen):
    e = (lax.axis_index("zl") * 4 + lax.axis_index("y")) * 2 + lax.axis_index("c")
    tok, cot, routes = tokens[0], cotangent[0], routes[0]
    gain1, gain2 = gain_first.reshape(1, D), gain_second.reshape(1, D)
    qkv, x_rows, c_rows, w_in_full, w_out_full, mid, att, gates, ot, lse = front(
        tok, cot, gain1, w_qkv, w_o, gain2, w_gate, routes, w_in, w_out
    )
    ret, y, dw_in, dw_out = experts(x_rows, c_rows, w_in_full, w_out_full)
    keep = (1 - lax.dynamic_slice_in_dim(frozen, 2 * e, 2)).astype(F32)
    tok_grad, grads, early, late, out, w_in_grad, w_out_grad = rear(
        ret, cot, routes, gates, mid, att, gain2, w_gate, w_o, qkv, ot, lse, tok, gain1, w_qkv, y, dw_in, dw_out
    )
    return (
        out[None],
        tok_grad[None],
        late[0],
        grads[:, : 3 * D].astype(F32),
        grads[:, 3 * D :].astype(F32),
        early[32],
        early[:32].T * (1 - frozen).astype(F32)[None, :],
        w_in_grad.astype(F32) * keep[:, None, None],
        w_out_grad.astype(F32) * keep[:, None, None],
    )


def solution(mesh):
    fine = Mesh(mesh.devices.reshape(2, 4, 2, 4, 2), ALL)
    seq, exp = ("zh", "x"), ("zl", "y", "c")
    rows, rest = P(exp, seq, None), P()
    in_specs = (rows, rows, rest, rest, rest, rest, rest, P(exp, None, seq), rows, rows, rest)
    out_specs = (rows, rows, rest, rest, rest, rest, rest, P(exp, None, seq), rows)
    return jax.shard_map(on_device, mesh=fine, in_specs=in_specs, out_specs=out_specs, check_vma=False)
```

```python
import functools
import math

import jax
import jax.numpy as jnp
from jax import lax
from jax.experimental import pallas as pl
from jax.experimental.pallas import tpu as pltpu
from jax.sharding import Mesh
from jax.sharding import PartitionSpec as P

D = 768
HEADS = 12
HEAD_DIM = 64
EXPERTS = 32
CAP = 32
ROWS = 256
BLOCKS = 8
FF = 3072
SLOTS = EXPERTS * CAP
EXTRA = 128
EPS = 1e-5
SCALE = HEAD_DIM ** -0.5
LOG2E = math.log2(math.e)
BF16 = jnp.bfloat16
F32 = jnp.float32
NEG = -1e30

SEQ = ("zh", "x")
MESH = pl.DeviceIdType.MESH
ALL = ("zh", "x", "zl", "y", "c")


def dot(a, b, ca=1, cb=0):
    return lax.dot_general(a, b, (((ca,), (cb,)), ((), ())), preferred_element_type=F32)


def params(mb=56):
    return pltpu.CompilerParams(vmem_limit_bytes=mb * 2**20)


def vspec(n):
    return [pl.BlockSpec(memory_space=pltpu.VMEM)] * n


def call(body, outs, n_in, scratch=(), **kw):
    return pl.pallas_call(
        body,
        out_shape=[jax.ShapeDtypeStruct(s, t) for s, t in outs],
        in_specs=vspec(n_in),
        out_specs=vspec(len(outs)),
        scratch_shapes=list(scratch),
        compiler_params=params(),
        **kw,
    )


def norm(v):
    mean = jnp.mean(v, axis=-1, keepdims=True)
    centred = v - mean
    inv = lax.rsqrt(jnp.mean(centred * centred, axis=-1, keepdims=True) + EPS)
    return centred * inv, inv


def norm_back(grad, gain, unit, inv):
    t = grad * gain
    m1 = jnp.mean(t, axis=-1, keepdims=True)
    m2 = jnp.mean(t * unit, axis=-1, keepdims=True)
    return inv * (t - m1 - unit * m2)


def lane_low():
    return lax.broadcasted_iota(jnp.int32, (1, 128), 1) < 64


def pair_up(wide, s):
    low = wide[:, 128 * (s // 2) : 128 * (s // 2) + 128]
    if s % 2:
        low = pltpu.roll(low, 64, 1)
    high = wide[:, 512 + 128 * (s // 4) : 640 + 128 * (s // 4)]
    if (s // 2) % 2 == 0:
        high = pltpu.roll(high, 64, 1)
    return jnp.where(lane_low(), low, high)


def unpair(tiles):
    out = []
    for t in range(4):
        out.append(
            jnp.where(lane_low(), tiles[2 * t], pltpu.roll(tiles[2 * t + 1], 64, 1))
        )
    for t in range(2):
        a = tiles[4 * t] + tiles[4 * t + 1]
        b = tiles[4 * t + 2] + tiles[4 * t + 3]
        out.append(jnp.where(lane_low(), pltpu.roll(a, 64, 1), b))
    return out


def project(tok_ref, gain_ref, part_weights, send_ref):
    unit, _ = norm(tok_ref[...].astype(F32))
    a1 = (unit * gain_ref[...]).astype(BF16)
    for part in range(3):
        wide = dot(a1, part_weights(part))
        for s in range(BLOCKS):
            send_ref[s, :, part * 128 : part * 128 + 128] = pair_up(wide, s).astype(
                BF16
            )


def unit_of(half, h, i):
    if h == 0:
        return 0, i, i + 1, i, i
    a, b = ((0, 1), (3, 2), (4, 5), (7, 6))[i]
    return 1, a + half * (b - a), 2 * i + 2, 2 * i, BLOCKS + i


def masked_scores(k, q, block, first, count):
    s = dot(k, q, 1, 1)
    start = first * ROWS
    tail = (count - first) * ROWS
    keys = lax.broadcasted_iota(jnp.int32, (tail, ROWS), 0) + start
    queries = lax.broadcasted_iota(jnp.int32, (tail, ROWS), 1) + block * ROWS
    end = jnp.where(keys <= queries, s[start:], NEG)
    return end if start == 0 else jnp.concatenate([s[:start], end], axis=0)


def head_mask(h):
    low = lane_low()
    return (low if h == 0 else jnp.logical_not(low)).astype(F32).astype(BF16)


def padded(h, t):
    zero = jnp.zeros_like(t)
    return jnp.concatenate([t, zero] if h == 0 else [zero, t], axis=0).T


def attend_forward(half, qkv_ref, o_ref, ot_ref, lse_ref, vt_ref, arrived, leave):
    c = SCALE * LOG2E
    for pair in range(BLOCKS // 2):
        for b in (2 * pair, 2 * pair + 1):
            arrived(b)
            vt_ref[:, b * ROWS : (b + 1) * ROWS] = qkv_ref[b, :, 256:384].T
            o_ref[b] = jnp.zeros((ROWS, 128), BF16)
        for unit in ((1, pair), (0, 2 * pair), (0, 2 * pair + 1)):
            h, block, count, first, u = unit_of(half, *unit)
            q = qkv_ref[block, :, 0:128] * head_mask(h)
            k = qkv_ref[0:count, :, 128:256].reshape(count * ROWS, 128)
            s = masked_scores(k, q, block, first, count)
            top = jnp.max(s, axis=0, keepdims=True)
            p = jnp.exp2((s - top) * c)
            total = jnp.sum(p, axis=0, keepdims=True)
            ot = dot(vt_ref[64 * h : 64 * h + 64, 0 : count * ROWS], p.astype(BF16))
            ot = ot / total
            ot_ref[u] = ot
            lse_ref[u] = jnp.broadcast_to(top * c + jnp.log2(total), (8, ROWS))
            o_ref[block] = (o_ref[block].astype(F32) + padded(h, ot)).astype(BF16)
        leave(2 * pair)
        leave(2 * pair + 1)


def attend_backward(half, qkv_ref, do_ref, ot_ref, lse_ref, out_ref, kt_ref, dk_ref, dv_ref, arrived, leave, beside):
    c = SCALE * LOG2E
    for b in range(BLOCKS):
        kt_ref[:, b * ROWS : (b + 1) * ROWS] = qkv_ref[b, :, 128:256].T
        out_ref[b, :, 0:128] = jnp.zeros((ROWS, 128), BF16)
    dk_ref[...] = jnp.zeros_like(dk_ref)
    dv_ref[...] = jnp.zeros_like(dv_ref)

    def one(h, i):
        h, block, count, first, u = unit_of(half, h, i)
        rows = count * ROWS
        q = qkv_ref[block, :, 0:128] * head_mask(h)
        do = do_ref[block] * head_mask(h)
        dot_rows = do.astype(F32).T[64 * h : 64 * h + 64]
        delta = jnp.sum(dot_rows * ot_ref[u], axis=0, keepdims=True)
        lse = lse_ref[u][0:1]
        k = qkv_ref[0:count, :, 128:256].reshape(rows, 128)
        v = qkv_ref[0:count, :, 256:384].reshape(rows, 128)
        s = masked_scores(k, q, block, first, count)
        p = jnp.exp2(s * c - lse)
        dp = dot(v, do, 1, 1)
        ds = (p * (dp - delta)).astype(BF16)
        dv_ref[0:rows] += dot(p.astype(BF16), do)
        dk_ref[0:rows] += dot(ds, q)
        dqt = dot(kt_ref[64 * h : 64 * h + 64, 0:rows], ds) * SCALE
        out_ref[block, :, 0:128] = (
            out_ref[block, :, 0:128].astype(F32) + padded(h, dqt)
        ).astype(BF16)

    for pair in reversed(range(BLOCKS // 2)):
        b = 2 * pair + 1
        arrived(b)
        arrived(b - 1)
        one(1, pair)
        for b in (b, b - 1):
            one(0, b)
            at = slice(b * ROWS, (b + 1) * ROWS)
            out_ref[b, :, 128:256] = (dk_ref[at] * SCALE).astype(BF16)
            out_ref[b, :, 256:384] = dv_ref[at].astype(BF16)
            leave(b)
        beside(pair)


def choices(routes):
    ids = lax.broadcasted_iota(jnp.int32, (ROWS, EXPERTS), 1)
    e1, e2 = routes[:, 0:1], routes[:, 1:2]
    m1, m2 = (e1 == ids).astype(F32), (e2 == ids).astype(F32)
    r = lax.broadcasted_iota(jnp.int32, (ROWS, ROWS), 0)
    k = lax.broadcasted_iota(jnp.int32, (ROWS, ROWS), 1)
    lower = (k < r).astype(F32).astype(BF16)
    earlier = dot(lower, (m1 + m2).astype(BF16))
    s1 = jnp.sum(earlier * m1, axis=1, keepdims=True)
    s2 = jnp.sum(earlier * m2, axis=1, keepdims=True)

    return m1, m2, (e1 * CAP).astype(F32) + s1, (e2 * CAP).astype(F32) + s2


def chosen(col):
    at = lax.broadcasted_iota(jnp.int32, (ROWS, SLOTS), 1).astype(F32)
    return (at == col).astype(F32).astype(BF16)


def chosen_t(col):
    row = jnp.broadcast_to(col, (ROWS, 128)).T[0:1]
    at = lax.broadcasted_iota(jnp.int32, (SLOTS, ROWS), 0).astype(F32)
    return (at == row).astype(F32).astype(BF16)


def two_parts(v):
    lane = lax.broadcasted_iota(jnp.int32, (v.shape[0], EXTRA), 1)
    high = v.astype(BF16).astype(F32)
    return jnp.where(lane == 0, high, jnp.where(lane == 1, v - high, 0.0)).astype(BF16)


def from_parts(v):
    lane = lax.broadcasted_iota(jnp.int32, v.shape, 1)
    return jnp.sum(jnp.where(lane < 2, v.astype(F32), 0.0), axis=1, keepdims=True)


def deal_body(cot_ref, routes_ref, send_ref):
    _, _, c1, c2 = choices(routes_ref[...])
    either = chosen_t(c1) + chosen_t(c2)
    send_ref[...] = dot(either, cot_ref[...]).astype(BF16)


def middle_body(o_ref, tok_ref, w_o, gain_ref, gate_ref, routes_ref, mid_ref, att_ref, send_ref, gates_ref):
    tiles = unpair([o_ref[s].astype(F32) for s in range(BLOCKS)])
    o = jnp.concatenate([t.astype(BF16) for t in tiles], axis=1)
    att_ref[...] = o
    mid = tok_ref[...].astype(F32) + dot(o, w_o)
    mid_ref[...] = mid
    unit, _ = norm(mid)
    a2 = (unit * gain_ref[...]).astype(BF16)
    logits = dot(a2, gate_ref[...])
    m1, m2, c1, c2 = choices(routes_ref[...])
    l1 = jnp.sum(logits * m1, axis=1, keepdims=True)
    l2 = jnp.sum(logits * m2, axis=1, keepdims=True)
    top = jnp.maximum(l1, l2)
    x1, x2 = jnp.exp(l1 - top), jnp.exp(l2 - top)
    g1, g2 = x1 / (x1 + x2), x2 / (x1 + x2)
    lane = lax.broadcasted_iota(jnp.int32, (ROWS, 128), 1)
    gates_ref[...] = jnp.where(lane == 0, g1, g2)
    t1, t2 = chosen_t(c1), chosen_t(c2)
    send_ref[:, 0:D] = dot(t1 + t2, a2).astype(BF16)
    send_ref[:, D:] = (dot(t1, two_parts(g1)) + dot(t2, two_parts(g2))).astype(BF16)


def gelu_parts(h):
    d = 1.0 + (0.3275911 * 0.5**0.5) * jnp.abs(h)
    r = pl.reciprocal(d, approx=True)
    t = r * (2.0 - d * r)
    e = jnp.exp2(h * h * (-0.5 * LOG2E))
    poly = t * (
        0.127414796
        + t * (-0.142248368 + t * (0.7107068705 + t * (-0.7265760135 + t * 0.5307027145)))
    )
    tail = poly * e
    phi = jnp.where(h >= 0, 1.0 - tail, tail)
    return h * phi, phi + h * e * (1.0 / math.sqrt(2.0 * math.pi))


def div(a, b):
    return lax.div(a, jnp.int32(b))


def rem(a, b):
    return lax.rem(a, jnp.int32(b))


def coords():
    return tuple(lax.axis_index(a) for a in ALL)


def near(x, pair):
    return x + rem(div(x, 2) + pair, 2) * (3 - 2 * x)


def neighbour(x):
    return x + 1 - 2 * rem(x, 2)


def expert_of(zh, x, zl, y):
    return 4 * (4 * zl + y) + 2 * div(x, 2) + zh


def remote(src, dst, send, recv, device):
    return pltpu.make_async_remote_copy(
        src_ref=src,
        dst_ref=dst,
        send_sem=send,
        recv_sem=recv,
        device_id=device,
        device_id_type=MESH,
    )


def await_bytes(ref, sem):
    pltpu.make_async_copy(ref, ref, sem).wait()


def chip_partner(me, k):
    zh, x, zl, y, c = me
    return (
        rem(zh + div(k, 8), 2),
        rem(x + rem(div(k, 2), 4), 4),
        zl,
        y,
        rem(c + rem(k, 2), 2),
    )


def core_partner(me, k):
    return me[:4] + (rem(me[4] + k, 2),)


def row_partner(me, k):
    zh, x, zl, y, c = me
    return (
        rem(zh + rem(div(k, 8), 2), 2),
        x + div(k, 16) * (3 - 2 * x),
        rem(zl + rem(div(k, 4), 2), 2),
        rem(y + rem(k, 4), 4),
        c,
    )


def head_partner(me, k):
    zh, x, zl, y, c = me
    t = rem(zh * 4 + x + k, 8)
    return t, (div(t, 4), rem(t, 4), zl, y, c)


def greet(me, partner, count):
    barrier = pltpu.get_barrier_semaphore()

    def one(k, carry):
        pl.semaphore_signal(
            barrier, inc=1, device_id=partner(me, k), device_id_type=MESH
        )
        return carry

    lax.fori_loop(1, count, one, 0)
    return count - 1


def greet_all(*groups):
    me = coords()
    total = sum(greet(me, partner, count) for partner, count in groups)
    pl.semaphore_wait(pltpu.get_barrier_semaphore(), total)
    return me


class HeadSwap:
    def __init__(self, me, send, recv, sems):
        self.me, self.send, self.recv, self.sems = me, send, recv, sems
        self.place = me[0] * 4 + me[1]

    def leave(self, t):
        s = self.place
        zh, x, zl, y, c = self.me
        local = pltpu.make_async_copy(self.send.at[t], self.recv.at[t], self.sems.at[1, t])
        away = remote(
            self.send.at[t], self.recv.at[s], self.sems.at[0, t], self.sems.at[1, s], (t // 4, t % 4, zl, y, c)
        )
        pl.when(s == t)(local.start)
        pl.when(s != t)(away.start)

    def start(self):
        s = self.place
        pltpu.make_async_copy(self.send.at[s], self.recv.at[s], self.sems.at[1, s]).start()
        for k in (2, 4, 6, 1, 3, 5, 7):
            t, device = head_partner(self.me, jnp.int32(k))
            remote(self.send.at[t], self.recv.at[s], self.sems.at[0, t], self.sems.at[1, s], device).start()

    def arrived(self, t):
        await_bytes(self.recv.at[t], self.sems.at[1, t])

    def wait_send(self):
        for k in range(1, 8):
            t, _ = head_partner(self.me, jnp.int32(k))
            await_bytes(self.send.at[t], self.sems.at[0, t])


class RowSwap:
    def __init__(self, me, send, recv, sems, back=False):
        self.me, self.send, self.recv, self.sems = me, send, recv, sems
        self.back = back

    def ends(self, k):
        zh, x, zl, y, c = self.me
        device = row_partner(self.me, k)
        mirrored = 16 * div(k, 16)
        if self.back:
            src = mirrored + 8 * device[0] + 4 * device[2] + device[3]
            dst = expert_of(zh, x, zl, y)
        else:
            src = expert_of(*device[:4])
            dst = mirrored + 8 * zh + 4 * zl + y
        rows = lambda n: pl.ds(pl.multiple_of(n * CAP, CAP), CAP)
        return self.send.at[rows(src)], self.recv.at[rows(dst)], device

    def start(self, first=0, last=32):
        if first == 0:
            src, dst, _ = self.ends(jnp.int32(0))
            pltpu.make_async_copy(src, dst, self.sems.at[1]).start()

        def one(k, carry):
            src, dst, device = self.ends(rem(9 * k, 32))
            remote(src, dst, self.sems.at[0], self.sems.at[1], device).start()
            return carry

        lax.fori_loop(max(first, 1), last, one, 0)

    def start_block(self, r):
        def one(q, carry):
            k = 16 * div(r, 2) + 8 * rem(r + self.me[0], 2) + rem(3 * q, 8)
            src, dst, device = self.ends(k)
            local = pltpu.make_async_copy(src, dst, self.sems.at[1])
            away = remote(src, dst, self.sems.at[0], self.sems.at[1], device)
            pl.when(k == 0)(local.start)
            pl.when(k != 0)(away.start)
            return carry

        lax.fori_loop(0, 8, one, 0)

    def wait_recv(self):
        await_bytes(self.recv, self.sems.at[1])

    def wait_send(self):
        await_bytes(self.send.at[pl.ds(0, 31 * CAP)], self.sems.at[0])

    def wait(self):
        self.wait_recv()
        self.wait_send()


def remote_params(n, mb=60):
    return pltpu.CompilerParams(
        vmem_limit_bytes=mb * 2**20, collective_id=n, has_side_effects=True
    )


VMEM = pl.BlockSpec(memory_space=pltpu.VMEM)
ANY = pl.BlockSpec(memory_space=pl.ANY)
DMA = pltpu.SemaphoreType.DMA


class Weights:
    def __init__(self, me, w_in, w_out, full_in, full_out, sems):
        self.me, self.refs, self.full, self.sems = me, (w_in, w_out), (full_in, full_out), sems

    def place(self, i, x, zh):
        at = pl.ds(pl.multiple_of(zh * 384, 128), 384)
        return self.full[0].at[x, :, at] if i == 0 else self.full[1].at[x, at, :]

    def first(self, i, b):
        zh, x, zl, y, c = self.me
        device = (jnp.int32(b), near(x, c), zl, y, zh)
        copy = remote(
            self.refs[i].at[b], self.place(i, x, zh), self.sems.at[0, i, b], self.sems.at[1, i, x], device
        )
        local = pltpu.make_async_copy(
            self.refs[i].at[b], self.place(i, x, zh), self.sems.at[1, i, x]
        )
        own = jnp.logical_and(
            jnp.logical_and(zh == b, div(x, 2) == c), zh == c
        )
        return copy, local, own

    def start(self, i):
        for b in range(2):
            copy, local, own = self.first(i, b)
            pl.when(own)(local.start)
            pl.when(jnp.logical_not(own))(copy.start)

    def forward(self, i, x, step):
        zh, me_x, zl, y, c = self.me
        piece = self.place(i, x, c)
        device = (zh, neighbour(me_x), zl, y, c) if step == 2 else (zh, me_x, zl, y, 1 - c)
        return remote(piece, piece, self.sems.at[2 * step - 2, i, x], self.sems.at[2 * step - 1, i, x], device)

    def sources(self, step):
        x = self.me[1]
        if step == 1:
            return x, 3 - x
        return neighbour(x), 3 - neighbour(x)

    def second(self, i):
        for x in self.sources(1):
            await_bytes(self.place(i, x, self.me[4]), self.sems.at[1, i, x])
            self.forward(i, x, 2).start()
            self.forward(i, x, 3).start()

    def third(self, i):
        for x in self.sources(2):
            self.forward(i, x, 2).wait_recv()
            self.forward(i, x, 3).start()

    def ready(self, i):
        for x in range(4):
            self.forward(i, jnp.int32(x), 3).wait_recv()

    def finish(self, i):
        for b in range(2):
            copy, _, own = self.first(i, b)
            pl.when(jnp.logical_not(own))(copy.wait_send)
        for x in self.sources(1):
            self.forward(i, x, 2).wait_send()
        for x in range(4):
            self.forward(i, jnp.int32(x), 3).wait_send()


STEP = 256
CHUNKS = 4
TILES = SLOTS // STEP


def row_block(r):
    return pl.ds(pl.multiple_of(r * STEP, STEP), STEP)


def half_rows(n):
    return pl.ds(pl.multiple_of(n * 384, 128), 384)


def front_body(tok_ref, cot_ref, gain1_ref, w_qkv_ref, w_o_ref, gain2_ref, gate_ref, routes_ref, w_in_ref, w_out_ref,
               qkv_ref, ret_ref, y_ref, mid_ref, att_ref, gates_ref, ot_ref, lse_ref, dwin_ref, total_ref,
               qkv_send, o_send, o_recv, x_send, c_send, x_ref, c_ref, vt_ref, full_in, full_out, g_ref, d_ref,
               dwout_ref, out_in, out_out, got_in, got_out, got2,
               head_sems, row_sems, weight_sems, load_sems, core_sems, pair_sems):
    loads = [
        pltpu.make_async_copy(w_qkv_ref.at[:, p * D : p * D + D], g_ref.at[p, 0:D], load_sems.at[p]) for p in range(3)
    ] + [pltpu.make_async_copy(w_o_ref, g_ref.at[3, 0:D], load_sems.at[3])]
    for load in loads:
        load.start()
    me = greet_all((chip_partner, 16), (row_partner, 32))
    zh, x, zl, y, c = me
    weights = Weights(me, w_in_ref, w_out_ref, full_in, full_out, weight_sems)
    heads = HeadSwap(me, qkv_send, qkv_ref, head_sems.at[0])
    heads_back = HeadSwap(me, o_send, o_recv, head_sems.at[1])
    rows_c = RowSwap(me, c_send, c_ref, row_sems.at[0])
    rows_x = RowSwap(me, x_send, x_ref, row_sems.at[1])
    rows_ret = RowSwap(me, x_send, ret_ref, row_sems.at[2], back=True)
    rows_y = RowSwap(me, c_send, y_ref, row_sems.at[3], back=True)
    weights.start(0)

    def part_weights(p):
        loads[p].wait()
        return g_ref[p, 0:D, :]

    project(tok_ref, gain1_ref, part_weights, qkv_send)
    heads.start()
    deal_body(cot_ref, routes_ref, c_send)
    heads.arrived(0)
    heads.arrived(1)
    weights.start(1)
    weights.second(0)
    attend_forward(
        rem(x, 2), qkv_ref, o_send, ot_ref, lse_ref, vt_ref,
        lambda b: heads.arrived(b) if b > 1 else None, heads_back.leave,
    )
    for t in range(BLOCKS):
        heads_back.arrived(t)
    loads[3].wait()
    middle_body(o_recv, tok_ref, g_ref[3, 0:D, :], gain2_ref, gate_ref, routes_ref, mid_ref, att_ref, x_send, gates_ref)
    rows_x.start()
    rows_c.start()
    weights.second(1)
    weights.third(0)
    weights.ready(0)
    rows_x.wait()

    def hidden(j):
        tiles = [slice(r * STEP, r * STEP + STEP) for r in range(TILES)]
        w = full_in[j]

        def after(at, h):
            g, d = gelu_parts(h)
            g_ref[j, at, :] = g.astype(BF16)
            d_ref[j, at, :] = d.astype(BF16)

        before = dot(x_ref[tiles[0], 0:D], w)
        for r in range(1, TILES):
            h = dot(x_ref[tiles[r], 0:D], w)
            after(tiles[r - 1], before)
            before = h
        after(tiles[-1], before)

    def hidden_loop(j, carry):
        hidden(j)
        return carry

    lax.fori_loop(0, CHUNKS - 1, hidden_loop, 0)
    weights.third(1)
    hidden(CHUNKS - 1)
    weights.ready(1)
    rows_c.wait()

    def produce(n, carry):
        r = rem(n + 2, TILES)
        at = row_block(r)
        c_ref[at, :] = (c_ref[at, :].astype(F32) * from_parts(x_ref[at, D:])).astype(BF16)
        out = dot(g_ref[0, at, :], full_out[0])
        for j in range(1, CHUNKS):
            out = out + dot(g_ref[j, at, :], full_out[j])
        c_send[at, :] = out.astype(BF16)
        rows_y.start_block(r)
        return carry

    lax.fori_loop(0, TILES, produce, 0)

    sibling = core_partner(me, 1)

    def over(i, j):
        pair = (out_in, got_in) if i == 0 else (out_out, got_out)
        return remote(pair[0].at[j], pair[1].at[j], core_sems.at[0, i, j], core_sems.at[1, i, j], sibling)

    def second_grad(j, carry):
        part = dot(g_ref[j], c_ref[...], 0, 0)
        out_out[j] = jnp.where(c == 0, part[384:], part[:384]).astype(BF16)
        over(1, j).start()
        dwout_ref[j] = jnp.where(c == 0, part[:384], part[384:]).astype(BF16)
        return carry

    lax.fori_loop(0, CHUNKS, second_grad, 0)

    def second_sum(j, carry):
        over(1, j).wait()
        dwout_ref[j] = (dwout_ref[j].astype(F32) + got_out[j].astype(F32)).astype(BF16)
        return carry

    lax.fori_loop(0, CHUNKS, second_sum, 0)
    pass_on, keep = (neighbour(x), 3 - neighbour(x)), (x, 3 - x)

    def second_over(j):
        return remote(dwout_ref.at[pass_on[j]], got2.at[j], pair_sems.at[0, j], pair_sems.at[1, j], (zh, neighbour(x), zl, y, c))

    for j in range(2):
        second_over(j).start()

    def back(n, carry):
        r = rem(n + 2, TILES)
        at = row_block(r)
        total = jnp.zeros((STEP, 128), F32)
        dx = jnp.zeros((STEP, D), F32)
        for j in range(CHUNKS):
            cw = dot(c_ref[at, :], full_out[j], 1, 1)
            dh = (d_ref[j, at, :].astype(F32) * cw).astype(BF16)
            prod = g_ref[j, at, :].astype(F32) * cw
            for t in range(D // 128):
                total = total + prod[:, 128 * t : 128 * t + 128]
            d_ref[j, at, :] = dh
            dx = dx + dot(dh, full_in[j], 1, 1)
        x_send[at, 0:D] = dx.astype(BF16)
        x_send[at, D:] = two_parts(jnp.sum(total, axis=1, keepdims=True))
        rows_ret.start_block(r)
        return carry

    lax.fori_loop(0, TILES, back, 0)

    def first_grad(j, carry):
        part = dot(x_ref[:, 0:D], d_ref[j], 0, 0)
        out_in[j] = jnp.where(c == 0, part[:, 384:], part[:, :384]).astype(BF16)
        over(0, j).start()
        dwin_ref[j] = jnp.where(c == 0, part[:, :384], part[:, 384:]).astype(BF16)
        return carry

    lax.fori_loop(0, CHUNKS, first_grad, 0)

    def first_sum(j, carry):
        over(0, j).wait()
        dwin_ref[j] = (dwin_ref[j].astype(F32) + got_in[j].astype(F32)).astype(BF16)
        return carry

    lax.fori_loop(0, CHUNKS, first_sum, 0)
    heads.wait_send()
    heads_back.wait_send()
    weights.finish(0)
    weights.finish(1)
    rows_y.wait()
    for j in range(2):
        second_over(j).wait()
        total_ref[j] = (dwout_ref[keep[j]].astype(F32) + got2[j].astype(F32)).astype(BF16)
    rows_ret.wait()


def front(tok, cot, gain1, w_qkv, w_o, gain2, gate, routes, w_in, w_out):
    buf = lambda *s: pltpu.VMEM(s, BF16)
    outs = [
        ((BLOCKS, ROWS, 384), BF16),
        ((SLOTS, D + EXTRA), BF16),
        ((SLOTS, D), BF16),
        ((ROWS, D), F32),
        ((ROWS, D), BF16),
        ((ROWS, 128), F32),
        ((12, 64, ROWS), F32),
        ((12, 8, ROWS), F32),
        ((CHUNKS, D, 384), BF16),
        ((2, 384, D), BF16),
    ]
    return pl.pallas_call(
        front_body,
        out_shape=[jax.ShapeDtypeStruct(s, t) for s, t in outs],
        in_specs=[VMEM] * 3 + [ANY] * 2 + [VMEM] * 3 + [ANY] * 2,
        out_specs=[VMEM] * len(outs),
        scratch_shapes=[
            buf(BLOCKS, ROWS, 384),
            buf(BLOCKS, ROWS, 128),
            buf(BLOCKS, ROWS, 128),
            buf(SLOTS, D + EXTRA),
            buf(SLOTS, D),
            buf(SLOTS, D + EXTRA),
            buf(SLOTS, D),
            buf(128, BLOCKS * ROWS),
            buf(CHUNKS, D, D),
            buf(CHUNKS, D, D),
            buf(CHUNKS, SLOTS, D),
            buf(CHUNKS, SLOTS, D),
            buf(CHUNKS, 384, D),
            buf(CHUNKS, D, 384),
            buf(CHUNKS, 384, D),
            buf(CHUNKS, D, 384),
            buf(CHUNKS, 384, D),
            buf(2, 384, D),
            DMA((2, 2, 8)),
            DMA((4, 2)),
            DMA((6, 2, 4)),
            DMA((4,)),
            DMA((2, 2, 4)),
            DMA((2, 2)),
        ],
        compiler_params=remote_params(0, 63),
    )(tok, cot, gain1, w_qkv, w_o, gain2, gate, routes, w_in, w_out)


def back_body(ret_ref, cot_ref, routes_ref, gates_ref, mid_ref, gain_ref, gate_w_ref, w_o_ref,
              send_ref, dmid_ref, gate_grad_ref, gain_grad_ref):
    m1, m2, c1, c2 = choices(routes_ref[...])
    s1, s2 = chosen(c1), chosen(c2)
    g1, g2 = gates_ref[:, 0:1], gates_ref[:, 1:2]
    extra = ret_ref[:, D:]
    d1, d2 = from_parts(dot(s1, extra)), from_parts(dot(s2, extra))
    dl = g2 * d1 - g1 * d2
    dlogits = (m1 - m2) * dl
    unit, inv = norm(mid_ref[...])
    high = dlogits.astype(BF16)
    low = (dlogits - high.astype(F32)).astype(BF16)
    gate_w = gate_w_ref[...]
    da2 = dot(s1 + s2, ret_ref[:, 0:D]) + dot(high, gate_w, 1, 1) + dot(low, gate_w, 1, 1)
    dmid = cot_ref[...].astype(F32) + norm_back(da2, gain_ref[...], unit, inv)
    dmid_ref[...] = dmid
    do = dot(dmid.astype(BF16), w_o_ref[...], 1, 1)
    for s in range(BLOCKS):
        send_ref[s] = pair_up(do, s).astype(BF16)

    def later():
        a2 = (unit * gain_ref[...]).astype(BF16)
        gate_grad_ref[...] = dot(high, a2, 0, 0) + dot(low, a2, 0, 0)
        gain_grad_ref[...] = jnp.sum(da2 * unit, axis=0, keepdims=True)

    return later


def axis_place(me, a):
    zh, x, zl, y, c = me
    return (x, y, 2 * zh + zl)[a]


def axis_peer(me, a, k):
    zh, x, zl, y, c = me
    p = rem(axis_place(me, a) + k, 4)
    if a == 0:
        return p, (zh, p, zl, y, c)
    if a == 1:
        return p, (zh, x, zl, p, c)
    return p, (div(p, 2), x, rem(p, 2), y, c)


def axis_partner(me, k):
    zh, x, zl, y, c = me
    along_z = div(k, 4)
    dz = rem(k + 1, 4) * along_z
    z = rem(2 * zh + zl + dz, 4)
    return div(z, 2), x, rem(z, 2), rem(y + k * (1 - along_z), 4), c


def multiple(n, w):
    return pl.ds(pl.multiple_of(n * w, w), w)


PEERS = (1, 2, 3)


class GroupSum:
    def __init__(self, me, g, axes, out, bufs, sems):
        self.me, self.g, self.axes, self.out, self.sems = me, g, axes, out, sems.at[g]
        self.s0, self.r0, self.a0, self.r1, self.a1, self.s2, self.r2, self.r3 = [b.at[g] for b in bufs]
        self.place = [axis_place(me, a) for a in axes]
        self.c = me[4]

    def copy(self, stage, k, src, dst):
        if stage in (0, 6):
            device = core_partner(self.me, 1)
        else:
            device = axis_peer(self.me, self.axes[(0, 0, 1, 2, 1, 0)[stage]], jnp.int32(k))[1]
        return remote(src, dst, self.sems.at[stage, 0, k], self.sems.at[stage, 1, k], device)

    def peer(self, t, k):
        return axis_peer(self.me, self.axes[t], jnp.int32(k))[0]

    def swap(self):
        return self.copy(0, 0, self.s0, self.r0)

    def scatter1(self, k):
        return self.copy(1, k, self.s0.at[multiple(self.peer(0, k), 192)], self.r1.at[k - 1])

    def scatter2(self, k):
        return self.copy(2, k, self.s2.at[multiple(self.peer(1, k), 48)], self.r2.at[k - 1])

    def share(self, k):
        mine = self.r3.at[self.place[2]]
        return self.copy(3, k, mine, mine)

    def block(self, rows):
        base = self.g * D + self.c * 384
        lanes = pl.ds(pl.multiple_of(base, 128), 384)
        i, j = self.place[0], self.place[1]
        if rows == 48:
            return self.out.at[multiple(4 * i + j, 48), lanes]
        if rows == 192:
            return self.out.at[multiple(i, 192), lanes]
        return self.out.at[:, lanes]

    def gather(self, stage, k):
        ref = self.block((48, 192, 768)[stage - 4])
        return self.copy(stage, k, ref, ref)

    def begin(self, grad):
        self.s0[...] = grad(1 - self.c).astype(BF16)
        self.swap().start()
        self.a0[...] = grad(self.c)

    def step1(self):
        self.swap().wait()
        self.a0[...] += self.r0[...].astype(F32)
        self.s0[...] = self.a0[...].astype(BF16)
        for k in PEERS:
            self.scatter1(k).start()

    def step2(self):
        for k in PEERS:
            self.scatter1(k).wait_recv()
        mine = self.a0[multiple(self.place[0], 192), :]
        for k in PEERS:
            mine = mine + self.r1[k - 1].astype(F32)
        self.a1[...] = mine
        self.s2[...] = mine.astype(BF16)
        for k in PEERS:
            self.scatter2(k).start()

    def step3(self):
        for k in PEERS:
            self.scatter2(k).wait_recv()
        mine = self.a1[multiple(self.place[1], 48), :]
        for k in PEERS:
            mine = mine + self.r2[k - 1].astype(F32)
        self.r3[self.place[2]] = mine.astype(BF16)
        for k in PEERS:
            self.share(k).start()

    def step4(self):
        for k in PEERS:
            p = axis_peer(self.me, self.axes[2], jnp.int32(k))[0]
            self.copy(3, 4 - k, self.r3.at[p], self.r3.at[p]).wait_recv()
        total = (self.r3[0].astype(F32) + self.r3[1].astype(F32)) + (
            self.r3[2].astype(F32) + self.r3[3].astype(F32)
        )
        self.block(48)[...] = total.astype(BF16)
        for k in PEERS:
            self.gather(4, k).start()

    def step5(self):
        for k in PEERS:
            self.gather(4, k).wait_recv()
        for k in PEERS:
            self.gather(5, k).start()

    def step6(self):
        for k in PEERS:
            self.gather(5, k).wait_recv()
        self.gather(6, 0).start()

    def finish(self):
        self.gather(6, 0).wait()
        for k in PEERS:
            self.scatter1(k).wait_send()
            self.scatter2(k).wait_send()
            self.share(k).wait_send()
            self.gather(4, k).wait_send()
            self.gather(5, k).wait_send()


class SmallSum:
    def __init__(self, me, mine, slots, sems):
        self.me, self.mine, self.slots, self.sems = me, mine, slots, sems

    def swap(self):
        return remote(self.mine.at[0], self.slots.at[0], self.sems.at[0, 0], self.sems.at[1, 0], core_partner(self.me, 1))

    def share(self, a, k):
        n = 3 * a + k
        return remote(self.mine.at[a + 1], self.slots.at[1 + 4 * a + axis_place(self.me, a)], self.sems.at[0, n],
                      self.sems.at[1, n], axis_peer(self.me, a, jnp.int32(k))[1])

    def begin(self):
        self.swap().start()

    def step(self, a):
        if a == 0:
            self.swap().wait_recv()
            total = self.mine[0] + self.slots[0]
        else:
            total = self.total(a - 1)
        if a < 3:
            self.mine[a + 1] = total
            for k in PEERS:
                self.share(a, k).start()
        return total

    def total(self, a):
        for k in PEERS:
            self.share(a, k).wait_recv()
        s, n = self.slots, 1 + 4 * a
        s[n + axis_place(self.me, a)] = self.mine[a + 1]
        return (s[n] + s[n + 1]) + (s[n + 2] + s[n + 3])

    def finish(self):
        self.swap().wait_send()
        for a in range(3):
            for k in PEERS:
                self.share(a, k).wait_send()


class Collect:
    def __init__(self, me, dw, got, total, fin, sems):
        self.me, self.dw, self.got, self.fin, self.sems = me, dw, got, fin, sems
        x = me[1]
        self.totals = (got, total)
        self.keep, self.pass_on = (x, 3 - x), (neighbour(x), 3 - neighbour(x))

    def second(self, j, at=slice(None)):
        zh, x, zl, y, c = self.me
        return remote(self.dw.at[self.pass_on[j], at], self.got.at[j, at], self.sems.at[0, 0, j], self.sems.at[1, 0, j],
                      (zh, neighbour(x), zl, y, c))

    def quarters(self, j):
        return [self.second(j, slice(192 * q, 192 * q + 192)) for q in range(4)]

    def third(self, i, j):
        zh, x, zl, y, c = self.me
        pair = div(x, 2)
        src = self.totals[i].at[j]
        copy = remote(src, self.fin[i].at[zh], self.sems.at[2, i, j], self.sems.at[3, i, zh], (c, self.keep[j], zl, y, pair))
        local = pltpu.make_async_copy(src, self.fin[i].at[zh], self.sems.at[3, i, zh])
        if j == 1:
            return copy, None, None
        return copy, local, jnp.logical_and(zh == c, pair == c)

    def add(self, j):
        self.second(j).wait_recv()
        self.got[j] = (self.dw[self.keep[j]].astype(F32) + self.got[j].astype(F32)).astype(BF16)

    def send(self, i, j):
        copy, local, own = self.third(i, j)
        if j == 1:
            copy.start()
        else:
            pl.when(own)(local.start)
            pl.when(jnp.logical_not(own))(copy.start)

    def finish(self):
        for j in range(2):
            self.second(j).wait_send()
        for i in range(2):
            for j in range(2):
                copy, _, own = self.third(i, j)
                if j == 1:
                    copy.wait_send()
                else:
                    pl.when(jnp.logical_not(own))(copy.wait_send)
            for b in range(2):
                await_bytes(self.fin[i].at[b], self.sems.at[3, i, b])


def rear_body(ret_ref, cot_ref, routes_ref, gates_ref, mid_ref, att_ref, gain2_ref, gate_w_ref, w_o_ref,
              qkv_ref, ot_ref, lse_ref, tok_ref, gain1_ref, w_qkv_ref, y_ref, dw_ref, total_ref,
              tok_grad_ref, grads_ref, early_ref, late_ref, out_ref, fin_in, fin_out,
              dmid_ref, do_send, do_recv, dqkv_send, dqkv_recv, kt_ref, dk_ref, dv_ref, d_ref, datt_ref, got,
              s0, r0, a0, r1, a1, s2, r2, r3, early, early_slots, late, late_slots,
              head_sems, collect_sems, group_sems, small_sems):
    me = greet_all((chip_partner, 16), (axis_partner, 7))
    heads = HeadSwap(me, do_send, do_recv, head_sems.at[0])
    heads_back = HeadSwap(me, dqkv_send, dqkv_recv, head_sems.at[1])
    collect = Collect(me, dw_ref, got, total_ref, (fin_in, fin_out), collect_sems)
    bufs = (s0, r0, a0, r1, a1, s2, r2, r3)
    orders = ((0, 1, 2), (1, 2, 0), (2, 0, 1), (1, 0, 2))
    groups = [GroupSum(me, g, orders[g], grads_ref, bufs, group_sems) for g in range(4)]
    qkv_groups, o_group = groups[:3], groups[3]
    small = SmallSum(me, early, early_slots, small_sems.at[0])
    small_late = SmallSum(me, late, late_slots, small_sems.at[1])
    early[...] = jnp.zeros_like(early)
    late[...] = jnp.zeros_like(late)

    parts = [copy.start for j in range(2) for copy in collect.quarters(j)]

    def pump(n):
        for _ in range(min(n, len(parts))):
            parts.pop(0)()

    pump(2)
    later = back_body(ret_ref, cot_ref, routes_ref, gates_ref, mid_ref, gain2_ref, gate_w_ref, w_o_ref,
                      do_send, dmid_ref, early.at[0, 0:32], early.at[0, 32:33])
    heads.start()
    later()
    small.begin()
    datt_ref[...] = dmid_ref[...].astype(BF16)
    o_group.begin(lambda n: dot(att_ref[...], datt_ref[:, pl.ds(pl.multiple_of(n * 384, 128), 384)], 0, 0))
    for t in range(BLOCKS):
        heads.arrived(t)
    pump(2)
    collect.send(1, 0)

    def beside(pair):
        if pair == 3:
            o_group.step1()
            small.step(0)
        pump(2)

    attend_backward(rem(me[1], 2), qkv_ref, do_recv, ot_ref, lse_ref, dqkv_send, kt_ref, dk_ref, dv_ref,
                    lambda b: None, heads_back.leave, beside)
    pump(4)
    collect.send(1, 1)
    _, _, c1, c2 = choices(routes_ref[...])
    rows = y_ref[...]
    mix = gates_ref[:, 0:1] * dot(chosen(c1), rows) + gates_ref[:, 1:2] * dot(chosen(c2), rows)
    out_ref[...] = (mid_ref[...] + mix).astype(BF16)
    o_group.step2()
    small.step(1)
    unit, inv = norm(tok_ref[...].astype(F32))
    a1_rows = (unit * gain1_ref[...]).astype(BF16)
    for t in range(BLOCKS):
        heads_back.arrived(t)
    for part in range(3):
        tiles = unpair(
            [dqkv_recv[s, :, part * 128 : part * 128 + 128].astype(F32) for s in range(BLOCKS)]
        )
        for t in range(6):
            d_ref[part, :, 128 * t : 128 * t + 128] = tiles[t].astype(BF16)
        qkv_groups[part].begin(
            lambda n: dot(a1_rows, d_ref[part, :, pl.ds(pl.multiple_of(n * 384, 128), 384)], 0, 0)
        )
    da1 = dot(d_ref[0], w_qkv_ref[:, 0:D], 1, 1)
    for part in (1, 2):
        da1 = da1 + dot(d_ref[part], w_qkv_ref[:, part * D : part * D + D], 1, 1)
    late[0, 0:1] = jnp.sum(da1 * unit, axis=0, keepdims=True)
    small_late.begin()
    for g in qkv_groups:
        g.step1()
    pump(16)
    o_group.step3()
    small.step(2)
    tok_grad_ref[...] = dmid_ref[...] + norm_back(da1, gain1_ref[...], unit, inv)
    small_late.step(0)
    for j in range(2):
        collect.add(j)
        collect.send(0, j)
    for g in qkv_groups:
        g.step2()
    o_group.step4()
    early_ref[...] = small.step(3)
    small_late.step(1)
    for g in qkv_groups:
        g.step3()
    o_group.step5()
    small_late.step(2)
    for g in qkv_groups:
        g.step4()
    late_ref[...] = small_late.step(3)
    o_group.step6()
    for g in qkv_groups:
        g.step5()
    for g in qkv_groups:
        g.step6()
    small.finish()
    small_late.finish()
    heads.wait_send()
    heads_back.wait_send()
    collect.finish()
    for g in groups:
        g.finish()


def rear(*args):
    buf = lambda *s: pltpu.VMEM(s, BF16)
    f32 = lambda *s: pltpu.VMEM(s, F32)
    return pl.pallas_call(
        rear_body,
        out_shape=[
            jax.ShapeDtypeStruct((ROWS, D), F32),
            jax.ShapeDtypeStruct((D, 4 * D), BF16),
            jax.ShapeDtypeStruct((40, D), F32),
            jax.ShapeDtypeStruct((8, D), F32),
            jax.ShapeDtypeStruct((ROWS, D), BF16),
            jax.ShapeDtypeStruct((2, D, 384), BF16),
            jax.ShapeDtypeStruct((2, 384, D), BF16),
        ],
        in_specs=[VMEM] * len(args),
        out_specs=[VMEM] * 7,
        scratch_shapes=[
            f32(ROWS, D),
            buf(BLOCKS, ROWS, 128),
            buf(BLOCKS, ROWS, 128),
            buf(BLOCKS, ROWS, 384),
            buf(BLOCKS, ROWS, 384),
            buf(128, BLOCKS * ROWS),
            f32(BLOCKS * ROWS, 128),
            f32(BLOCKS * ROWS, 128),
            buf(3, ROWS, D),
            buf(ROWS, D),
            buf(2, D, 384),
            buf(4, D, 384),
            buf(4, D, 384),
            f32(4, D, 384),
            buf(4, 3, 192, 384),
            f32(4, 192, 384),
            buf(4, 192, 384),
            buf(4, 3, 48, 384),
            buf(4, 4, 48, 384),
            f32(4, 40, D),
            f32(13, 40, D),
            f32(4, 8, D),
            f32(13, 8, D),
            DMA((2, 2, 8)),
            DMA((4, 2, 2)),
            DMA((4, 7, 2, 4)),
            DMA((2, 2, 10)),
        ],
        compiler_params=remote_params(2),
    )(*args)


def on_device(tokens, cotangent, gain_first, w_qkv, w_o, gain_second, w_gate, w_in, w_out, routes, frozen):
    e = (lax.axis_index("zl") * 4 + lax.axis_index("y")) * 2 + lax.axis_index("c")
    tok, cot, routes = tokens[0], cotangent[0], routes[0]
    gain1, gain2 = gain_first.reshape(1, D), gain_second.reshape(1, D)
    qkv, ret, y, mid, att, gates, ot, lse, dw_in, total_out = front(
        tok, cot, gain1, w_qkv, w_o, gain2, w_gate, routes, w_in, w_out
    )
    keep = (1 - lax.dynamic_slice_in_dim(frozen, 2 * e, 2)).astype(F32)
    tok_grad, grads, early, late, out, w_in_grad, w_out_grad = rear(
        ret, cot, routes, gates, mid, att, gain2, w_gate, w_o, qkv, ot, lse, tok, gain1, w_qkv, y, dw_in, total_out
    )
    return (
        out[None],
        tok_grad[None],
        late[0],
        grads[:, : 3 * D].astype(F32),
        grads[:, 3 * D :].astype(F32),
        early[32],
        early[:32].T * (1 - frozen).astype(F32)[None, :],
        w_in_grad.astype(F32) * keep[:, None, None],
        w_out_grad.astype(F32) * keep[:, None, None],
    )


def solution(mesh):
    fine = Mesh(mesh.devices.reshape(2, 4, 2, 4, 2), ALL)
    seq, exp = ("zh", "x"), ("zl", "y", "c")
    rows, rest = P(exp, seq, None), P()
    in_specs = (rows, rows, rest, rest, rest, rest, rest, P(exp, None, seq), rows, rows, rest)
    out_specs = (rows, rows, rest, rest, rest, rest, rest, P(exp, None, seq), rows)
    return jax.shard_map(on_device, mesh=fine, in_specs=in_specs, out_specs=out_specs, check_vma=False)
```

```python
import functools
import math

import jax
import jax.numpy as jnp
from jax import lax
from jax.experimental import pallas as pl
from jax.experimental.pallas import tpu as pltpu
from jax.sharding import Mesh
from jax.sharding import PartitionSpec as P

D = 768
HEADS = 12
HEAD_DIM = 64
EXPERTS = 32
CAP = 32
ROWS = 256
BLOCKS = 8
FF = 3072
SLOTS = EXPERTS * CAP
EXTRA = 128
EPS = 1e-5
SCALE = HEAD_DIM ** -0.5
LOG2E = math.log2(math.e)
BF16 = jnp.bfloat16
F32 = jnp.float32
NEG = -1e30

SEQ = ("zh", "x")
MESH = pl.DeviceIdType.MESH
ALL = ("zh", "x", "zl", "y", "c")


def dot(a, b, ca=1, cb=0):
    return lax.dot_general(a, b, (((ca,), (cb,)), ((), ())), preferred_element_type=F32)


def params(mb=56):
    return pltpu.CompilerParams(vmem_limit_bytes=mb * 2**20)


def vspec(n):
    return [pl.BlockSpec(memory_space=pltpu.VMEM)] * n


def call(body, outs, n_in, scratch=(), **kw):
    return pl.pallas_call(
        body,
        out_shape=[jax.ShapeDtypeStruct(s, t) for s, t in outs],
        in_specs=vspec(n_in),
        out_specs=vspec(len(outs)),
        scratch_shapes=list(scratch),
        compiler_params=params(),
        **kw,
    )


def norm(v):
    mean = jnp.mean(v, axis=-1, keepdims=True)
    centred = v - mean
    inv = lax.rsqrt(jnp.mean(centred * centred, axis=-1, keepdims=True) + EPS)
    return centred * inv, inv


def row_of(gain_ref):
    return gain_ref[...].reshape(1, D)


def norm_back(grad, gain, unit, inv):
    t = grad * gain
    m1 = jnp.mean(t, axis=-1, keepdims=True)
    m2 = jnp.mean(t * unit, axis=-1, keepdims=True)
    return inv * (t - m1 - unit * m2)


def lane_low():
    return lax.broadcasted_iota(jnp.int32, (1, 128), 1) < 64


def pair_up(wide, s):
    low = wide[:, 128 * (s // 2) : 128 * (s // 2) + 128]
    if s % 2:
        low = pltpu.roll(low, 64, 1)
    high = wide[:, 512 + 128 * (s // 4) : 640 + 128 * (s // 4)]
    if (s // 2) % 2 == 0:
        high = pltpu.roll(high, 64, 1)
    return jnp.where(lane_low(), low, high)


def unpair(tiles):
    out = []
    for t in range(4):
        out.append(
            jnp.where(lane_low(), tiles[2 * t], pltpu.roll(tiles[2 * t + 1], 64, 1))
        )
    for t in range(2):
        a = tiles[4 * t] + tiles[4 * t + 1]
        b = tiles[4 * t + 2] + tiles[4 * t + 3]
        out.append(jnp.where(lane_low(), pltpu.roll(a, 64, 1), b))
    return out


def project(tok_ref, gain_ref, part_weights, send_ref):
    unit, _ = norm(tok_ref[...].astype(F32))
    a1 = (unit * row_of(gain_ref)).astype(BF16)
    for part in range(3):
        wide = dot(a1, part_weights(part))
        for s in range(BLOCKS):
            send_ref[s, :, part * 128 : part * 128 + 128] = pair_up(wide, s).astype(
                BF16
            )


def unit_of(half, h, i):
    if h == 0:
        return 0, i, i + 1, i, i
    a, b = ((0, 1), (3, 2), (4, 5), (7, 6))[i]
    return 1, a + half * (b - a), 2 * i + 2, 2 * i, BLOCKS + i


def masked_scores(k, q, block, first, count):
    s = dot(k, q, 1, 1)
    start = first * ROWS
    tail = (count - first) * ROWS
    keys = lax.broadcasted_iota(jnp.int32, (tail, ROWS), 0) + start
    queries = lax.broadcasted_iota(jnp.int32, (tail, ROWS), 1) + block * ROWS
    end = jnp.where(keys <= queries, s[start:], NEG)
    return end if start == 0 else jnp.concatenate([s[:start], end], axis=0)


def head_mask(h):
    low = lane_low()
    return (low if h == 0 else jnp.logical_not(low)).astype(F32).astype(BF16)


def padded(h, t):
    zero = jnp.zeros_like(t)
    return jnp.concatenate([t, zero] if h == 0 else [zero, t], axis=0).T


def attend_forward(half, qkv_ref, o_ref, ot_ref, lse_ref, vt_ref, arrived, leave):
    c = SCALE * LOG2E
    for pair in range(BLOCKS // 2):
        for b in (2 * pair, 2 * pair + 1):
            arrived(b)
            vt_ref[:, b * ROWS : (b + 1) * ROWS] = qkv_ref[b, :, 256:384].T
            o_ref[b] = jnp.zeros((ROWS, 128), BF16)
        for unit in ((1, pair), (0, 2 * pair), (0, 2 * pair + 1)):
            h, block, count, first, u = unit_of(half, *unit)
            q = qkv_ref[block, :, 0:128] * head_mask(h)
            k = qkv_ref[0:count, :, 128:256].reshape(count * ROWS, 128)
            s = masked_scores(k, q, block, first, count)
            top = jnp.max(s, axis=0, keepdims=True)
            p = jnp.exp2((s - top) * c)
            total = jnp.sum(p, axis=0, keepdims=True)
            ot = dot(vt_ref[64 * h : 64 * h + 64, 0 : count * ROWS], p.astype(BF16))
            ot = ot / total
            ot_ref[u] = ot
            lse_ref[u] = jnp.broadcast_to(top * c + jnp.log2(total), (8, ROWS))
            o_ref[block] = (o_ref[block].astype(F32) + padded(h, ot)).astype(BF16)
        if pair % 2:
            leave(pair // 2)


def attend_backward(half, qkv_ref, do_ref, ot_ref, lse_ref, out_ref, kt_ref, dk_ref, dv_ref, arrived, leave, beside):
    c = SCALE * LOG2E
    for b in range(BLOCKS):
        kt_ref[:, b * ROWS : (b + 1) * ROWS] = qkv_ref[b, :, 128:256].T
        out_ref[b, :, 0:128] = jnp.zeros((ROWS, 128), BF16)
    dk_ref[...] = jnp.zeros_like(dk_ref)
    dv_ref[...] = jnp.zeros_like(dv_ref)

    def one(h, i):
        h, block, count, first, u = unit_of(half, h, i)
        rows = count * ROWS
        q = qkv_ref[block, :, 0:128] * head_mask(h)
        do = do_ref[block] * head_mask(h)
        dot_rows = do.astype(F32).T[64 * h : 64 * h + 64]
        delta = jnp.sum(dot_rows * ot_ref[u], axis=0, keepdims=True)
        lse = lse_ref[u][0:1]
        k = qkv_ref[0:count, :, 128:256].reshape(rows, 128)
        v = qkv_ref[0:count, :, 256:384].reshape(rows, 128)
        s = masked_scores(k, q, block, first, count)
        p = jnp.exp2(s * c - lse)
        dp = dot(v, do, 1, 1)
        ds = (p * (dp - delta)).astype(BF16)
        dv_ref[0:rows] += dot(p.astype(BF16), do)
        dk_ref[0:rows] += dot(ds, q)
        dqt = dot(kt_ref[64 * h : 64 * h + 64, 0:rows], ds) * SCALE
        out_ref[block, :, 0:128] = (
            out_ref[block, :, 0:128].astype(F32) + padded(h, dqt)
        ).astype(BF16)

    for pair in reversed(range(BLOCKS // 2)):
        b = 2 * pair + 1
        arrived(b)
        arrived(b - 1)
        one(1, pair)
        for b in (b, b - 1):
            one(0, b)
            at = slice(b * ROWS, (b + 1) * ROWS)
            out_ref[b, :, 128:256] = (dk_ref[at] * SCALE).astype(BF16)
            out_ref[b, :, 256:384] = dv_ref[at].astype(BF16)
        beside(pair)
        if pair % 2 == 0:
            leave(pair // 2)


def choices(routes):
    ids = lax.broadcasted_iota(jnp.int32, (ROWS, EXPERTS), 1).astype(F32)
    e1, e2 = [jnp.broadcast_to(routes[k : k + 1].astype(F32), (8, ROWS)).T[:, 0:1] for k in range(2)]
    m1, m2 = (e1 == ids).astype(F32), (e2 == ids).astype(F32)
    r = lax.broadcasted_iota(jnp.int32, (ROWS, ROWS), 0)
    k = lax.broadcasted_iota(jnp.int32, (ROWS, ROWS), 1)
    lower = (k < r).astype(F32).astype(BF16)
    earlier = dot(lower, (m1 + m2).astype(BF16))
    s1 = jnp.sum(earlier * m1, axis=1, keepdims=True)
    s2 = jnp.sum(earlier * m2, axis=1, keepdims=True)

    return m1, m2, e1 * CAP + s1, e2 * CAP + s2


def chosen(col):
    at = lax.broadcasted_iota(jnp.int32, (ROWS, SLOTS), 1).astype(F32)
    return (at == col).astype(F32).astype(BF16)


def chosen_t(col):
    row = jnp.broadcast_to(col, (ROWS, 128)).T[0:1]
    at = lax.broadcasted_iota(jnp.int32, (SLOTS, ROWS), 0).astype(F32)
    return (at == row).astype(F32).astype(BF16)


def two_parts(v):
    lane = lax.broadcasted_iota(jnp.int32, (v.shape[0], EXTRA), 1)
    high = v.astype(BF16).astype(F32)
    return jnp.where(lane == 0, high, jnp.where(lane == 1, v - high, 0.0)).astype(BF16)


def from_parts(v):
    lane = lax.broadcasted_iota(jnp.int32, v.shape, 1)
    return jnp.sum(jnp.where(lane < 2, v.astype(F32), 0.0), axis=1, keepdims=True)


def deal_body(cot_ref, routes_ref, send_ref):
    _, _, c1, c2 = choices(routes_ref[...])
    either = chosen_t(c1) + chosen_t(c2)
    send_ref[...] = dot(either, cot_ref[...]).astype(BF16)


def middle_body(o_ref, tok_ref, w_o, gain_ref, gate_ref, routes_ref, mid_ref, att_ref, send_ref, gates_ref):
    tiles = unpair([o_ref[s].astype(F32) for s in range(BLOCKS)])
    o = jnp.concatenate([t.astype(BF16) for t in tiles], axis=1)
    att_ref[...] = o
    mid = tok_ref[...].astype(F32) + dot(o, w_o)
    mid_ref[...] = mid
    unit, _ = norm(mid)
    a2 = (unit * row_of(gain_ref)).astype(BF16)
    logits = dot(a2, gate_ref[...], 1, 1)
    m1, m2, c1, c2 = choices(routes_ref[...])
    l1 = jnp.sum(logits * m1, axis=1, keepdims=True)
    l2 = jnp.sum(logits * m2, axis=1, keepdims=True)
    top = jnp.maximum(l1, l2)
    x1, x2 = jnp.exp(l1 - top), jnp.exp(l2 - top)
    g1, g2 = x1 / (x1 + x2), x2 / (x1 + x2)
    lane = lax.broadcasted_iota(jnp.int32, (ROWS, 128), 1)
    gates_ref[...] = jnp.where(lane == 0, g1, g2)
    t1, t2 = chosen_t(c1), chosen_t(c2)
    send_ref[:, 0:D] = dot(t1 + t2, a2).astype(BF16)
    send_ref[:, D:] = (dot(t1, two_parts(g1)) + dot(t2, two_parts(g2))).astype(BF16)


def gelu_parts(h):
    d = 1.0 + (0.3275911 * 0.5**0.5) * jnp.abs(h)
    r = pl.reciprocal(d, approx=True)
    t = r * (2.0 - d * r)
    e = jnp.exp2(h * h * (-0.5 * LOG2E))
    poly = t * (
        0.127414796
        + t * (-0.142248368 + t * (0.7107068705 + t * (-0.7265760135 + t * 0.5307027145)))
    )
    tail = poly * e
    phi = jnp.where(h >= 0, 1.0 - tail, tail)
    return h * phi, phi + h * e * (1.0 / math.sqrt(2.0 * math.pi))


def div(a, b):
    return lax.div(a, jnp.int32(b))


def rem(a, b):
    return lax.rem(a, jnp.int32(b))


def coords():
    return tuple(lax.axis_index(a) for a in ALL)


def near(x, pair):
    return x + rem(div(x, 2) + pair, 2) * (3 - 2 * x)


def neighbour(x):
    return x + 1 - 2 * rem(x, 2)


def expert_of(zh, x, zl, y):
    return 4 * (4 * zl + y) + 2 * div(x, 2) + zh


def remote(src, dst, send, recv, device):
    return pltpu.make_async_remote_copy(
        src_ref=src,
        dst_ref=dst,
        send_sem=send,
        recv_sem=recv,
        device_id=device,
        device_id_type=MESH,
    )


def await_bytes(ref, sem):
    pltpu.make_async_copy(ref, ref, sem).wait()


def chip_partner(me, k):
    zh, x, zl, y, c = me
    return (
        rem(zh + div(k, 8), 2),
        rem(x + rem(div(k, 2), 4), 4),
        zl,
        y,
        rem(c + rem(k, 2), 2),
    )


def core_partner(me, k):
    return me[:4] + (rem(me[4] + k, 2),)


def row_partner(me, k):
    zh, x, zl, y, c = me
    return (
        rem(zh + rem(div(k, 8), 2), 2),
        x + div(k, 16) * (3 - 2 * x),
        rem(zl + rem(div(k, 4), 2), 2),
        rem(y + rem(k, 4), 4),
        c,
    )


def head_partner(me, k):
    zh, x, zl, y, c = me
    t = rem(zh * 4 + x + k, 8)
    return t, (div(t, 4), rem(t, 4), zl, y, c)


def greet(me, partner, count):
    barrier = pltpu.get_barrier_semaphore()

    def one(k, carry):
        pl.semaphore_signal(
            barrier, inc=1, device_id=partner(me, k), device_id_type=MESH
        )
        return carry

    lax.fori_loop(1, count, one, 0)
    return count - 1


def hello(*groups):
    me = coords()
    return me, sum(greet(me, partner, count) for partner, count in groups)


def enter(total):
    pl.semaphore_wait(pltpu.get_barrier_semaphore(), total)


class HeadSwap:
    def __init__(self, me, send, recv, sems):
        self.me, self.send, self.recv, self.sems = me, send, recv, sems
        self.place = me[0] * 4 + me[1]

    def leave(self, half):
        s = self.place
        zh, x, zl, y, c = self.me
        for k in (2, 1, 3, 0):
            p = rem(x + k, 4)
            t = 4 * half + p
            away = remote(
                self.send.at[t], self.recv.at[s], self.sems.at[0, t], self.sems.at[1, s], (jnp.int32(half), p, zl, y, c)
            )
            if k:
                away.start()
            else:
                local = pltpu.make_async_copy(self.send.at[t], self.recv.at[t], self.sems.at[1, t])
                pl.when(zh == half)(local.start)
                pl.when(zh != half)(away.start)

    def start(self):
        s = self.place
        pltpu.make_async_copy(self.send.at[s], self.recv.at[s], self.sems.at[1, s]).start()
        for k in (2, 4, 6, 1, 3, 5, 7):
            t, device = head_partner(self.me, jnp.int32(k))
            remote(self.send.at[t], self.recv.at[s], self.sems.at[0, t], self.sems.at[1, s], device).start()

    def arrived(self, t):
        await_bytes(self.recv.at[t], self.sems.at[1, t])

    def wait_send(self):
        for k in range(1, 8):
            t, _ = head_partner(self.me, jnp.int32(k))
            await_bytes(self.send.at[t], self.sems.at[0, t])


class RowSwap:
    def __init__(self, me, send, recv, sems, back=False):
        self.me, self.send, self.recv, self.sems = me, send, recv, sems
        self.back = back

    def slot(self, kx, kz, ky):
        return 8 * rem(8 + ky - kz - 2 * kx, 4) + 4 * kx + kz

    def ends(self, k):
        zh, x, zl, y, c = self.me
        device = row_partner(self.me, k)
        kx, kz, ky = div(k, 16), rem(div(k, 4), 4), rem(k, 4)
        if self.back:
            src = self.slot(kx, kz, ky)
            dst = expert_of(zh, x, zl, y)
        else:
            src = expert_of(*device[:4])
            dst = self.slot(kx, kz, 4 - ky)
        rows = lambda n: pl.ds(pl.multiple_of(n * CAP, CAP), CAP)
        return self.send.at[rows(src)], self.recv.at[rows(dst)], device

    def start(self, first=0, last=32):
        if first == 0:
            src, dst, _ = self.ends(jnp.int32(0))
            pltpu.make_async_copy(src, dst, self.sems.at[1]).start()

        def one(k, carry):
            src, dst, device = self.ends(rem(9 * k, 32))
            remote(src, dst, self.sems.at[0], self.sems.at[1], device).start()
            return carry

        lax.fori_loop(max(first, 1), last, one, 0)

    def start_block(self, r):
        def one(n, carry):
            q = rem(3 * n, 8)
            kx, kz = div(q, 4), rem(q, 4)
            k = 16 * kx + 4 * kz + rem(r + kz + 2 * kx, 4)
            src, dst, device = self.ends(k)
            local = pltpu.make_async_copy(src, dst, self.sems.at[1])
            away = remote(src, dst, self.sems.at[0], self.sems.at[1], device)
            pl.when(k == 0)(local.start)
            pl.when(k != 0)(away.start)
            return carry

        lax.fori_loop(0, 8, one, 0)

    def wait_recv(self):
        await_bytes(self.recv, self.sems.at[1])

    def wait_send(self, first=0, last=31):
        await_bytes(self.send.at[pl.ds(0, (last - first) * CAP)], self.sems.at[0])

    def wait(self):
        self.wait_recv()
        self.wait_send()


def remote_params(n, mb=60):
    return pltpu.CompilerParams(
        vmem_limit_bytes=mb * 2**20, collective_id=n, has_side_effects=True
    )


VMEM = pl.BlockSpec(memory_space=pltpu.VMEM)
ANY = pl.BlockSpec(memory_space=pl.ANY)
DMA = pltpu.SemaphoreType.DMA


class Weights:
    def __init__(self, me, w_in, w_out, full_in, full_out, sems):
        self.me, self.refs, self.full, self.sems = me, (w_in, w_out), (full_in, full_out), sems

    def place(self, i, x, zh):
        at = pl.ds(pl.multiple_of(zh * 384, 128), 384)
        return self.full[0].at[x, :, at] if i == 0 else self.full[1].at[x, at, :]

    def first(self, i, b):
        zh, x, zl, y, c = self.me
        device = (jnp.int32(b), near(x, c), zl, y, zh)
        copy = remote(
            self.refs[i].at[b], self.place(i, x, zh), self.sems.at[0, i, b], self.sems.at[1, i, x], device
        )
        local = pltpu.make_async_copy(
            self.refs[i].at[b], self.place(i, x, zh), self.sems.at[1, i, x]
        )
        own = jnp.logical_and(
            jnp.logical_and(zh == b, div(x, 2) == c), zh == c
        )
        return copy, local, own

    def start(self, i):
        for b in range(2):
            copy, local, own = self.first(i, b)
            pl.when(own)(local.start)
            pl.when(jnp.logical_not(own))(copy.start)

    def forward(self, i, x, step):
        zh, me_x, zl, y, c = self.me
        piece = self.place(i, x, c)
        device = (zh, neighbour(me_x), zl, y, c) if step == 2 else (zh, me_x, zl, y, 1 - c)
        return remote(piece, piece, self.sems.at[2 * step - 2, i, x], self.sems.at[2 * step - 1, i, x], device)

    def sources(self, step):
        x = self.me[1]
        if step == 1:
            return x, 3 - x
        return neighbour(x), 3 - neighbour(x)

    def second(self, i):
        for x in self.sources(1):
            await_bytes(self.place(i, x, self.me[4]), self.sems.at[1, i, x])
            self.forward(i, x, 2).start()
            self.forward(i, x, 3).start()

    def third(self, i):
        for x in self.sources(2):
            self.forward(i, x, 2).wait_recv()
            self.forward(i, x, 3).start()

    def ready(self, i):
        for x in range(4):
            self.forward(i, jnp.int32(x), 3).wait_recv()

    def finish(self, i):
        for b in range(2):
            copy, _, own = self.first(i, b)
            pl.when(jnp.logical_not(own))(copy.wait_send)
        for x in self.sources(1):
            self.forward(i, x, 2).wait_send()
        for x in range(4):
            self.forward(i, jnp.int32(x), 3).wait_send()


STEP = 256
CHUNKS = 4
TILES = SLOTS // STEP


def row_block(r):
    return pl.ds(pl.multiple_of(r * STEP, STEP), STEP)


def half_rows(n):
    return pl.ds(pl.multiple_of(n * 384, 128), 384)


def front_body(tok_ref, cot_ref, gain1_ref, w_qkv_ref, w_o_ref, gain2_ref, gate_ref, routes_ref, w_in_ref, w_out_ref,
               qkv_out, ret_ref, y_ref, mid_out, att_out, gates_out, ot_out, lse_out, dwin_out, total_out,
               qkv_ref, mid_ref, att_ref, gates_ref, ot_ref, lse_ref, total_ref, xt_ref,
               qkv_send, o_send, o_recv, x_send, c_send, x_ref, c_ref, vt_ref, full_in, full_out, g_ref, d_ref,
               part_in, part_out, got_in, got_out, got2,
               head_sems, row_sems, weight_sems, load_sems, save_sems, core_sems, pair_sems):
    loads = [
        pltpu.make_async_copy(w_qkv_ref.at[:, p * D : p * D + D], g_ref.at[p, 0:D], load_sems.at[p]) for p in range(3)
    ] + [pltpu.make_async_copy(w_o_ref, g_ref.at[3, 0:D], load_sems.at[3])]
    for load in loads:
        load.start()
    me, greeted = hello((chip_partner, 16), (row_partner, 32))
    zh, x, zl, y, c = me
    weights = Weights(me, w_in_ref, w_out_ref, full_in, full_out, weight_sems)
    heads = HeadSwap(me, qkv_send, qkv_ref, head_sems.at[0])
    heads_back = HeadSwap(me, o_send, o_recv, head_sems.at[1])
    rows_c = RowSwap(me, c_send, c_ref, row_sems.at[0])
    rows_x = RowSwap(me, x_send, x_ref, row_sems.at[1])
    rows_ret = RowSwap(me, x_send, ret_ref, row_sems.at[2], back=True)
    rows_y = RowSwap(me, c_send, y_ref, row_sems.at[3], back=True)

    def part_weights(p):
        loads[p].wait()
        return g_ref[p, 0:D, :]

    project(tok_ref, gain1_ref, part_weights, qkv_send)
    enter(greeted)
    heads.start()
    weights.start(0)
    deal_body(cot_ref, routes_ref, c_send)
    heads.arrived(0)
    heads.arrived(1)
    weights.start(1)
    attend_forward(
        rem(x, 2), qkv_ref, o_send, ot_ref, lse_ref, vt_ref,
        lambda b: heads.arrived(b) if b > 1 else None, heads_back.leave,
    )
    weights.second(0)
    for t in range(BLOCKS):
        heads_back.arrived(t)
    loads[3].wait()
    middle_body(o_recv, tok_ref, g_ref[3, 0:D, :], gain2_ref, gate_ref, routes_ref, mid_ref, att_ref, x_send, gates_ref)
    rows_x.start()
    saves = [
        pltpu.make_async_copy(src, dst, save_sems.at[n])
        for n, (src, dst) in enumerate(
            ((qkv_ref, qkv_out), (mid_ref, mid_out), (att_ref, att_out), (gates_ref, gates_out), (ot_ref, ot_out), (lse_ref, lse_out))
        )
    ]
    for save in saves:
        save.start()
    weights.second(1)
    weights.third(0)
    rows_x.wait_send(0, 22)
    rows_c.start()
    weights.ready(0)
    rows_x.wait_recv()
    rows_x.wait_send(22, 31)

    def hidden(j):
        tiles = [slice(r * STEP, r * STEP + STEP) for r in range(TILES)]
        w = full_in[j]

        def after(at, h):
            g, d = gelu_parts(h)
            g_ref[j, at, :] = g.astype(BF16)
            d_ref[j, at, :] = d.astype(BF16)

        before = dot(x_ref[tiles[0], 0:D], w)
        for r in range(1, TILES):
            h = dot(x_ref[tiles[r], 0:D], w)
            after(tiles[r - 1], before)
            before = h
        after(tiles[-1], before)

    def hidden_loop(j, carry):
        hidden(j)
        return carry

    lax.fori_loop(0, CHUNKS - 1, hidden_loop, 0)
    weights.third(1)
    hidden(CHUNKS - 1)
    for r in range(TILES):
        xt_ref[:, r * STEP : (r + 1) * STEP] = x_ref[r * STEP : (r + 1) * STEP, 0:D].T
    weights.ready(1)
    rows_c.wait()

    def produce(n, carry):
        r = TILES - 1 - n
        at = row_block(r)
        c_ref[at, :] = (c_ref[at, :].astype(F32) * from_parts(x_ref[at, D:])).astype(BF16)
        out = dot(g_ref[0, at, :], full_out[0])
        for j in range(1, CHUNKS):
            out = out + dot(g_ref[j, at, :], full_out[j])
        c_send[at, :] = out.astype(BF16)
        rows_y.start_block(r)
        return carry

    lax.fori_loop(0, TILES, produce, 0)

    sibling = core_partner(me, 1)

    def half(i, j, n):
        return part_in.at[j, :, half_rows(n)] if i == 0 else part_out.at[j, half_rows(n), :]

    def over(i, j):
        got = (got_in, got_out)[i]
        return remote(half(i, j, 1 - c), got.at[j], core_sems.at[0, i, j], core_sems.at[1, i, j], sibling)

    def second_grad(j, carry):
        part_out[j] = dot(g_ref[j], c_ref[...], 0, 0).astype(BF16)
        over(1, j).start()
        return carry

    lax.fori_loop(0, CHUNKS, second_grad, 0)

    def second_sum(j, carry):
        over(1, j).wait()
        got_out[j] = (half(1, j, c)[...].astype(F32) + got_out[j].astype(F32)).astype(BF16)
        return carry

    lax.fori_loop(0, CHUNKS, second_sum, 0)
    pass_on, keep = (neighbour(x), 3 - neighbour(x)), (x, 3 - x)

    def pair_over(n):
        return remote(got_out.at[pass_on[n]], got2.at[n], pair_sems.at[0, n], pair_sems.at[1, n], (zh, neighbour(x), zl, y, c))

    for n in range(2):
        pair_over(n).start()

    def back(n, carry):
        r = TILES - 1 - n
        at = row_block(r)
        total = jnp.zeros((STEP, 128), F32)
        dx = jnp.zeros((STEP, D), F32)
        for j in range(CHUNKS):
            cw = dot(c_ref[at, :], full_out[j], 1, 1)
            dh = (d_ref[j, at, :].astype(F32) * cw).astype(BF16)
            prod = g_ref[j, at, :].astype(F32) * cw
            for t in range(D // 128):
                total = total + prod[:, 128 * t : 128 * t + 128]
            d_ref[j, at, :] = dh
            dx = dx + dot(dh, full_in[j], 1, 1)
        x_send[at, 0:D] = dx.astype(BF16)
        x_send[at, D:] = two_parts(jnp.sum(total, axis=1, keepdims=True))
        rows_ret.start_block(r)
        return carry

    lax.fori_loop(0, TILES, back, 0)

    def first_grad(n, carry):
        j, r = div(n, 3), rem(n, 3)
        part_in[j, row_block(r), :] = dot(xt_ref[row_block(r), :], d_ref[j]).astype(BF16)

        @pl.when(r == 2)
        def _():
            over(0, j).start()

        return carry

    lax.fori_loop(0, 3 * CHUNKS, first_grad, 0)

    def first_save(j):
        return pltpu.make_async_copy(got_in.at[j], dwin_out.at[j], save_sems.at[7])

    def first_sum(j, carry):
        over(0, j).wait()
        got_in[j] = (half(0, j, c)[...].astype(F32) + got_in[j].astype(F32)).astype(BF16)
        first_save(j).start()
        return carry

    lax.fori_loop(0, CHUNKS, first_sum, 0)
    heads.wait_send()
    heads_back.wait_send()
    weights.finish(0)
    weights.finish(1)
    for n in range(2):
        pair_over(n).wait()
        total_ref[n] = (got_out[keep[n]].astype(F32) + got2[n].astype(F32)).astype(BF16)
    last = pltpu.make_async_copy(total_ref, total_out, save_sems.at[6])
    last.start()
    for save in saves:
        save.wait()
    rows_y.wait()
    rows_ret.wait()
    last.wait()
    await_bytes(dwin_out, save_sems.at[7])


def front(tok, cot, gain1, w_qkv, w_o, gain2, gate, routes, w_in, w_out):
    buf = lambda *s: pltpu.VMEM(s, BF16)
    f32 = lambda *s: pltpu.VMEM(s, F32)
    outs = [
        ((BLOCKS, ROWS, 384), BF16),
        ((SLOTS, D + EXTRA), BF16),
        ((SLOTS, D), BF16),
        ((ROWS, D), F32),
        ((ROWS, D), BF16),
        ((ROWS, 128), F32),
        ((12, 64, ROWS), F32),
        ((12, 8, ROWS), F32),
        ((CHUNKS, D, 384), BF16),
        ((2, 384, D), BF16),
    ]
    return pl.pallas_call(
        front_body,
        out_shape=[jax.ShapeDtypeStruct(s, t) for s, t in outs],
        in_specs=[VMEM] * 3 + [ANY] * 2 + [VMEM] * 3 + [ANY] * 2,
        out_specs=[ANY] * len(outs),
        scratch_shapes=[
            buf(BLOCKS, ROWS, 384),
            f32(ROWS, D),
            buf(ROWS, D),
            f32(ROWS, 128),
            f32(12, 64, ROWS),
            f32(12, 8, ROWS),
            buf(2, 384, D),
            buf(D, SLOTS),
            buf(BLOCKS, ROWS, 384),
            buf(BLOCKS, ROWS, 128),
            buf(BLOCKS, ROWS, 128),
            buf(SLOTS, D + EXTRA),
            buf(SLOTS, D),
            buf(SLOTS, D + EXTRA),
            buf(SLOTS, D),
            buf(128, BLOCKS * ROWS),
            buf(CHUNKS, D, D),
            buf(CHUNKS, D, D),
            buf(CHUNKS, SLOTS, D),
            buf(CHUNKS, SLOTS, D),
            buf(CHUNKS, D, D),
            buf(CHUNKS, D, D),
            buf(CHUNKS, D, 384),
            buf(CHUNKS, 384, D),
            buf(2, 384, D),
            DMA((2, 2, 8)),
            DMA((4, 2)),
            DMA((6, 2, 4)),
            DMA((4,)),
            DMA((8,)),
            DMA((2, 2, 4)),
            DMA((2, 2)),
        ],
        compiler_params=remote_params(0, 63),
    )(tok, cot, gain1, w_qkv, w_o, gain2, gate, routes, w_in, w_out)


def back_body(ret_ref, cot_ref, routes_ref, gates_ref, mid_ref, gain_ref, gate_w_ref, w_o_ref,
              send_ref, dmid_ref, gate_grad_ref, gain_grad_ref):
    m1, m2, c1, c2 = choices(routes_ref[...])
    s1, s2 = chosen(c1), chosen(c2)
    g1, g2 = gates_ref[:, 0:1], gates_ref[:, 1:2]
    extra = ret_ref[:, D:]
    d1, d2 = from_parts(dot(s1, extra)), from_parts(dot(s2, extra))
    dl = g2 * d1 - g1 * d2
    dlogits = (m1 - m2) * dl
    unit, inv = norm(mid_ref[...])
    high = dlogits.astype(BF16)
    low = (dlogits - high.astype(F32)).astype(BF16)
    gate_w = gate_w_ref[...]
    da2 = dot(s1 + s2, ret_ref[:, 0:D]) + dot(high, gate_w) + dot(low, gate_w)
    dmid = cot_ref[...].astype(F32) + norm_back(da2, row_of(gain_ref), unit, inv)
    dmid_ref[...] = dmid
    do = dot(dmid.astype(BF16), w_o_ref[...], 1, 1)
    for s in range(BLOCKS):
        send_ref[s] = pair_up(do, s).astype(BF16)

    def later():
        a2 = (unit * row_of(gain_ref)).astype(BF16)
        gate_grad_ref[...] = dot(high, a2, 0, 0) + dot(low, a2, 0, 0)
        gain_grad_ref[...] = jnp.sum(da2 * unit, axis=0, keepdims=True)

    return later


def axis_place(me, a):
    zh, x, zl, y, c = me
    return (x, y, 2 * zh + zl)[a]


def axis_peer(me, a, k):
    zh, x, zl, y, c = me
    p = rem(axis_place(me, a) + k, 4)
    if a == 0:
        return p, (zh, p, zl, y, c)
    if a == 1:
        return p, (zh, x, zl, p, c)
    return p, (div(p, 2), x, rem(p, 2), y, c)


def axis_partner(me, k):
    zh, x, zl, y, c = me
    along_z = div(k, 4)
    dz = rem(k + 1, 4) * along_z
    z = rem(2 * zh + zl + dz, 4)
    return div(z, 2), x, rem(z, 2), rem(y + k * (1 - along_z), 4), c


def multiple(n, w):
    return pl.ds(pl.multiple_of(n * w, w), w)


PEERS = (1, 2, 3)


class GroupSum:
    def __init__(self, me, g, axes, out, bufs, sems):
        self.me, self.g, self.axes, self.out, self.sems = me, g, axes, out, sems.at[g]
        self.s0, self.r0, self.a0, self.r1, self.a1, self.s2, self.r2, self.r3, self.whole = [b.at[g] for b in bufs]
        self.place = [axis_place(me, a) for a in axes]
        self.c = me[4]

    def copy(self, stage, k, src, dst):
        if stage in (0, 6):
            device = core_partner(self.me, 1)
        else:
            device = axis_peer(self.me, self.axes[(0, 0, 1, 2, 1, 0)[stage]], jnp.int32(k))[1]
        return remote(src, dst, self.sems.at[stage, 0, k], self.sems.at[stage, 1, k], device)

    def peer(self, t, k):
        return axis_peer(self.me, self.axes[t], jnp.int32(k))[0]

    def swap(self):
        return self.copy(0, 0, self.s0, self.r0)

    def scatter1(self, k):
        return self.copy(1, k, self.s0.at[multiple(self.peer(0, k), 192)], self.r1.at[k - 1])

    def scatter2(self, k):
        return self.copy(2, k, self.s2.at[multiple(self.peer(1, k), 48)], self.r2.at[k - 1])

    def share(self, k):
        mine = self.r3.at[self.place[2]]
        return self.copy(3, k, mine, mine)

    def block(self, rows):
        i, j = self.place[0], self.place[1]
        if rows == 48:
            return self.whole.at[multiple(4 * i + j, 48)]
        if rows == 192:
            return self.whole.at[multiple(i, 192)]
        return self.whole

    def gather(self, stage, k):
        ref = self.block((48, 192, 768)[stage - 4])
        if stage < 6:
            return self.copy(stage, k, ref, ref)
        lanes = pl.ds(pl.multiple_of(self.g * D + self.c * 384, 128), 384)
        return self.copy(stage, k, ref, self.out.at[:, lanes])

    def save(self):
        lanes = pl.ds(pl.multiple_of(self.g * D + self.c * 384, 128), 384)
        return pltpu.make_async_copy(self.whole, self.out.at[:, lanes], self.sems.at[6, 0, 1])

    def begin(self, grad):
        self.s0[...] = grad(1 - self.c).astype(BF16)
        self.swap().start()
        self.a0[...] = grad(self.c)

    def step1(self):
        self.swap().wait()
        self.a0[...] += self.r0[...].astype(F32)
        self.s0[...] = self.a0[...].astype(BF16)
        for k in PEERS:
            self.scatter1(k).start()

    def step2(self):
        for k in PEERS:
            self.scatter1(k).wait_recv()
        mine = self.a0[multiple(self.place[0], 192), :]
        for k in PEERS:
            mine = mine + self.r1[k - 1].astype(F32)
        self.a1[...] = mine
        self.s2[...] = mine.astype(BF16)
        for k in PEERS:
            self.scatter2(k).start()

    def step3(self):
        for k in PEERS:
            self.scatter2(k).wait_recv()
        mine = self.a1[multiple(self.place[1], 48), :]
        for k in PEERS:
            mine = mine + self.r2[k - 1].astype(F32)
        self.r3[self.place[2]] = mine.astype(BF16)
        for k in PEERS:
            self.share(k).start()

    def step4(self):
        for k in PEERS:
            p = axis_peer(self.me, self.axes[2], jnp.int32(k))[0]
            self.copy(3, 4 - k, self.r3.at[p], self.r3.at[p]).wait_recv()
        total = (self.r3[0].astype(F32) + self.r3[1].astype(F32)) + (
            self.r3[2].astype(F32) + self.r3[3].astype(F32)
        )
        self.block(48)[...] = total.astype(BF16)
        for k in PEERS:
            self.gather(4, k).start()

    def step5(self):
        for k in PEERS:
            self.gather(4, k).wait_recv()
        for k in PEERS:
            self.gather(5, k).start()

    def step6(self):
        for k in PEERS:
            self.gather(5, k).wait_recv()
        self.gather(6, 0).start()
        self.save().start()

    def finish(self):
        self.gather(6, 0).wait()
        self.save().wait()
        for k in PEERS:
            self.scatter1(k).wait_send()
            self.scatter2(k).wait_send()
            self.share(k).wait_send()
            self.gather(4, k).wait_send()
            self.gather(5, k).wait_send()


class SmallSum:
    def __init__(self, me, mine, over, slots, out, sems):
        self.me, self.mine, self.over, self.slots, self.out, self.sems = me, mine, over, slots, out, sems

    def half(self, ref, n):
        return ref.at[:, half_rows(n)]

    def swap(self):
        return remote(self.over.at[0], self.over.at[1], self.sems.at[0, 0], self.sems.at[1, 0], core_partner(self.me, 1))

    def share(self, a, k):
        n = 3 * a + k
        mine = self.slots.at[a, axis_place(self.me, a)]
        return remote(mine, mine, self.sems.at[0, n], self.sems.at[1, n], axis_peer(self.me, a, jnp.int32(k))[1])

    def join(self):
        mine = self.half(self.out, self.me[4])
        return remote(mine, mine, self.sems.at[0, 10], self.sems.at[1, 10], core_partner(self.me, 1))

    def begin(self):
        self.over[0] = self.half(self.mine, 1 - self.me[4])[...].astype(BF16)
        self.swap().start()

    def step(self, a):
        if a == 0:
            self.swap().wait_recv()
            total = self.half(self.mine, self.me[4])[...] + self.over[1].astype(F32)
        else:
            for k in PEERS:
                self.share(a - 1, k).wait_recv()
            s = [self.slots[a - 1, p].astype(F32) for p in range(4)]
            total = (s[0] + s[1]) + (s[2] + s[3])
        if a < 3:
            self.slots[a, axis_place(self.me, a)] = total.astype(BF16)
            for k in PEERS:
                self.share(a, k).start()
        else:
            self.half(self.out, self.me[4])[...] = total.astype(BF16)
            self.join().start()

    def finish(self):
        self.join().wait()
        self.swap().wait_send()
        for a in range(3):
            for k in PEERS:
                self.share(a, k).wait_send()


class Collect:
    def __init__(self, me, dw, kept, got, total, fin, sems):
        self.me, self.dw, self.kept, self.got, self.fin, self.sems = me, dw, kept, got, fin, sems
        x = me[1]
        self.totals = (got, total)
        self.keep, self.pass_on = (x, 3 - x), (neighbour(x), 3 - neighbour(x))

    def second(self, j, at=slice(None)):
        zh, x, zl, y, c = self.me
        return remote(self.dw.at[self.pass_on[j], at], self.got.at[j, at], self.sems.at[0, 0, j], self.sems.at[1, 0, j],
                      (zh, neighbour(x), zl, y, c))

    def quarters(self, j):
        return [self.second(j, slice(192 * q, 192 * q + 192)) for q in range(4)]

    def third(self, i, j):
        zh, x, zl, y, c = self.me
        pair = div(x, 2)
        src = self.totals[i].at[j]
        copy = remote(src, self.fin[i].at[zh], self.sems.at[2, i, j], self.sems.at[3, i, zh], (c, self.keep[j], zl, y, pair))
        local = pltpu.make_async_copy(src, self.fin[i].at[zh], self.sems.at[3, i, zh])
        if j == 1:
            return copy, None, None
        return copy, local, jnp.logical_and(zh == c, pair == c)

    def load(self, j, sem):
        return pltpu.make_async_copy(self.dw.at[self.keep[j]], self.kept.at[j], sem)

    def add(self, j):
        self.second(j).wait_recv()
        self.got[j] = (self.kept[j].astype(F32) + self.got[j].astype(F32)).astype(BF16)

    def send(self, i, j):
        copy, local, own = self.third(i, j)
        if j == 1:
            copy.start()
        else:
            pl.when(own)(local.start)
            pl.when(jnp.logical_not(own))(copy.start)

    def finish(self):
        for j in range(2):
            self.second(j).wait_send()
        for i in range(2):
            for j in range(2):
                copy, _, own = self.third(i, j)
                if j == 1:
                    copy.wait_send()
                else:
                    pl.when(jnp.logical_not(own))(copy.wait_send)
            for b in range(2):
                await_bytes(self.fin[i].at[b], self.sems.at[3, i, b])


def rear_body(cot_ref, routes_ref, gain2_ref, gate_w_ref, tok_ref, gain1_ref,
              ret_in, gates_in, mid_in, att_in, w_o_in, qkv_in, ot_in, lse_in, w_qkv_in, y_in, dw_ref, total_ref,
              tok_grad_out, grads_out, early_ref, late_ref, out_out, fin_in, fin_out,
              ret_ref, gates_ref, mid_ref, att_ref, w_o_ref, qkv_ref, ot_ref, lse_ref, w_qkv_ref, y_ref, kept, out_ref, tok_grad_ref,
              dmid_ref, do_send, do_recv, dqkv_send, dqkv_recv, kt_ref, dk_ref, dv_ref, d_ref, datt_ref, got,
              s0, r0, a0, r1, a1, s2, r2, r3, whole, early, early_over, early_slots, late, late_over, late_slots,
              load_sems, save_sems, head_sems, collect_sems, group_sems, small_sems):
    me = coords()
    collect = Collect(me, dw_ref, kept, got, total_ref, (fin_in, fin_out), collect_sems)
    pairs = (
        (ret_in, ret_ref), (mid_in, mid_ref), (gates_in, gates_ref), (w_o_in, w_o_ref), (att_in, att_ref), (y_in, y_ref),
        (qkv_in, qkv_ref), (ot_in, ot_ref), (lse_in, lse_ref), (w_qkv_in, w_qkv_ref),
    )
    loads = [pltpu.make_async_copy(src, dst, load_sems.at[n]) for n, (src, dst) in enumerate(pairs)]
    loads += [collect.load(j, load_sems.at[10 + j]) for j in range(2)]
    for load in loads:
        load.start()
    _, greeted = hello((chip_partner, 16), (axis_partner, 7))
    heads = HeadSwap(me, do_send, do_recv, head_sems.at[0])
    heads_back = HeadSwap(me, dqkv_send, dqkv_recv, head_sems.at[1])
    bufs = (s0, r0, a0, r1, a1, s2, r2, r3, whole)
    orders = ((0, 1, 2), (1, 2, 0), (2, 0, 1), (1, 0, 2))
    groups = [GroupSum(me, g, orders[g], grads_out, bufs, group_sems) for g in range(4)]
    qkv_groups, o_group = groups[:3], groups[3]
    small = SmallSum(me, early, early_over, early_slots, early_ref, small_sems.at[0])
    small_late = SmallSum(me, late, late_over, late_slots, late_ref, small_sems.at[1])
    early[...] = jnp.zeros_like(early)
    late[...] = jnp.zeros_like(late)
    parts = [copy.start for j in range(2) for copy in collect.quarters(j)]

    def pump(n):
        for _ in range(min(n, len(parts))):
            parts.pop(0)()

    for load in loads[:4]:
        load.wait()
    enter(greeted)
    pump(2)
    collect.send(1, 0)
    later = back_body(ret_ref, cot_ref, routes_ref, gates_ref, mid_ref, gain2_ref, gate_w_ref, w_o_ref,
                      do_send, dmid_ref, early.at[0:32], early.at[32:33])
    heads.start()
    later()
    small.begin()
    datt_ref[...] = dmid_ref[...].astype(BF16)
    for load in loads[4:]:
        load.wait()
    o_group.begin(lambda n: dot(att_ref[...], datt_ref[:, half_rows(n)], 0, 0))
    _, _, c1, c2 = choices(routes_ref[...])
    rows = y_ref[...]
    mix = gates_ref[:, 0:1] * dot(chosen(c1), rows) + gates_ref[:, 1:2] * dot(chosen(c2), rows)
    out_ref[...] = (mid_ref[...] + mix).astype(BF16)
    saves = [pltpu.make_async_copy(out_ref, out_out, save_sems.at[0]), pltpu.make_async_copy(tok_grad_ref, tok_grad_out, save_sems.at[1])]
    saves[0].start()
    for t in range(BLOCKS):
        heads.arrived(t)
    small.step(0)
    o_group.step1()
    collect.send(1, 1)
    pump(2)

    attend_backward(rem(me[1], 2), qkv_ref, do_recv, ot_ref, lse_ref, dqkv_send, kt_ref, dk_ref, dv_ref,
                    lambda b: None, heads_back.leave, lambda pair: None)
    small.step(1)
    o_group.step2()
    pump(4)
    collect.add(0)
    collect.send(0, 0)
    unit, inv = norm(tok_ref[...].astype(F32))
    a1_rows = (unit * row_of(gain1_ref)).astype(BF16)
    for t in range(BLOCKS):
        heads_back.arrived(t)
    for part in range(3):
        tiles = unpair(
            [dqkv_recv[s, :, part * 128 : part * 128 + 128].astype(F32) for s in range(BLOCKS)]
        )
        for t in range(6):
            d_ref[part, :, 128 * t : 128 * t + 128] = tiles[t].astype(BF16)
        qkv_groups[part].begin(lambda n: dot(a1_rows, d_ref[part, :, half_rows(n)], 0, 0))
    small.step(2)
    o_group.step3()
    for g in qkv_groups:
        g.step1()
    da1 = dot(d_ref[0], w_qkv_ref[:, 0:D], 1, 1)
    for part in (1, 2):
        da1 = da1 + dot(d_ref[part], w_qkv_ref[:, part * D : part * D + D], 1, 1)
    late[0:1] = jnp.sum(da1 * unit, axis=0, keepdims=True)
    small_late.begin()
    tok_grad_ref[...] = dmid_ref[...] + norm_back(da1, row_of(gain1_ref), unit, inv)
    saves[1].start()
    small.step(3)
    o_group.step4()
    small_late.step(0)
    for g in qkv_groups:
        g.step2()
    small_late.step(1)
    for g in qkv_groups:
        g.step3()
    collect.add(1)
    collect.send(0, 1)
    o_group.step5()
    small_late.step(2)
    for g in qkv_groups:
        g.step4()
    small_late.step(3)
    for g in qkv_groups:
        g.step5()
    o_group.step6()
    for g in qkv_groups:
        g.step6()
    small.finish()
    small_late.finish()
    heads.wait_send()
    heads_back.wait_send()
    collect.finish()
    for g in groups:
        g.finish()
    for save in saves:
        save.wait()


def rear(*args):
    buf = lambda *s: pltpu.VMEM(s, BF16)
    f32 = lambda *s: pltpu.VMEM(s, F32)
    return pl.pallas_call(
        rear_body,
        out_shape=[
            jax.ShapeDtypeStruct((ROWS, D), F32),
            jax.ShapeDtypeStruct((D, 4 * D), BF16),
            jax.ShapeDtypeStruct((48, D), BF16),
            jax.ShapeDtypeStruct((16, D), BF16),
            jax.ShapeDtypeStruct((ROWS, D), BF16),
            jax.ShapeDtypeStruct((2, D, 384), BF16),
            jax.ShapeDtypeStruct((2, 384, D), BF16),
        ],
        in_specs=[VMEM] * 6 + [ANY] * 12,
        out_specs=[ANY, ANY, VMEM, VMEM, ANY, ANY, ANY],
        scratch_shapes=[
            buf(SLOTS, D + EXTRA),
            f32(ROWS, 128),
            f32(ROWS, D),
            buf(ROWS, D),
            buf(D, D),
            buf(BLOCKS, ROWS, 384),
            f32(12, 64, ROWS),
            f32(12, 8, ROWS),
            buf(D, 3 * D),
            buf(SLOTS, D),
            buf(2, D, 384),
            buf(ROWS, D),
            f32(ROWS, D),
            f32(ROWS, D),
            buf(BLOCKS, ROWS, 128),
            buf(BLOCKS, ROWS, 128),
            buf(BLOCKS, ROWS, 384),
            buf(BLOCKS, ROWS, 384),
            buf(128, BLOCKS * ROWS),
            f32(BLOCKS * ROWS, 128),
            f32(BLOCKS * ROWS, 128),
            buf(3, ROWS, D),
            buf(ROWS, D),
            buf(2, D, 384),
            buf(4, D, 384),
            buf(4, D, 384),
            f32(4, D, 384),
            buf(4, 3, 192, 384),
            f32(4, 192, 384),
            buf(4, 192, 384),
            buf(4, 3, 48, 384),
            buf(4, 4, 48, 384),
            buf(4, D, 384),
            f32(48, D),
            buf(2, 48, 384),
            buf(3, 4, 48, 384),
            f32(16, D),
            buf(2, 16, 384),
            buf(3, 4, 16, 384),
            DMA((12,)),
            DMA((2,)),
            DMA((2, 2, 8)),
            DMA((4, 2, 2)),
            DMA((4, 7, 2, 4)),
            DMA((2, 2, 11)),
        ],
        compiler_params=remote_params(2),
    )(*args)


def on_device(tokens, cotangent, gain_first, w_qkv, w_o, gain_second, w_gate, w_in, w_out, routes, frozen):
    e = (lax.axis_index("zl") * 4 + lax.axis_index("y")) * 2 + lax.axis_index("c")
    tok, cot, routes, gate_t = tokens[0], cotangent[0], routes[0].T, w_gate.T
    qkv, ret, y, mid, att, gates, ot, lse, dw_in, total_out = front(
        tok, cot, gain_first, w_qkv, w_o, gain_second, gate_t, routes, w_in, w_out
    )
    keep = (1 - lax.dynamic_slice_in_dim(frozen, 2 * e, 2)).astype(F32)
    tok_grad, grads, early, late, out, w_in_grad, w_out_grad = rear(
        cot, routes, gain_second, gate_t, tok, gain_first, ret, gates, mid, att, w_o, qkv, ot, lse, w_qkv, y, dw_in, total_out
    )
    return (
        out[None],
        tok_grad[None],
        late[0].astype(F32),
        grads[:, : 3 * D].astype(F32),
        grads[:, 3 * D :].astype(F32),
        early[32].astype(F32),
        early[:32].T.astype(F32) * (1 - frozen).astype(F32)[None, :],
        w_in_grad.astype(F32) * keep[:, None, None],
        w_out_grad.astype(F32) * keep[:, None, None],
    )


def solution(mesh):
    fine = Mesh(mesh.devices.reshape(2, 4, 2, 4, 2), ALL)
    seq, exp = ("zh", "x"), ("zl", "y", "c")
    rows, rest = P(exp, seq, None), P()
    in_specs = (rows, rows, rest, rest, rest, rest, rest, P(exp, None, seq), rows, rows, rest)
    out_specs = (rows, rows, rest, rest, rest, rest, rest, P(exp, None, seq), rows)
    return jax.shard_map(on_device, mesh=fine, in_specs=in_specs, out_specs=out_specs, check_vma=False)
```

```python
import functools
import math

import jax
import jax.numpy as jnp
from jax import lax
from jax.experimental import pallas as pl
from jax.experimental.pallas import tpu as pltpu
from jax.sharding import Mesh
from jax.sharding import PartitionSpec as P

D = 768
HEADS = 12
HEAD_DIM = 64
EXPERTS = 32
CAP = 32
ROWS = 256
BLOCKS = 8
FF = 3072
SLOTS = EXPERTS * CAP
EXTRA = 128
EPS = 1e-5
SCALE = HEAD_DIM ** -0.5
LOG2E = math.log2(math.e)
BF16 = jnp.bfloat16
F32 = jnp.float32
NEG = -1e30

SEQ = ("zh", "x")
MESH = pl.DeviceIdType.MESH
ALL = ("zh", "x", "zl", "y", "c")


def dot(a, b, ca=1, cb=0):
    return lax.dot_general(a, b, (((ca,), (cb,)), ((), ())), preferred_element_type=F32)


def params(mb=56):
    return pltpu.CompilerParams(vmem_limit_bytes=mb * 2**20)


def vspec(n):
    return [pl.BlockSpec(memory_space=pltpu.VMEM)] * n


def call(body, outs, n_in, scratch=(), **kw):
    return pl.pallas_call(
        body,
        out_shape=[jax.ShapeDtypeStruct(s, t) for s, t in outs],
        in_specs=vspec(n_in),
        out_specs=vspec(len(outs)),
        scratch_shapes=list(scratch),
        compiler_params=params(),
        **kw,
    )


def norm(v):
    mean = jnp.mean(v, axis=-1, keepdims=True)
    centred = v - mean
    inv = lax.rsqrt(jnp.mean(centred * centred, axis=-1, keepdims=True) + EPS)
    return centred * inv, inv


def row_of(gain_ref):
    return gain_ref[...].reshape(1, D)


def norm_back(grad, gain, unit, inv):
    t = grad * gain
    m1 = jnp.mean(t, axis=-1, keepdims=True)
    m2 = jnp.mean(t * unit, axis=-1, keepdims=True)
    return inv * (t - m1 - unit * m2)


def lane_low():
    return lax.broadcasted_iota(jnp.int32, (1, 128), 1) < 64


def pair_up(wide, s):
    low = wide[:, 128 * (s // 2) : 128 * (s // 2) + 128]
    if s % 2:
        low = pltpu.roll(low, 64, 1)
    high = wide[:, 512 + 128 * (s // 4) : 640 + 128 * (s // 4)]
    if (s // 2) % 2 == 0:
        high = pltpu.roll(high, 64, 1)
    return jnp.where(lane_low(), low, high)


def unpair(tiles):
    out = []
    for t in range(4):
        out.append(
            jnp.where(lane_low(), tiles[2 * t], pltpu.roll(tiles[2 * t + 1], 64, 1))
        )
    for t in range(2):
        a = tiles[4 * t] + tiles[4 * t + 1]
        b = tiles[4 * t + 2] + tiles[4 * t + 3]
        out.append(jnp.where(lane_low(), pltpu.roll(a, 64, 1), b))
    return out


def project(tok_ref, gain_ref, part_weights, send_ref):
    unit, _ = norm(tok_ref[...].astype(F32))
    a1 = (unit * row_of(gain_ref)).astype(BF16)
    for part in range(3):
        wide = dot(a1, part_weights(part))
        for s in range(BLOCKS):
            send_ref[s, :, part * 128 : part * 128 + 128] = pair_up(wide, s).astype(
                BF16
            )


def unit_of(half, h, i):
    if h == 0:
        return 0, i, i + 1, i, i
    a, b = ((0, 1), (3, 2), (4, 5), (7, 6))[i]
    return 1, a + half * (b - a), 2 * i + 2, 2 * i, BLOCKS + i


def masked_scores(k, q, block, first, count):
    s = dot(k, q, 1, 1)
    start = first * ROWS
    tail = (count - first) * ROWS
    keys = lax.broadcasted_iota(jnp.int32, (tail, ROWS), 0) + start
    queries = lax.broadcasted_iota(jnp.int32, (tail, ROWS), 1) + block * ROWS
    end = jnp.where(keys <= queries, s[start:], NEG)
    return end if start == 0 else jnp.concatenate([s[:start], end], axis=0)


def head_mask(h):
    low = lane_low()
    return (low if h == 0 else jnp.logical_not(low)).astype(F32).astype(BF16)


def padded(h, t):
    zero = jnp.zeros_like(t)
    return jnp.concatenate([t, zero] if h == 0 else [zero, t], axis=0).T


def attend_forward(half, qkv_ref, o_ref, ot_ref, lse_ref, vt_ref, arrived, leave):
    c = SCALE * LOG2E
    for pair in range(BLOCKS // 2):
        for b in (2 * pair, 2 * pair + 1):
            arrived(b)
            vt_ref[:, b * ROWS : (b + 1) * ROWS] = qkv_ref[b, :, 256:384].T
            o_ref[b] = jnp.zeros((ROWS, 128), BF16)
        for unit in ((1, pair), (0, 2 * pair), (0, 2 * pair + 1)):
            h, block, count, first, u = unit_of(half, *unit)
            q = qkv_ref[block, :, 0:128] * head_mask(h)
            k = qkv_ref[0:count, :, 128:256].reshape(count * ROWS, 128)
            s = masked_scores(k, q, block, first, count)
            top = jnp.max(s, axis=0, keepdims=True)
            p = jnp.exp2((s - top) * c)
            total = jnp.sum(p, axis=0, keepdims=True)
            ot = dot(vt_ref[64 * h : 64 * h + 64, 0 : count * ROWS], p.astype(BF16))
            ot = ot / total
            ot_ref[u] = ot
            lse_ref[u] = jnp.broadcast_to(top * c + jnp.log2(total), (8, ROWS))
            o_ref[block] = (o_ref[block].astype(F32) + padded(h, ot)).astype(BF16)
        if pair % 2:
            leave(pair // 2)


def attend_backward(half, qkv_ref, do_ref, ot_ref, lse_ref, out_ref, kt_ref, dk_ref, dv_ref, arrived, leave, beside):
    c = SCALE * LOG2E
    for b in range(BLOCKS):
        kt_ref[:, b * ROWS : (b + 1) * ROWS] = qkv_ref[b, :, 128:256].T
        out_ref[b, :, 0:128] = jnp.zeros((ROWS, 128), BF16)
    dk_ref[...] = jnp.zeros_like(dk_ref)
    dv_ref[...] = jnp.zeros_like(dv_ref)

    def one(h, i):
        h, block, count, first, u = unit_of(half, h, i)
        rows = count * ROWS
        q = qkv_ref[block, :, 0:128] * head_mask(h)
        do = do_ref[block] * head_mask(h)
        dot_rows = do.astype(F32).T[64 * h : 64 * h + 64]
        delta = jnp.sum(dot_rows * ot_ref[u], axis=0, keepdims=True)
        lse = lse_ref[u][0:1]
        k = qkv_ref[0:count, :, 128:256].reshape(rows, 128)
        v = qkv_ref[0:count, :, 256:384].reshape(rows, 128)
        s = masked_scores(k, q, block, first, count)
        p = jnp.exp2(s * c - lse)
        dp = dot(v, do, 1, 1)
        ds = (p * (dp - delta)).astype(BF16)
        dv_ref[0:rows] += dot(p.astype(BF16), do)
        dk_ref[0:rows] += dot(ds, q)
        dqt = dot(kt_ref[64 * h : 64 * h + 64, 0:rows], ds) * SCALE
        out_ref[block, :, 0:128] = (
            out_ref[block, :, 0:128].astype(F32) + padded(h, dqt)
        ).astype(BF16)

    for pair in reversed(range(BLOCKS // 2)):
        b = 2 * pair + 1
        arrived(b)
        arrived(b - 1)
        one(1, pair)
        for b in (b, b - 1):
            one(0, b)
            at = slice(b * ROWS, (b + 1) * ROWS)
            out_ref[b, :, 128:256] = (dk_ref[at] * SCALE).astype(BF16)
            out_ref[b, :, 256:384] = dv_ref[at].astype(BF16)
        beside(pair)
        if pair % 2 == 0:
            leave(pair // 2)


def choices(routes):
    ids = lax.broadcasted_iota(jnp.int32, (ROWS, EXPERTS), 1).astype(F32)
    e1, e2 = [jnp.broadcast_to(routes[k : k + 1].astype(F32), (8, ROWS)).T[:, 0:1] for k in range(2)]
    m1, m2 = (e1 == ids).astype(F32), (e2 == ids).astype(F32)
    r = lax.broadcasted_iota(jnp.int32, (ROWS, ROWS), 0)
    k = lax.broadcasted_iota(jnp.int32, (ROWS, ROWS), 1)
    lower = (k < r).astype(F32).astype(BF16)
    earlier = dot(lower, (m1 + m2).astype(BF16))
    s1 = jnp.sum(earlier * m1, axis=1, keepdims=True)
    s2 = jnp.sum(earlier * m2, axis=1, keepdims=True)

    return m1, m2, e1 * CAP + s1, e2 * CAP + s2


def chosen(col):
    at = lax.broadcasted_iota(jnp.int32, (ROWS, SLOTS), 1).astype(F32)
    return (at == col).astype(F32).astype(BF16)


def chosen_t(col):
    row = jnp.broadcast_to(col, (ROWS, 128)).T[0:1]
    at = lax.broadcasted_iota(jnp.int32, (SLOTS, ROWS), 0).astype(F32)
    return (at == row).astype(F32).astype(BF16)


def two_parts(v):
    lane = lax.broadcasted_iota(jnp.int32, (v.shape[0], EXTRA), 1)
    high = v.astype(BF16).astype(F32)
    return jnp.where(lane == 0, high, jnp.where(lane == 1, v - high, 0.0)).astype(BF16)


def from_parts(v):
    lane = lax.broadcasted_iota(jnp.int32, v.shape, 1)
    return jnp.sum(jnp.where(lane < 2, v.astype(F32), 0.0), axis=1, keepdims=True)


def deal_body(cot_ref, routes_ref, send_ref):
    _, _, c1, c2 = choices(routes_ref[...])
    either = chosen_t(c1) + chosen_t(c2)
    send_ref[...] = dot(either, cot_ref[...]).astype(BF16)


def middle_body(o_ref, tok_ref, w_o, gain_ref, gate_ref, routes_ref, mid_ref, att_ref, send_ref, gates_ref):
    tiles = unpair([o_ref[s].astype(F32) for s in range(BLOCKS)])
    o = jnp.concatenate([t.astype(BF16) for t in tiles], axis=1)
    att_ref[...] = o
    mid = tok_ref[...].astype(F32) + dot(o, w_o)
    mid_ref[...] = mid
    unit, _ = norm(mid)
    a2 = (unit * row_of(gain_ref)).astype(BF16)
    logits = dot(a2, gate_ref[...], 1, 1)
    m1, m2, c1, c2 = choices(routes_ref[...])
    l1 = jnp.sum(logits * m1, axis=1, keepdims=True)
    l2 = jnp.sum(logits * m2, axis=1, keepdims=True)
    top = jnp.maximum(l1, l2)
    x1, x2 = jnp.exp(l1 - top), jnp.exp(l2 - top)
    g1, g2 = x1 / (x1 + x2), x2 / (x1 + x2)
    lane = lax.broadcasted_iota(jnp.int32, (ROWS, 128), 1)
    gates_ref[...] = jnp.where(lane == 0, g1, g2)
    t1, t2 = chosen_t(c1), chosen_t(c2)
    send_ref[:, 0:D] = dot(t1 + t2, a2).astype(BF16)
    send_ref[:, D:] = (dot(t1, two_parts(g1)) + dot(t2, two_parts(g2))).astype(BF16)


def gelu_parts(h):
    t = pl.reciprocal(1.0 + (0.3275911 * 0.5**0.5) * jnp.abs(h), approx=True)
    e = jnp.exp2(h * h * (-0.5 * LOG2E))
    poly = t * (
        0.127414796
        + t * (-0.142248368 + t * (0.7107068705 + t * (-0.7265760135 + t * 0.5307027145)))
    )
    tail = poly * e
    phi = jnp.where(h >= 0, 1.0 - tail, tail)
    return h * phi, phi + h * e * (1.0 / math.sqrt(2.0 * math.pi))


def div(a, b):
    return lax.div(a, jnp.int32(b))


def rem(a, b):
    return lax.rem(a, jnp.int32(b))


def coords():
    return tuple(lax.axis_index(a) for a in ALL)


def near(x, pair):
    return x + rem(div(x, 2) + pair, 2) * (3 - 2 * x)


def neighbour(x):
    return x + 1 - 2 * rem(x, 2)


def expert_of(zh, x, zl, y):
    return 4 * (4 * zl + y) + 2 * div(x, 2) + zh


def remote(src, dst, send, recv, device):
    return pltpu.make_async_remote_copy(
        src_ref=src,
        dst_ref=dst,
        send_sem=send,
        recv_sem=recv,
        device_id=device,
        device_id_type=MESH,
    )


def await_bytes(ref, sem):
    pltpu.make_async_copy(ref, ref, sem).wait()


def chip_partner(me, k):
    zh, x, zl, y, c = me
    return (
        rem(zh + div(k, 8), 2),
        rem(x + rem(div(k, 2), 4), 4),
        zl,
        y,
        rem(c + rem(k, 2), 2),
    )


def core_partner(me, k):
    return me[:4] + (rem(me[4] + k, 2),)


def row_partner(me, k):
    zh, x, zl, y, c = me
    return (
        rem(zh + rem(div(k, 8), 2), 2),
        x + div(k, 16) * (3 - 2 * x),
        rem(zl + rem(div(k, 4), 2), 2),
        rem(y + rem(k, 4), 4),
        c,
    )


def head_partner(me, k):
    zh, x, zl, y, c = me
    t = rem(zh * 4 + x + k, 8)
    return t, (div(t, 4), rem(t, 4), zl, y, c)


def greet(me, partner, count):
    barrier = pltpu.get_barrier_semaphore()

    def one(k, carry):
        pl.semaphore_signal(
            barrier, inc=1, device_id=partner(me, k), device_id_type=MESH
        )
        return carry

    lax.fori_loop(1, count, one, 0)
    return count - 1


def hello(*groups):
    me = coords()
    return me, sum(greet(me, partner, count) for partner, count in groups)


def enter(total):
    pl.semaphore_wait(pltpu.get_barrier_semaphore(), total)


class HeadSwap:
    def __init__(self, me, send, recv, sems):
        self.me, self.send, self.recv, self.sems = me, send, recv, sems
        self.place = me[0] * 4 + me[1]

    def leave(self, half):
        s = self.place
        zh, x, zl, y, c = self.me
        for k in (2, 1, 3, 0):
            p = rem(x + k, 4)
            t = 4 * half + p
            away = remote(
                self.send.at[t], self.recv.at[s], self.sems.at[0, t], self.sems.at[1, s], (jnp.int32(half), p, zl, y, c)
            )
            if k:
                away.start()
            else:
                local = pltpu.make_async_copy(self.send.at[t], self.recv.at[t], self.sems.at[1, t])
                pl.when(zh == half)(local.start)
                pl.when(zh != half)(away.start)

    def start(self):
        s = self.place
        pltpu.make_async_copy(self.send.at[s], self.recv.at[s], self.sems.at[1, s]).start()
        for k in (2, 4, 6, 1, 3, 5, 7):
            t, device = head_partner(self.me, jnp.int32(k))
            remote(self.send.at[t], self.recv.at[s], self.sems.at[0, t], self.sems.at[1, s], device).start()

    def arrived(self, t):
        await_bytes(self.recv.at[t], self.sems.at[1, t])

    def wait_send(self):
        for k in range(1, 8):
            t, _ = head_partner(self.me, jnp.int32(k))
            await_bytes(self.send.at[t], self.sems.at[0, t])


class RowSwap:
    def __init__(self, me, send, recv, sems, back=False):
        self.me, self.send, self.recv, self.sems = me, send, recv, sems
        self.back = back

    def slot(self, kx, kz, ky):
        return 8 * rem(8 + ky - kz - 2 * kx, 4) + 4 * kx + kz

    def ends(self, k):
        zh, x, zl, y, c = self.me
        device = row_partner(self.me, k)
        kx, kz, ky = div(k, 16), rem(div(k, 4), 4), rem(k, 4)
        if self.back:
            src = self.slot(kx, kz, ky)
            dst = expert_of(zh, x, zl, y)
        else:
            src = expert_of(*device[:4])
            dst = self.slot(kx, kz, 4 - ky)
        rows = lambda n: pl.ds(pl.multiple_of(n * CAP, CAP), CAP)
        return self.send.at[rows(src)], self.recv.at[rows(dst)], device

    def start(self, first=0, last=32):
        if first == 0:
            src, dst, _ = self.ends(jnp.int32(0))
            pltpu.make_async_copy(src, dst, self.sems.at[1]).start()

        def one(k, carry):
            src, dst, device = self.ends(rem(9 * k, 32))
            remote(src, dst, self.sems.at[0], self.sems.at[1], device).start()
            return carry

        lax.fori_loop(max(first, 1), last, one, 0)

    def start_block(self, r):
        def one(n, carry):
            q = rem(3 * n, 8)
            kx, kz = div(q, 4), rem(q, 4)
            k = 16 * kx + 4 * kz + rem(r + kz + 2 * kx, 4)
            src, dst, device = self.ends(k)
            local = pltpu.make_async_copy(src, dst, self.sems.at[1])
            away = remote(src, dst, self.sems.at[0], self.sems.at[1], device)
            pl.when(k == 0)(local.start)
            pl.when(k != 0)(away.start)
            return carry

        lax.fori_loop(0, 8, one, 0)

    def wait_recv(self):
        await_bytes(self.recv, self.sems.at[1])

    def wait_send(self, first=0, last=31):
        await_bytes(self.send.at[pl.ds(0, (last - first) * CAP)], self.sems.at[0])

    def wait(self):
        self.wait_recv()
        self.wait_send()


def remote_params(n, mb=60):
    return pltpu.CompilerParams(
        vmem_limit_bytes=mb * 2**20, collective_id=n, has_side_effects=True
    )


VMEM = pl.BlockSpec(memory_space=pltpu.VMEM)
ANY = pl.BlockSpec(memory_space=pl.ANY)
DMA = pltpu.SemaphoreType.DMA


class Weights:
    def __init__(self, me, w_in, w_out, full_in, full_out, sems):
        self.me, self.refs, self.full, self.sems = me, (w_in, w_out), (full_in, full_out), sems

    def place(self, i, x, zh):
        at = pl.ds(pl.multiple_of(zh * 384, 128), 384)
        return self.full[0].at[x, :, at] if i == 0 else self.full[1].at[x, at, :]

    def first(self, i, b):
        zh, x, zl, y, c = self.me
        device = (jnp.int32(b), near(x, c), zl, y, zh)
        copy = remote(
            self.refs[i].at[b], self.place(i, x, zh), self.sems.at[0, i, b], self.sems.at[1, i, x], device
        )
        local = pltpu.make_async_copy(
            self.refs[i].at[b], self.place(i, x, zh), self.sems.at[1, i, x]
        )
        own = jnp.logical_and(
            jnp.logical_and(zh == b, div(x, 2) == c), zh == c
        )
        return copy, local, own

    def start(self, i):
        for b in range(2):
            copy, local, own = self.first(i, b)
            pl.when(own)(local.start)
            pl.when(jnp.logical_not(own))(copy.start)

    def forward(self, i, x, step):
        zh, me_x, zl, y, c = self.me
        piece = self.place(i, x, c)
        device = (zh, neighbour(me_x), zl, y, c) if step == 2 else (zh, me_x, zl, y, 1 - c)
        return remote(piece, piece, self.sems.at[2 * step - 2, i, x], self.sems.at[2 * step - 1, i, x], device)

    def sources(self, step):
        x = self.me[1]
        if step == 1:
            return x, 3 - x
        return neighbour(x), 3 - neighbour(x)

    def second(self, i):
        for x in self.sources(1):
            await_bytes(self.place(i, x, self.me[4]), self.sems.at[1, i, x])
            self.forward(i, x, 2).start()
            self.forward(i, x, 3).start()

    def third(self, i):
        for x in self.sources(2):
            self.forward(i, x, 2).wait_recv()
            self.forward(i, x, 3).start()

    def ready(self, i):
        for x in range(4):
            self.forward(i, jnp.int32(x), 3).wait_recv()

    def finish(self, i):
        for b in range(2):
            copy, _, own = self.first(i, b)
            pl.when(jnp.logical_not(own))(copy.wait_send)
        for x in self.sources(1):
            self.forward(i, x, 2).wait_send()
        for x in range(4):
            self.forward(i, jnp.int32(x), 3).wait_send()


STEP = 256
CHUNKS = 4
TILES = SLOTS // STEP


def row_block(r):
    return pl.ds(pl.multiple_of(r * STEP, STEP), STEP)


def half_rows(n):
    return pl.ds(pl.multiple_of(n * 384, 128), 384)


def front_body(tok_ref, cot_ref, gain1_ref, w_qkv_ref, w_o_ref, gain2_ref, gate_ref, routes_ref, w_in_ref, w_out_ref,
               qkv_out, ret_ref, y_ref, mid_out, att_out, gates_out, ot_out, lse_out, dwin_out, total_out,
               qkv_ref, mid_ref, att_ref, gates_ref, ot_ref, lse_ref, total_ref, xt_ref,
               qkv_send, o_send, o_recv, x_send, c_send, x_ref, c_ref, vt_ref, full_in, full_out, g_ref, d_ref,
               part_in, part_out, got_in, got_out, got2,
               head_sems, row_sems, weight_sems, load_sems, save_sems, core_sems, pair_sems):
    loads = [
        pltpu.make_async_copy(w_qkv_ref.at[:, p * D : p * D + D], g_ref.at[p, 0:D], load_sems.at[p]) for p in range(3)
    ] + [pltpu.make_async_copy(w_o_ref, g_ref.at[3, 0:D], load_sems.at[3])]
    for load in loads:
        load.start()
    me, greeted = hello((chip_partner, 16), (row_partner, 32))
    zh, x, zl, y, c = me
    weights = Weights(me, w_in_ref, w_out_ref, full_in, full_out, weight_sems)
    heads = HeadSwap(me, qkv_send, qkv_ref, head_sems.at[0])
    heads_back = HeadSwap(me, o_send, o_recv, head_sems.at[1])
    rows_c = RowSwap(me, c_send, c_ref, row_sems.at[0])
    rows_x = RowSwap(me, x_send, x_ref, row_sems.at[1])
    rows_ret = RowSwap(me, x_send, ret_ref, row_sems.at[2], back=True)
    rows_y = RowSwap(me, c_send, y_ref, row_sems.at[3], back=True)

    def part_weights(p):
        loads[p].wait()
        return g_ref[p, 0:D, :]

    project(tok_ref, gain1_ref, part_weights, qkv_send)
    enter(greeted)
    heads.start()
    weights.start(0)
    deal_body(cot_ref, routes_ref, c_send)
    heads.arrived(0)
    heads.arrived(1)
    weights.start(1)
    attend_forward(
        rem(x, 2), qkv_ref, o_send, ot_ref, lse_ref, vt_ref,
        lambda b: heads.arrived(b) if b > 1 else None, heads_back.leave,
    )
    weights.second(0)
    for t in range(BLOCKS):
        heads_back.arrived(t)
    loads[3].wait()
    middle_body(o_recv, tok_ref, g_ref[3, 0:D, :], gain2_ref, gate_ref, routes_ref, mid_ref, att_ref, x_send, gates_ref)
    rows_x.start()
    saves = [
        pltpu.make_async_copy(src, dst, save_sems.at[n])
        for n, (src, dst) in enumerate(
            ((qkv_ref, qkv_out), (mid_ref, mid_out), (att_ref, att_out), (gates_ref, gates_out), (ot_ref, ot_out), (lse_ref, lse_out))
        )
    ]
    for save in saves:
        save.start()
    weights.second(1)
    weights.third(0)
    rows_x.wait_send(0, 22)
    rows_c.start()
    weights.ready(0)
    rows_x.wait_recv()
    rows_x.wait_send(22, 31)

    def hidden(j):
        tiles = [slice(r * STEP, r * STEP + STEP) for r in range(TILES)]
        w = full_in[j]

        def after(at, h):
            g, d = gelu_parts(h)
            g_ref[j, at, :] = g.astype(BF16)
            d_ref[j, at, :] = d.astype(BF16)

        before = dot(x_ref[tiles[0], 0:D], w)
        for r in range(1, TILES):
            h = dot(x_ref[tiles[r], 0:D], w)
            after(tiles[r - 1], before)
            before = h
        after(tiles[-1], before)

    def hidden_loop(j, carry):
        @pl.when(j == CHUNKS - 1)
        def _():
            weights.third(1)

        hidden(j)
        return carry

    lax.fori_loop(0, CHUNKS, hidden_loop, 0)
    for r in range(TILES):
        xt_ref[:, r * STEP : (r + 1) * STEP] = x_ref[r * STEP : (r + 1) * STEP, 0:D].T
    weights.ready(1)
    rows_c.wait()

    def produce(n, carry):
        r = TILES - 1 - n
        at = row_block(r)
        c_ref[at, :] = (c_ref[at, :].astype(F32) * from_parts(x_ref[at, D:])).astype(BF16)
        out = dot(g_ref[0, at, :], full_out[0])
        for j in range(1, CHUNKS):
            out = out + dot(g_ref[j, at, :], full_out[j])
        c_send[at, :] = out.astype(BF16)
        rows_y.start_block(r)
        return carry

    lax.fori_loop(0, TILES, produce, 0)

    sibling = core_partner(me, 1)

    def half(i, j, n):
        return part_in.at[j, :, half_rows(n)] if i == 0 else part_out.at[j, half_rows(n), :]

    def over(i, j):
        got = (got_in, got_out)[i]
        return remote(half(i, j, 1 - c), got.at[j], core_sems.at[0, i, j], core_sems.at[1, i, j], sibling)

    def second_grad(j, carry):
        part_out[j] = dot(g_ref[j], c_ref[...], 0, 0).astype(BF16)
        over(1, j).start()
        return carry

    lax.fori_loop(0, CHUNKS, second_grad, 0)

    def second_sum(j, carry):
        over(1, j).wait()
        got_out[j] = (half(1, j, c)[...].astype(F32) + got_out[j].astype(F32)).astype(BF16)
        return carry

    lax.fori_loop(0, CHUNKS, second_sum, 0)
    pass_on, keep = (neighbour(x), 3 - neighbour(x)), (x, 3 - x)

    def pair_over(n):
        return remote(got_out.at[pass_on[n]], got2.at[n], pair_sems.at[0, n], pair_sems.at[1, n], (zh, neighbour(x), zl, y, c))

    for n in range(2):
        pair_over(n).start()

    def back(n, carry):
        r = TILES - 1 - n
        at = row_block(r)
        total = jnp.zeros((STEP, 128), F32)
        dx = jnp.zeros((STEP, D), F32)
        for j in range(CHUNKS):
            cw = dot(c_ref[at, :], full_out[j], 1, 1)
            dh = (d_ref[j, at, :].astype(F32) * cw).astype(BF16)
            prod = g_ref[j, at, :].astype(F32) * cw
            for t in range(D // 128):
                total = total + prod[:, 128 * t : 128 * t + 128]
            d_ref[j, at, :] = dh
            dx = dx + dot(dh, full_in[j], 1, 1)
        x_send[at, 0:D] = dx.astype(BF16)
        x_send[at, D:] = two_parts(jnp.sum(total, axis=1, keepdims=True))
        rows_ret.start_block(r)
        return carry

    lax.fori_loop(0, TILES, back, 0)

    def first_grad(n, carry):
        j, r = div(n, 3), rem(n, 3)
        part_in[j, row_block(r), :] = dot(xt_ref[row_block(r), :], d_ref[j]).astype(BF16)

        @pl.when(r == 2)
        def _():
            over(0, j).start()

        return carry

    lax.fori_loop(0, 3 * CHUNKS, first_grad, 0)

    def first_save(j):
        return pltpu.make_async_copy(got_in.at[j], dwin_out.at[j], save_sems.at[7])

    def first_sum(j, carry):
        over(0, j).wait()
        got_in[j] = (half(0, j, c)[...].astype(F32) + got_in[j].astype(F32)).astype(BF16)
        first_save(j).start()
        return carry

    lax.fori_loop(0, CHUNKS, first_sum, 0)
    heads.wait_send()
    heads_back.wait_send()
    weights.finish(0)
    weights.finish(1)
    for n in range(2):
        pair_over(n).wait()
        total_ref[n] = (got_out[keep[n]].astype(F32) + got2[n].astype(F32)).astype(BF16)
    last = pltpu.make_async_copy(total_ref, total_out, save_sems.at[6])
    last.start()
    for save in saves:
        save.wait()
    rows_y.wait()
    rows_ret.wait()
    last.wait()
    await_bytes(dwin_out, save_sems.at[7])


def front(tok, cot, gain1, w_qkv, w_o, gain2, gate, routes, w_in, w_out):
    buf = lambda *s: pltpu.VMEM(s, BF16)
    f32 = lambda *s: pltpu.VMEM(s, F32)
    outs = [
        ((BLOCKS, ROWS, 384), BF16),
        ((SLOTS, D + EXTRA), BF16),
        ((SLOTS, D), BF16),
        ((ROWS, D), F32),
        ((ROWS, D), BF16),
        ((ROWS, 128), F32),
        ((12, 64, ROWS), F32),
        ((12, 8, ROWS), F32),
        ((CHUNKS, D, 384), BF16),
        ((2, 384, D), BF16),
    ]
    return pl.pallas_call(
        front_body,
        out_shape=[jax.ShapeDtypeStruct(s, t) for s, t in outs],
        in_specs=[VMEM] * 3 + [ANY] * 2 + [VMEM] * 3 + [ANY] * 2,
        out_specs=[ANY] * len(outs),
        scratch_shapes=[
            buf(BLOCKS, ROWS, 384),
            f32(ROWS, D),
            buf(ROWS, D),
            f32(ROWS, 128),
            f32(12, 64, ROWS),
            f32(12, 8, ROWS),
            buf(2, 384, D),
            buf(D, SLOTS),
            buf(BLOCKS, ROWS, 384),
            buf(BLOCKS, ROWS, 128),
            buf(BLOCKS, ROWS, 128),
            buf(SLOTS, D + EXTRA),
            buf(SLOTS, D),
            buf(SLOTS, D + EXTRA),
            buf(SLOTS, D),
            buf(128, BLOCKS * ROWS),
            buf(CHUNKS, D, D),
            buf(CHUNKS, D, D),
            buf(CHUNKS, SLOTS, D),
            buf(CHUNKS, SLOTS, D),
            buf(CHUNKS, D, D),
            buf(CHUNKS, D, D),
            buf(CHUNKS, D, 384),
            buf(CHUNKS, 384, D),
            buf(2, 384, D),
            DMA((2, 2, 8)),
            DMA((4, 2)),
            DMA((6, 2, 4)),
            DMA((4,)),
            DMA((8,)),
            DMA((2, 2, 4)),
            DMA((2, 2)),
        ],
        compiler_params=remote_params(0, 63),
    )(tok, cot, gain1, w_qkv, w_o, gain2, gate, routes, w_in, w_out)


def back_body(ret_ref, cot_ref, routes_ref, gates_ref, mid_ref, gain_ref, gate_w_ref, w_o_ref,
              send_ref, dmid_ref, gate_grad_ref, gain_grad_ref):
    m1, m2, c1, c2 = choices(routes_ref[...])
    s1, s2 = chosen(c1), chosen(c2)
    g1, g2 = gates_ref[:, 0:1], gates_ref[:, 1:2]
    extra = ret_ref[:, D:]
    d1, d2 = from_parts(dot(s1, extra)), from_parts(dot(s2, extra))
    dl = g2 * d1 - g1 * d2
    dlogits = (m1 - m2) * dl
    unit, inv = norm(mid_ref[...])
    high = dlogits.astype(BF16)
    low = (dlogits - high.astype(F32)).astype(BF16)
    gate_w = gate_w_ref[...]
    da2 = dot(s1 + s2, ret_ref[:, 0:D]) + dot(high, gate_w) + dot(low, gate_w)
    dmid = cot_ref[...].astype(F32) + norm_back(da2, row_of(gain_ref), unit, inv)
    dmid_ref[...] = dmid
    do = dot(dmid.astype(BF16), w_o_ref[...], 1, 1)
    for s in range(BLOCKS):
        send_ref[s] = pair_up(do, s).astype(BF16)

    def later():
        a2 = (unit * row_of(gain_ref)).astype(BF16)
        gate_grad_ref[...] = dot(high, a2, 0, 0) + dot(low, a2, 0, 0)
        gain_grad_ref[...] = jnp.sum(da2 * unit, axis=0, keepdims=True)

    return later


def axis_place(me, a):
    zh, x, zl, y, c = me
    return (x, y, 2 * zh + zl)[a]


def axis_peer(me, a, k):
    zh, x, zl, y, c = me
    p = rem(axis_place(me, a) + k, 4)
    if a == 0:
        return p, (zh, p, zl, y, c)
    if a == 1:
        return p, (zh, x, zl, p, c)
    return p, (div(p, 2), x, rem(p, 2), y, c)


def axis_partner(me, k):
    zh, x, zl, y, c = me
    along_z = div(k, 4)
    dz = rem(k + 1, 4) * along_z
    z = rem(2 * zh + zl + dz, 4)
    return div(z, 2), x, rem(z, 2), rem(y + k * (1 - along_z), 4), c


def multiple(n, w):
    return pl.ds(pl.multiple_of(n * w, w), w)


PEERS = (1, 2, 3)


class GroupSum:
    def __init__(self, me, g, axes, out, bufs, sems):
        self.me, self.g, self.axes, self.out, self.sems = me, g, axes, out, sems.at[g]
        self.s0, self.r0, self.a0, self.r1, self.a1, self.s2, self.r2, self.r3, self.whole = [b.at[g] for b in bufs]
        self.place = [axis_place(me, a) for a in axes]
        self.c = me[4]

    def copy(self, stage, k, src, dst):
        if stage in (0, 6):
            device = core_partner(self.me, 1)
        else:
            device = axis_peer(self.me, self.axes[(0, 0, 1, 2, 1, 0)[stage]], jnp.int32(k))[1]
        return remote(src, dst, self.sems.at[stage, 0, k], self.sems.at[stage, 1, k], device)

    def peer(self, t, k):
        return axis_peer(self.me, self.axes[t], jnp.int32(k))[0]

    def swap(self):
        return self.copy(0, 0, self.s0, self.r0)

    def scatter1(self, k):
        return self.copy(1, k, self.s0.at[multiple(self.peer(0, k), 192)], self.r1.at[k - 1])

    def scatter2(self, k):
        return self.copy(2, k, self.s2.at[multiple(self.peer(1, k), 48)], self.r2.at[k - 1])

    def share(self, k):
        mine = self.r3.at[self.place[2]]
        return self.copy(3, k, mine, mine)

    def block(self, rows):
        i, j = self.place[0], self.place[1]
        if rows == 48:
            return self.whole.at[multiple(4 * i + j, 48)]
        if rows == 192:
            return self.whole.at[multiple(i, 192)]
        return self.whole

    def gather(self, stage, k):
        ref = self.block((48, 192, 768)[stage - 4])
        if stage < 6:
            return self.copy(stage, k, ref, ref)
        lanes = pl.ds(pl.multiple_of(self.g * D + self.c * 384, 128), 384)
        return self.copy(stage, k, ref, self.out.at[:, lanes])

    def save(self):
        lanes = pl.ds(pl.multiple_of(self.g * D + self.c * 384, 128), 384)
        return pltpu.make_async_copy(self.whole, self.out.at[:, lanes], self.sems.at[6, 0, 1])

    def begin(self, grad):
        self.s0[...] = grad(1 - self.c).astype(BF16)
        self.swap().start()
        self.a0[...] = grad(self.c)

    def step1(self):
        self.swap().wait()
        self.a0[...] += self.r0[...].astype(F32)
        self.s0[...] = self.a0[...].astype(BF16)
        for k in PEERS:
            self.scatter1(k).start()

    def step2(self):
        for k in PEERS:
            self.scatter1(k).wait_recv()
        mine = self.a0[multiple(self.place[0], 192), :]
        for k in PEERS:
            mine = mine + self.r1[k - 1].astype(F32)
        self.a1[...] = mine
        self.s2[...] = mine.astype(BF16)
        for k in PEERS:
            self.scatter2(k).start()

    def step3(self):
        for k in PEERS:
            self.scatter2(k).wait_recv()
        mine = self.a1[multiple(self.place[1], 48), :]
        for k in PEERS:
            mine = mine + self.r2[k - 1].astype(F32)
        self.r3[self.place[2]] = mine.astype(BF16)
        for k in PEERS:
            self.share(k).start()

    def step4(self):
        for k in PEERS:
            p = axis_peer(self.me, self.axes[2], jnp.int32(k))[0]
            self.copy(3, 4 - k, self.r3.at[p], self.r3.at[p]).wait_recv()
        total = (self.r3[0].astype(F32) + self.r3[1].astype(F32)) + (
            self.r3[2].astype(F32) + self.r3[3].astype(F32)
        )
        self.block(48)[...] = total.astype(BF16)
        for k in PEERS:
            self.gather(4, k).start()

    def step5(self):
        for k in PEERS:
            self.gather(4, k).wait_recv()
        for k in PEERS:
            self.gather(5, k).start()

    def step6(self):
        for k in PEERS:
            self.gather(5, k).wait_recv()
        self.gather(6, 0).start()
        self.save().start()

    def finish(self):
        self.gather(6, 0).wait()
        self.save().wait()
        for k in PEERS:
            self.scatter1(k).wait_send()
            self.scatter2(k).wait_send()
            self.share(k).wait_send()
            self.gather(4, k).wait_send()
            self.gather(5, k).wait_send()


class SmallSum:
    def __init__(self, me, mine, over, slots, out, sems):
        self.me, self.mine, self.over, self.slots, self.out, self.sems = me, mine, over, slots, out, sems

    def half(self, ref, n):
        return ref.at[:, half_rows(n)]

    def swap(self):
        return remote(self.over.at[0], self.over.at[1], self.sems.at[0, 0], self.sems.at[1, 0], core_partner(self.me, 1))

    def share(self, a, k):
        n = 3 * a + k
        mine = self.slots.at[a, axis_place(self.me, a)]
        return remote(mine, mine, self.sems.at[0, n], self.sems.at[1, n], axis_peer(self.me, a, jnp.int32(k))[1])

    def join(self):
        mine = self.half(self.out, self.me[4])
        return remote(mine, mine, self.sems.at[0, 10], self.sems.at[1, 10], core_partner(self.me, 1))

    def begin(self):
        self.over[0] = self.half(self.mine, 1 - self.me[4])[...].astype(BF16)
        self.swap().start()

    def step(self, a):
        if a == 0:
            self.swap().wait_recv()
            total = self.half(self.mine, self.me[4])[...] + self.over[1].astype(F32)
        else:
            for k in PEERS:
                self.share(a - 1, k).wait_recv()
            s = [self.slots[a - 1, p].astype(F32) for p in range(4)]
            total = (s[0] + s[1]) + (s[2] + s[3])
        if a < 3:
            self.slots[a, axis_place(self.me, a)] = total.astype(BF16)
            for k in PEERS:
                self.share(a, k).start()
        else:
            self.half(self.out, self.me[4])[...] = total.astype(BF16)
            self.join().start()

    def finish(self):
        self.join().wait()
        self.swap().wait_send()
        for a in range(3):
            for k in PEERS:
                self.share(a, k).wait_send()


class Collect:
    def __init__(self, me, dw, kept, got, total, fin, sems):
        self.me, self.dw, self.kept, self.got, self.fin, self.sems = me, dw, kept, got, fin, sems
        x = me[1]
        self.totals = (got, total)
        self.keep, self.pass_on = (x, 3 - x), (neighbour(x), 3 - neighbour(x))

    def second(self, j, at=slice(None)):
        zh, x, zl, y, c = self.me
        return remote(self.dw.at[self.pass_on[j], at], self.got.at[j, at], self.sems.at[0, 0, j], self.sems.at[1, 0, j],
                      (zh, neighbour(x), zl, y, c))

    def quarters(self, j):
        return [self.second(j, slice(192 * q, 192 * q + 192)) for q in range(4)]

    def third(self, i, j, n=None):
        zh, x, zl, y, c = self.me
        pair = div(x, 2)
        size = (D, 384)[i] // 2
        at = slice(None) if n is None else slice(n * size, n * size + size)
        src, dst = self.totals[i].at[j, at], self.fin[i].at[zh, at]
        copy = remote(src, dst, self.sems.at[2, i, j], self.sems.at[3, i, zh], (c, self.keep[j], zl, y, pair))
        local = pltpu.make_async_copy(src, dst, self.sems.at[3, i, zh])
        if j == 1:
            return copy, None, None
        return copy, local, jnp.logical_and(zh == c, pair == c)

    def load(self, j, sem):
        return pltpu.make_async_copy(self.dw.at[self.keep[j]], self.kept.at[j], sem)

    def add(self, j):
        self.second(j).wait_recv()
        self.got[j] = (self.kept[j].astype(F32) + self.got[j].astype(F32)).astype(BF16)

    def send(self, i, j, parts=(0, 1)):
        for n in parts:
            copy, local, own = self.third(i, j, n)
            if j == 1:
                copy.start()
            else:
                pl.when(own)(local.start)
                pl.when(jnp.logical_not(own))(copy.start)

    def finish(self):
        for j in range(2):
            self.second(j).wait_send()
        for i in range(2):
            for j in range(2):
                copy, _, own = self.third(i, j)
                if j == 1:
                    copy.wait_send()
                else:
                    pl.when(jnp.logical_not(own))(copy.wait_send)
            for b in range(2):
                await_bytes(self.fin[i].at[b], self.sems.at[3, i, b])


def rear_body(cot_ref, routes_ref, gain2_ref, gate_w_ref, tok_ref, gain1_ref,
              ret_in, gates_in, mid_in, att_in, w_o_in, qkv_in, ot_in, lse_in, w_qkv_in, y_in, dw_ref, total_ref,
              tok_grad_out, grads_out, early_ref, late_ref, out_out, fin_in, fin_out,
              ret_ref, gates_ref, mid_ref, att_ref, w_o_ref, qkv_ref, ot_ref, lse_ref, w_qkv_ref, y_ref, kept, out_ref, tok_grad_ref,
              dmid_ref, do_send, do_recv, dqkv_send, dqkv_recv, kt_ref, dk_ref, dv_ref, d_ref, datt_ref, got,
              s0, r0, a0, r1, a1, s2, r2, r3, whole, early, early_over, early_slots, late, late_over, late_slots,
              load_sems, save_sems, head_sems, collect_sems, group_sems, small_sems):
    me = coords()
    collect = Collect(me, dw_ref, kept, got, total_ref, (fin_in, fin_out), collect_sems)
    pairs = (
        (ret_in, ret_ref), (mid_in, mid_ref), (gates_in, gates_ref), (w_o_in, w_o_ref), (att_in, att_ref), (y_in, y_ref),
        (qkv_in, qkv_ref), (ot_in, ot_ref), (lse_in, lse_ref), (w_qkv_in, w_qkv_ref),
    )
    loads = [pltpu.make_async_copy(src, dst, load_sems.at[n]) for n, (src, dst) in enumerate(pairs)]
    loads += [collect.load(j, load_sems.at[10 + j]) for j in range(2)]
    for load in loads:
        load.start()
    _, greeted = hello((chip_partner, 16), (axis_partner, 7))
    heads = HeadSwap(me, do_send, do_recv, head_sems.at[0])
    heads_back = HeadSwap(me, dqkv_send, dqkv_recv, head_sems.at[1])
    bufs = (s0, r0, a0, r1, a1, s2, r2, r3, whole)
    orders = ((0, 1, 2), (1, 2, 0), (2, 0, 1), (1, 0, 2))
    groups = [GroupSum(me, g, orders[g], grads_out, bufs, group_sems) for g in range(4)]
    qkv_groups, o_group = groups[:3], groups[3]
    small = SmallSum(me, early, early_over, early_slots, early_ref, small_sems.at[0])
    small_late = SmallSum(me, late, late_over, late_slots, late_ref, small_sems.at[1])
    early[...] = jnp.zeros_like(early)
    late[...] = jnp.zeros_like(late)
    parts = [copy.start for j in range(2) for copy in collect.quarters(j)]

    def pump(n):
        for _ in range(min(n, len(parts))):
            parts.pop(0)()

    for load in loads[:4]:
        load.wait()
    enter(greeted)
    pump(2)
    collect.send(1, 0)
    later = back_body(ret_ref, cot_ref, routes_ref, gates_ref, mid_ref, gain2_ref, gate_w_ref, w_o_ref,
                      do_send, dmid_ref, early.at[0:32], early.at[32:33])
    heads.start()
    later()
    small.begin()
    datt_ref[...] = dmid_ref[...].astype(BF16)
    for load in loads[4:]:
        load.wait()
    o_group.begin(lambda n: dot(att_ref[...], datt_ref[:, half_rows(n)], 0, 0))
    _, _, c1, c2 = choices(routes_ref[...])
    rows = y_ref[...]
    mix = gates_ref[:, 0:1] * dot(chosen(c1), rows) + gates_ref[:, 1:2] * dot(chosen(c2), rows)
    out_ref[...] = (mid_ref[...] + mix).astype(BF16)
    saves = [pltpu.make_async_copy(out_ref, out_out, save_sems.at[0]), pltpu.make_async_copy(tok_grad_ref, tok_grad_out, save_sems.at[1])]
    saves[0].start()
    for t in range(BLOCKS):
        heads.arrived(t)
    small.step(0)
    o_group.step1()
    collect.send(1, 1)
    pump(2)

    attend_backward(rem(me[1], 2), qkv_ref, do_recv, ot_ref, lse_ref, dqkv_send, kt_ref, dk_ref, dv_ref,
                    lambda b: None, heads_back.leave, lambda pair: None)
    small.step(1)
    o_group.step2()
    pump(4)
    collect.add(0)
    collect.send(0, 0)
    unit, inv = norm(tok_ref[...].astype(F32))
    a1_rows = (unit * row_of(gain1_ref)).astype(BF16)
    for t in range(BLOCKS):
        heads_back.arrived(t)
    for part in range(3):
        tiles = unpair(
            [dqkv_recv[s, :, part * 128 : part * 128 + 128].astype(F32) for s in range(BLOCKS)]
        )
        for t in range(6):
            d_ref[part, :, 128 * t : 128 * t + 128] = tiles[t].astype(BF16)
        qkv_groups[part].begin(lambda n: dot(a1_rows, d_ref[part, :, half_rows(n)], 0, 0))
        if part:
            qkv_groups[part - 1].step1()
    small.step(2)
    o_group.step3()
    qkv_groups[2].step1()
    da1 = dot(d_ref[0], w_qkv_ref[:, 0:D], 1, 1)
    for part in (1, 2):
        da1 = da1 + dot(d_ref[part], w_qkv_ref[:, part * D : part * D + D], 1, 1)
    late[0:1] = jnp.sum(da1 * unit, axis=0, keepdims=True)
    small_late.begin()
    tok_grad_ref[...] = dmid_ref[...] + norm_back(da1, row_of(gain1_ref), unit, inv)
    saves[1].start()
    small.step(3)
    o_group.step4()
    small_late.step(0)
    for g in qkv_groups:
        g.step2()
    small_late.step(1)
    for g in qkv_groups:
        g.step3()
    collect.add(1)
    o_group.step5()
    small_late.step(2)
    for g in qkv_groups:
        g.step4()
    small_late.step(3)
    for g in qkv_groups:
        g.step5()
    collect.send(0, 1)
    o_group.step6()
    for g in qkv_groups:
        g.step6()
    small.finish()
    small_late.finish()
    heads.wait_send()
    heads_back.wait_send()
    collect.finish()
    for g in groups:
        g.finish()
    for save in saves:
        save.wait()


def rear(*args):
    buf = lambda *s: pltpu.VMEM(s, BF16)
    f32 = lambda *s: pltpu.VMEM(s, F32)
    return pl.pallas_call(
        rear_body,
        out_shape=[
            jax.ShapeDtypeStruct((ROWS, D), F32),
            jax.ShapeDtypeStruct((D, 4 * D), BF16),
            jax.ShapeDtypeStruct((48, D), BF16),
            jax.ShapeDtypeStruct((16, D), BF16),
            jax.ShapeDtypeStruct((ROWS, D), BF16),
            jax.ShapeDtypeStruct((2, D, 384), BF16),
            jax.ShapeDtypeStruct((2, 384, D), BF16),
        ],
        in_specs=[VMEM] * 6 + [ANY] * 12,
        out_specs=[ANY, ANY, VMEM, VMEM, ANY, ANY, ANY],
        scratch_shapes=[
            buf(SLOTS, D + EXTRA),
            f32(ROWS, 128),
            f32(ROWS, D),
            buf(ROWS, D),
            buf(D, D),
            buf(BLOCKS, ROWS, 384),
            f32(12, 64, ROWS),
            f32(12, 8, ROWS),
            buf(D, 3 * D),
            buf(SLOTS, D),
            buf(2, D, 384),
            buf(ROWS, D),
            f32(ROWS, D),
            f32(ROWS, D),
            buf(BLOCKS, ROWS, 128),
            buf(BLOCKS, ROWS, 128),
            buf(BLOCKS, ROWS, 384),
            buf(BLOCKS, ROWS, 384),
            buf(128, BLOCKS * ROWS),
            f32(BLOCKS * ROWS, 128),
            f32(BLOCKS * ROWS, 128),
            buf(3, ROWS, D),
            buf(ROWS, D),
            buf(2, D, 384),
            buf(4, D, 384),
            buf(4, D, 384),
            f32(4, D, 384),
            buf(4, 3, 192, 384),
            f32(4, 192, 384),
            buf(4, 192, 384),
            buf(4, 3, 48, 384),
            buf(4, 4, 48, 384),
            buf(4, D, 384),
            f32(48, D),
            buf(2, 48, 384),
            buf(3, 4, 48, 384),
            f32(16, D),
            buf(2, 16, 384),
            buf(3, 4, 16, 384),
            DMA((12,)),
            DMA((2,)),
            DMA((2, 2, 8)),
            DMA((4, 2, 2)),
            DMA((4, 7, 2, 4)),
            DMA((2, 2, 11)),
        ],
        compiler_params=remote_params(2),
    )(*args)


PIECES = 8


def results_body(frozen_ref, grads_ref, win_ref, wout_ref, tok_ref, out_ref, early_ref, late_ref,
                 qkv_grad, o_grad, win_grad, wout_grad, tok_grad, out, gain1_grad, gain2_grad, gate_grad):
    expert = (lax.axis_index("zl") * 4 + lax.axis_index("y")) * 4 + lax.axis_index("c") * 2
    qkv_grad[...] = grads_ref[:, : 3 * D].astype(F32)
    o_grad[...] = grads_ref[:, 3 * D :].astype(F32)
    for b in range(2):
        keep = (1 - frozen_ref[expert + b]).astype(F32)
        win_grad[b] = win_ref[b].astype(F32) * keep
        wout_grad[b] = wout_ref[b].astype(F32) * keep
    tok_grad[...] = tok_ref[...]
    out[...] = out_ref[...]

    @pl.when(pl.program_id(0) == 0)
    def _():
        gain1_grad[...] = late_ref[0:1].astype(F32).reshape(D)
        gain2_grad[...] = early_ref[32:33].astype(F32).reshape(D)
        gate = early_ref[0:32].astype(F32)
        for k in range(EXPERTS):
            gate_grad[k : k + 1] = gate[k : k + 1] * (1 - frozen_ref[k]).astype(F32)


def results(frozen, *args):
    n = PIECES
    whole = lambda *s: pl.BlockSpec(s, lambda i: (0,) * len(s))
    rows = lambda a, b: pl.BlockSpec((a // n, b), lambda i: (i, 0))
    slices = lambda a, b: pl.BlockSpec((2, a // n, b), lambda i: (0, i, 0))
    outs = [
        ((D, 3 * D), F32, rows(D, 3 * D)),
        ((D, D), F32, rows(D, D)),
        ((2, D, 384), F32, slices(D, 384)),
        ((2, 384, D), F32, slices(384, D)),
        ((ROWS, D), F32, rows(ROWS, D)),
        ((ROWS, D), BF16, rows(ROWS, D)),
        ((D,), F32, whole(D)),
        ((D,), F32, whole(D)),
        ((EXPERTS, D), F32, whole(EXPERTS, D)),
    ]
    return pl.pallas_call(
        results_body,
        grid=(n,),
        out_shape=[jax.ShapeDtypeStruct(s, t) for s, t, _ in outs],
        in_specs=[
            pl.BlockSpec(memory_space=pltpu.SMEM),
            rows(D, 4 * D),
            slices(D, 384),
            slices(384, D),
            rows(ROWS, D),
            rows(ROWS, D),
            whole(48, D),
            whole(16, D),
        ],
        out_specs=[m for _, _, m in outs],
        compiler_params=params(60),
    )(frozen, *args)


def on_device(tokens, cotangent, gain_first, w_qkv, w_o, gain_second, w_gate, w_in, w_out, routes, frozen):
    tok, cot, routes, gate_t = tokens[0], cotangent[0], routes[0].T, w_gate.T
    qkv, ret, y, mid, att, gates, ot, lse, dw_in, total_out = front(
        tok, cot, gain_first, w_qkv, w_o, gain_second, gate_t, routes, w_in, w_out
    )
    tok_grad, grads, early, late, out, w_in_grad, w_out_grad = rear(
        cot, routes, gain_second, gate_t, tok, gain_first, ret, gates, mid, att, w_o, qkv, ot, lse, w_qkv, y, dw_in, total_out
    )
    qkv_grad, o_grad, w_in_grad, w_out_grad, tok_grad, out, gain1_grad, gain2_grad, gate_grad = results(
        frozen, grads, w_in_grad, w_out_grad, tok_grad, out, early, late
    )
    return (
        out[None], tok_grad[None], gain1_grad, qkv_grad, o_grad, gain2_grad, gate_grad.T, w_in_grad, w_out_grad
    )


def solution(mesh):
    fine = Mesh(mesh.devices.reshape(2, 4, 2, 4, 2), ALL)
    seq, exp = ("zh", "x"), ("zl", "y", "c")
    rows, rest = P(exp, seq, None), P()
    in_specs = (rows, rows, rest, rest, rest, rest, rest, P(exp, None, seq), rows, rows, rest)
    out_specs = (rows, rows, rest, rest, rest, rest, rest, P(exp, None, seq), rows)
    return jax.shard_map(on_device, mesh=fine, in_specs=in_specs, out_specs=out_specs, check_vma=False)
```

```python
import functools
import math

import jax
import jax.numpy as jnp
from jax import lax
from jax.experimental import pallas as pl
from jax.experimental.pallas import tpu as pltpu
from jax.sharding import Mesh
from jax.sharding import PartitionSpec as P

D = 768
HEADS = 12
HEAD_DIM = 64
EXPERTS = 32
CAP = 32
ROWS = 256
BLOCKS = 8
FF = 3072
SLOTS = EXPERTS * CAP
EPS = 1e-5
SCALE = HEAD_DIM ** -0.5
LOG2E = math.log2(math.e)
BF16 = jnp.bfloat16
F32 = jnp.float32
NEG = -1e30

SEQ = ("zh", "x")
MESH = pl.DeviceIdType.MESH
ALL = ("zh", "x", "zl", "y", "c")


def dot(a, b, ca=1, cb=0):
    return lax.dot_general(a, b, (((ca,), (cb,)), ((), ())), preferred_element_type=F32)


def params(mb=56):
    return pltpu.CompilerParams(vmem_limit_bytes=mb * 2**20)


def vspec(n):
    return [pl.BlockSpec(memory_space=pltpu.VMEM)] * n


def call(body, outs, n_in, scratch=(), **kw):
    return pl.pallas_call(
        body,
        out_shape=[jax.ShapeDtypeStruct(s, t) for s, t in outs],
        in_specs=vspec(n_in),
        out_specs=vspec(len(outs)),
        scratch_shapes=list(scratch),
        compiler_params=params(),
        **kw,
    )


def norm(v):
    mean = jnp.mean(v, axis=-1, keepdims=True)
    centred = v - mean
    inv = lax.rsqrt(jnp.mean(centred * centred, axis=-1, keepdims=True) + EPS)
    return centred * inv, inv


def row_of(gain_ref):
    return gain_ref[...].reshape(1, D)


def norm_back(grad, gain, unit, inv):
    t = grad * gain
    m1 = jnp.mean(t, axis=-1, keepdims=True)
    m2 = jnp.mean(t * unit, axis=-1, keepdims=True)
    return inv * (t - m1 - unit * m2)


def lane_low():
    return lax.broadcasted_iota(jnp.int32, (1, 128), 1) < 64


def pair_up(wide, s):
    low = wide[:, 128 * (s // 2) : 128 * (s // 2) + 128]
    if s % 2:
        low = pltpu.roll(low, 64, 1)
    high = wide[:, 512 + 128 * (s // 4) : 640 + 128 * (s // 4)]
    if (s // 2) % 2 == 0:
        high = pltpu.roll(high, 64, 1)
    return jnp.where(lane_low(), low, high)


def unpair(tiles):
    out = []
    for t in range(4):
        out.append(
            jnp.where(lane_low(), tiles[2 * t], pltpu.roll(tiles[2 * t + 1], 64, 1))
        )
    for t in range(2):
        a = tiles[4 * t] + tiles[4 * t + 1]
        b = tiles[4 * t + 2] + tiles[4 * t + 3]
        out.append(jnp.where(lane_low(), pltpu.roll(a, 64, 1), b))
    return out


def project(tok_ref, gain_ref, part_weights, send_ref):
    unit, _ = norm(tok_ref[...].astype(F32))
    a1 = (unit * row_of(gain_ref)).astype(BF16)
    for part in range(3):
        wide = dot(a1, part_weights(part))
        for s in range(BLOCKS):
            send_ref[s, :, part * 128 : part * 128 + 128] = pair_up(wide, s).astype(
                BF16
            )


def unit_of(half, h, i):
    if h == 0:
        return 0, i, i + 1, i, i
    a, b = ((0, 1), (3, 2), (4, 5), (7, 6))[i]
    return 1, a + half * (b - a), 2 * i + 2, 2 * i, BLOCKS + i


def masked_scores(k, q, block, first, count):
    s = dot(k, q, 1, 1)
    start = first * ROWS
    tail = (count - first) * ROWS
    keys = lax.broadcasted_iota(jnp.int32, (tail, ROWS), 0) + start
    queries = lax.broadcasted_iota(jnp.int32, (tail, ROWS), 1) + block * ROWS
    end = jnp.where(keys <= queries, s[start:], NEG)
    return end if start == 0 else jnp.concatenate([s[:start], end], axis=0)


def head_mask(h):
    low = lane_low()
    return (low if h == 0 else jnp.logical_not(low)).astype(F32).astype(BF16)


def padded(h, t):
    zero = jnp.zeros_like(t)
    return jnp.concatenate([t, zero] if h == 0 else [zero, t], axis=0).T


def attend_forward(half, qkv_ref, o_ref, ot_ref, lse_ref, vt_ref, arrived, leave):
    c = SCALE * LOG2E
    for pair in range(BLOCKS // 2):
        for b in (2 * pair, 2 * pair + 1):
            arrived(b)
            vt_ref[:, b * ROWS : (b + 1) * ROWS] = qkv_ref[b, :, 256:384].T
            o_ref[b] = jnp.zeros((ROWS, 128), BF16)
        for unit in ((1, pair), (0, 2 * pair), (0, 2 * pair + 1)):
            h, block, count, first, u = unit_of(half, *unit)
            q = qkv_ref[block, :, 0:128] * head_mask(h)
            k = qkv_ref[0:count, :, 128:256].reshape(count * ROWS, 128)
            s = masked_scores(k, q, block, first, count)
            top = jnp.max(s, axis=0, keepdims=True)
            p = jnp.exp2((s - top) * c)
            total = jnp.sum(p, axis=0, keepdims=True)
            ot = dot(vt_ref[64 * h : 64 * h + 64, 0 : count * ROWS], p.astype(BF16))
            ot = ot / total
            ot_ref[u] = ot
            lse_ref[u] = jnp.broadcast_to(top * c + jnp.log2(total), (8, ROWS))
            o_ref[block] = (o_ref[block].astype(F32) + padded(h, ot)).astype(BF16)
        if pair % 2:
            leave(pair // 2)


def attend_backward(half, qkv_ref, do_ref, ot_ref, lse_ref, out_ref, kt_ref, dk_ref, dv_ref, arrived, leave, beside):
    c = SCALE * LOG2E
    for b in range(BLOCKS):
        kt_ref[:, b * ROWS : (b + 1) * ROWS] = qkv_ref[b, :, 128:256].T
        out_ref[b, :, 0:128] = jnp.zeros((ROWS, 128), BF16)
    dk_ref[...] = jnp.zeros_like(dk_ref)
    dv_ref[...] = jnp.zeros_like(dv_ref)

    def one(h, i):
        h, block, count, first, u = unit_of(half, h, i)
        rows = count * ROWS
        q = qkv_ref[block, :, 0:128] * head_mask(h)
        do = do_ref[block] * head_mask(h)
        dot_rows = do.astype(F32).T[64 * h : 64 * h + 64]
        delta = jnp.sum(dot_rows * ot_ref[u], axis=0, keepdims=True)
        lse = lse_ref[u][0:1]
        k = qkv_ref[0:count, :, 128:256].reshape(rows, 128)
        v = qkv_ref[0:count, :, 256:384].reshape(rows, 128)
        s = masked_scores(k, q, block, first, count)
        p = jnp.exp2(s * c - lse)
        dp = dot(v, do, 1, 1)
        ds = (p * (dp - delta)).astype(BF16)
        dv_ref[0:rows] += dot(p.astype(BF16), do)
        dk_ref[0:rows] += dot(ds, q)
        dqt = dot(kt_ref[64 * h : 64 * h + 64, 0:rows], ds) * SCALE
        out_ref[block, :, 0:128] = (
            out_ref[block, :, 0:128].astype(F32) + padded(h, dqt)
        ).astype(BF16)

    for pair in reversed(range(BLOCKS // 2)):
        b = 2 * pair + 1
        arrived(b)
        arrived(b - 1)
        one(1, pair)
        for b in (b, b - 1):
            one(0, b)
            at = slice(b * ROWS, (b + 1) * ROWS)
            out_ref[b, :, 128:256] = (dk_ref[at] * SCALE).astype(BF16)
            out_ref[b, :, 256:384] = dv_ref[at].astype(BF16)
        beside(pair)
        if pair % 2 == 0:
            leave(pair // 2)


def choices(routes):
    ids = lax.broadcasted_iota(jnp.int32, (ROWS, EXPERTS), 1).astype(F32)
    e1, e2 = [jnp.broadcast_to(routes[k : k + 1].astype(F32), (8, ROWS)).T[:, 0:1] for k in range(2)]
    m1, m2 = (e1 == ids).astype(F32), (e2 == ids).astype(F32)
    r = lax.broadcasted_iota(jnp.int32, (ROWS, ROWS), 0)
    k = lax.broadcasted_iota(jnp.int32, (ROWS, ROWS), 1)
    lower = (k < r).astype(F32).astype(BF16)
    earlier = dot(lower, (m1 + m2).astype(BF16))
    s1 = jnp.sum(earlier * m1, axis=1, keepdims=True)
    s2 = jnp.sum(earlier * m2, axis=1, keepdims=True)

    return m1, m2, e1 * CAP + s1, e2 * CAP + s2


def chosen(col):
    at = lax.broadcasted_iota(jnp.int32, (ROWS, SLOTS), 1).astype(F32)
    return (at == col).astype(F32).astype(BF16)


def chosen_t(col):
    row = jnp.broadcast_to(col, (ROWS, 128)).T[0:1]
    at = lax.broadcasted_iota(jnp.int32, (SLOTS, ROWS), 0).astype(F32)
    return (at == row).astype(F32).astype(BF16)


def deal_body(cot_ref, routes_ref, gates_ref, send_ref):
    _, _, c1, c2 = choices(routes_ref[...])
    c = cot_ref[...].astype(F32)
    first, second = (gates_ref[:, 0:1] * c).astype(BF16), (gates_ref[:, 1:2] * c).astype(BF16)
    send_ref[...] = (dot(chosen_t(c1), first) + dot(chosen_t(c2), second)).astype(BF16)


def middle_body(o_ref, tok_ref, w_o, gain_ref, gate_ref, routes_ref, mid_ref, att_ref, send_ref, gates_ref):
    tiles = unpair([o_ref[s].astype(F32) for s in range(BLOCKS)])
    o = jnp.concatenate([t.astype(BF16) for t in tiles], axis=1)
    att_ref[...] = o
    mid = tok_ref[...].astype(F32) + dot(o, w_o)
    mid_ref[...] = mid
    unit, _ = norm(mid)
    a2 = (unit * row_of(gain_ref)).astype(BF16)
    logits = dot(a2, gate_ref[...], 1, 1)
    m1, m2, c1, c2 = choices(routes_ref[...])
    l1 = jnp.sum(logits * m1, axis=1, keepdims=True)
    l2 = jnp.sum(logits * m2, axis=1, keepdims=True)
    top = jnp.maximum(l1, l2)
    x1, x2 = jnp.exp(l1 - top), jnp.exp(l2 - top)
    g1, g2 = x1 / (x1 + x2), x2 / (x1 + x2)
    lane = lax.broadcasted_iota(jnp.int32, (ROWS, 128), 1)
    gates_ref[...] = jnp.where(lane == 0, g1, g2)
    send_ref[...] = dot(chosen_t(c1) + chosen_t(c2), a2).astype(BF16)


def gelu_parts(h):
    t = pl.reciprocal(1.0 + (0.3275911 * 0.5**0.5) * jnp.abs(h), approx=True)
    e = jnp.exp2(h * h * (-0.5 * LOG2E))
    poly = t * (
        0.127414796
        + t * (-0.142248368 + t * (0.7107068705 + t * (-0.7265760135 + t * 0.5307027145)))
    )
    tail = poly * e
    phi = jnp.where(h >= 0, 1.0 - tail, tail)
    return h * phi, phi + h * e * (1.0 / math.sqrt(2.0 * math.pi))


def div(a, b):
    return lax.div(a, jnp.int32(b))


def rem(a, b):
    return lax.rem(a, jnp.int32(b))


def coords():
    return tuple(lax.axis_index(a) for a in ALL)


def near(x, pair):
    return x + rem(div(x, 2) + pair, 2) * (3 - 2 * x)


def neighbour(x):
    return x + 1 - 2 * rem(x, 2)


def expert_of(zh, x, zl, y):
    return 4 * (4 * zl + y) + 2 * div(x, 2) + zh


def remote(src, dst, send, recv, device):
    return pltpu.make_async_remote_copy(
        src_ref=src,
        dst_ref=dst,
        send_sem=send,
        recv_sem=recv,
        device_id=device,
        device_id_type=MESH,
    )


def await_bytes(ref, sem):
    pltpu.make_async_copy(ref, ref, sem).wait()


def chip_partner(me, k):
    zh, x, zl, y, c = me
    return (
        rem(zh + div(k, 8), 2),
        rem(x + rem(div(k, 2), 4), 4),
        zl,
        y,
        rem(c + rem(k, 2), 2),
    )


def core_partner(me, k):
    return me[:4] + (rem(me[4] + k, 2),)


def row_partner(me, k):
    zh, x, zl, y, c = me
    return (
        rem(zh + rem(div(k, 8), 2), 2),
        x + div(k, 16) * (3 - 2 * x),
        rem(zl + rem(div(k, 4), 2), 2),
        rem(y + rem(k, 4), 4),
        c,
    )


def head_partner(me, k):
    zh, x, zl, y, c = me
    t = rem(zh * 4 + x + k, 8)
    return t, (div(t, 4), rem(t, 4), zl, y, c)


def greet(me, partner, count):
    barrier = pltpu.get_barrier_semaphore()

    def one(k, carry):
        pl.semaphore_signal(
            barrier, inc=1, device_id=partner(me, k), device_id_type=MESH
        )
        return carry

    lax.fori_loop(1, count, one, 0)
    return count - 1


def hello(*groups):
    me = coords()
    return me, sum(greet(me, partner, count) for partner, count in groups)


def enter(total):
    pl.semaphore_wait(pltpu.get_barrier_semaphore(), total)


class HeadSwap:
    def __init__(self, me, send, recv, sems):
        self.me, self.send, self.recv, self.sems = me, send, recv, sems
        self.place = me[0] * 4 + me[1]

    def leave(self, half):
        s = self.place
        zh, x, zl, y, c = self.me
        for k in (2, 1, 3, 0):
            p = rem(x + k, 4)
            t = 4 * half + p
            away = remote(
                self.send.at[t], self.recv.at[s], self.sems.at[0, t], self.sems.at[1, s], (jnp.int32(half), p, zl, y, c)
            )
            if k:
                away.start()
            else:
                local = pltpu.make_async_copy(self.send.at[t], self.recv.at[t], self.sems.at[1, t])
                pl.when(zh == half)(local.start)
                pl.when(zh != half)(away.start)

    def start(self):
        s = self.place
        pltpu.make_async_copy(self.send.at[s], self.recv.at[s], self.sems.at[1, s]).start()
        for k in (2, 4, 6, 1, 3, 5, 7):
            t, device = head_partner(self.me, jnp.int32(k))
            remote(self.send.at[t], self.recv.at[s], self.sems.at[0, t], self.sems.at[1, s], device).start()

    def arrived(self, t):
        await_bytes(self.recv.at[t], self.sems.at[1, t])

    def wait_send(self):
        for k in range(1, 8):
            t, _ = head_partner(self.me, jnp.int32(k))
            await_bytes(self.send.at[t], self.sems.at[0, t])


class RowSwap:
    def __init__(self, me, send, recv, sems, back=False):
        self.me, self.send, self.recv, self.sems = me, send, recv, sems
        self.back = back

    def slot(self, kx, kz, ky):
        return 8 * rem(8 + ky - kz - 2 * kx, 4) + 4 * kx + kz

    def ends(self, k):
        zh, x, zl, y, c = self.me
        device = row_partner(self.me, k)
        kx, kz, ky = div(k, 16), rem(div(k, 4), 4), rem(k, 4)
        if self.back:
            src = self.slot(kx, kz, ky)
            dst = expert_of(zh, x, zl, y)
        else:
            src = expert_of(*device[:4])
            dst = self.slot(kx, kz, 4 - ky)
        rows = lambda n: pl.ds(pl.multiple_of(n * CAP, CAP), CAP)
        return self.send.at[rows(src)], self.recv.at[rows(dst)], device

    def start(self, first=0, last=32):
        if first == 0:
            src, dst, _ = self.ends(jnp.int32(0))
            pltpu.make_async_copy(src, dst, self.sems.at[1]).start()

        def one(k, carry):
            src, dst, device = self.ends(rem(9 * k, 32))
            remote(src, dst, self.sems.at[0], self.sems.at[1], device).start()
            return carry

        lax.fori_loop(max(first, 1), last, one, 0)

    def start_block(self, r):
        def one(n, carry):
            q = rem(3 * n, 8)
            kx, kz = div(q, 4), rem(q, 4)
            k = 16 * kx + 4 * kz + rem(r + kz + 2 * kx, 4)
            src, dst, device = self.ends(k)
            local = pltpu.make_async_copy(src, dst, self.sems.at[1])
            away = remote(src, dst, self.sems.at[0], self.sems.at[1], device)
            pl.when(k == 0)(local.start)
            pl.when(k != 0)(away.start)
            return carry

        lax.fori_loop(0, 8, one, 0)

    def wait_recv(self):
        await_bytes(self.recv, self.sems.at[1])

    def wait_send(self, first=0, last=31):
        await_bytes(self.send.at[pl.ds(0, (last - first) * CAP)], self.sems.at[0])

    def wait(self):
        self.wait_recv()
        self.wait_send()


def remote_params(n, mb=60):
    return pltpu.CompilerParams(
        vmem_limit_bytes=mb * 2**20, collective_id=n, has_side_effects=True
    )


VMEM = pl.BlockSpec(memory_space=pltpu.VMEM)
ANY = pl.BlockSpec(memory_space=pl.ANY)
DMA = pltpu.SemaphoreType.DMA


class Weights:
    def __init__(self, me, w_in, w_out, full_in, full_out, sems):
        self.me, self.refs, self.full, self.sems = me, (w_in, w_out), (full_in, full_out), sems

    def place(self, i, x, zh):
        at = pl.ds(pl.multiple_of(zh * 384, 128), 384)
        return self.full[0].at[x, :, at] if i == 0 else self.full[1].at[x, at, :]

    def first(self, i, b):
        zh, x, zl, y, c = self.me
        device = (jnp.int32(b), near(x, c), zl, y, zh)
        copy = remote(
            self.refs[i].at[b], self.place(i, x, zh), self.sems.at[0, i, b], self.sems.at[1, i, x], device
        )
        local = pltpu.make_async_copy(
            self.refs[i].at[b], self.place(i, x, zh), self.sems.at[1, i, x]
        )
        own = jnp.logical_and(
            jnp.logical_and(zh == b, div(x, 2) == c), zh == c
        )
        return copy, local, own

    def start(self, i):
        for b in range(2):
            copy, local, own = self.first(i, b)
            pl.when(own)(local.start)
            pl.when(jnp.logical_not(own))(copy.start)

    def forward(self, i, x, step):
        zh, me_x, zl, y, c = self.me
        piece = self.place(i, x, c)
        device = (zh, neighbour(me_x), zl, y, c) if step == 2 else (zh, me_x, zl, y, 1 - c)
        return remote(piece, piece, self.sems.at[2 * step - 2, i, x], self.sems.at[2 * step - 1, i, x], device)

    def sources(self, step):
        x = self.me[1]
        if step == 1:
            return x, 3 - x
        return neighbour(x), 3 - neighbour(x)

    def second(self, i):
        for x in self.sources(1):
            await_bytes(self.place(i, x, self.me[4]), self.sems.at[1, i, x])
            self.forward(i, x, 2).start()
            self.forward(i, x, 3).start()

    def third(self, i):
        for x in self.sources(2):
            self.forward(i, x, 2).wait_recv()
            self.forward(i, x, 3).start()

    def ready(self, i):
        for x in range(4):
            self.forward(i, jnp.int32(x), 3).wait_recv()

    def finish(self, i):
        for b in range(2):
            copy, _, own = self.first(i, b)
            pl.when(jnp.logical_not(own))(copy.wait_send)
        for x in self.sources(1):
            self.forward(i, x, 2).wait_send()
        for x in range(4):
            self.forward(i, jnp.int32(x), 3).wait_send()


STEP = 256
CHUNKS = 4
TILES = SLOTS // STEP


def row_block(r):
    return pl.ds(pl.multiple_of(r * STEP, STEP), STEP)


def half_rows(n):
    return pl.ds(pl.multiple_of(n * 384, 128), 384)


def front_body(tok_ref, cot_ref, gain1_ref, w_qkv_ref, w_o_ref, gain2_ref, gate_ref, routes_ref, w_in_ref, w_out_ref,
               qkv_out, ret_ref, y_ref, mid_out, att_out, gates_out, ot_out, lse_out, dwin_out, total_out,
               qkv_ref, mid_ref, att_ref, gates_ref, ot_ref, lse_ref, total_ref, xt_ref,
               qkv_send, o_send, o_recv, x_send, c_send, x_ref, c_ref, vt_ref, full_in, full_out, g_ref, d_ref,
               part_in, part_out, got_in, got_out, got2,
               head_sems, row_sems, weight_sems, load_sems, save_sems, core_sems, pair_sems):
    loads = [
        pltpu.make_async_copy(w_qkv_ref.at[:, p * D : p * D + D], g_ref.at[p, 0:D], load_sems.at[p]) for p in range(3)
    ] + [pltpu.make_async_copy(w_o_ref, g_ref.at[3, 0:D], load_sems.at[3])]
    for load in loads:
        load.start()
    me, greeted = hello((chip_partner, 16), (row_partner, 32))
    zh, x, zl, y, c = me
    weights = Weights(me, w_in_ref, w_out_ref, full_in, full_out, weight_sems)
    heads = HeadSwap(me, qkv_send, qkv_ref, head_sems.at[0])
    heads_back = HeadSwap(me, o_send, o_recv, head_sems.at[1])
    rows_c = RowSwap(me, c_send, c_ref, row_sems.at[0])
    rows_x = RowSwap(me, x_send, x_ref, row_sems.at[1])
    rows_ret = RowSwap(me, x_send, ret_ref, row_sems.at[2], back=True)
    rows_y = RowSwap(me, c_send, y_ref, row_sems.at[3], back=True)

    def part_weights(p):
        loads[p].wait()
        return g_ref[p, 0:D, :]

    project(tok_ref, gain1_ref, part_weights, qkv_send)
    enter(greeted)
    heads.start()
    weights.start(0)
    heads.arrived(0)
    heads.arrived(1)
    weights.start(1)
    attend_forward(
        rem(x, 2), qkv_ref, o_send, ot_ref, lse_ref, vt_ref,
        lambda b: heads.arrived(b) if b > 1 else None, heads_back.leave,
    )
    weights.second(0)
    for t in range(BLOCKS):
        heads_back.arrived(t)
    loads[3].wait()
    middle_body(o_recv, tok_ref, g_ref[3, 0:D, :], gain2_ref, gate_ref, routes_ref, mid_ref, att_ref, x_send, gates_ref)
    rows_x.start()
    saves = [
        pltpu.make_async_copy(src, dst, save_sems.at[n])
        for n, (src, dst) in enumerate(
            ((qkv_ref, qkv_out), (mid_ref, mid_out), (att_ref, att_out), (gates_ref, gates_out), (ot_ref, ot_out), (lse_ref, lse_out))
        )
    ]
    for save in saves:
        save.start()
    deal_body(cot_ref, routes_ref, gates_ref, c_send)
    weights.second(1)
    weights.third(0)
    rows_x.wait_send(0, 22)
    rows_c.start()
    weights.ready(0)
    rows_x.wait_recv()
    rows_x.wait_send(22, 31)

    def hidden(j):
        tiles = [slice(r * STEP, r * STEP + STEP) for r in range(TILES)]
        w = full_in[j]

        def after(at, h):
            g, d = gelu_parts(h)
            g_ref[j, at, :] = g.astype(BF16)
            d_ref[j, at, :] = d.astype(BF16)

        before = dot(x_ref[tiles[0], :], w)
        for r in range(1, TILES):
            h = dot(x_ref[tiles[r], :], w)
            after(tiles[r - 1], before)
            before = h
        after(tiles[-1], before)

    def hidden_loop(j, carry):
        @pl.when(j == CHUNKS - 1)
        def _():
            weights.third(1)

        hidden(j)
        return carry

    lax.fori_loop(0, CHUNKS, hidden_loop, 0)
    for r in range(TILES):
        xt_ref[:, r * STEP : (r + 1) * STEP] = x_ref[r * STEP : (r + 1) * STEP, :].T
    weights.ready(1)
    rows_c.wait()

    def produce(n, carry):
        r = TILES - 1 - n
        at = row_block(r)
        out = dot(g_ref[0, at, :], full_out[0])
        for j in range(1, CHUNKS):
            out = out + dot(g_ref[j, at, :], full_out[j])
        c_send[at, :] = out.astype(BF16)
        rows_y.start_block(r)
        return carry

    lax.fori_loop(0, TILES, produce, 0)

    sibling = core_partner(me, 1)

    def half(i, j, n):
        return part_in.at[j, :, half_rows(n)] if i == 0 else part_out.at[j, half_rows(n), :]

    def over(i, j):
        got = (got_in, got_out)[i]
        return remote(half(i, j, 1 - c), got.at[j], core_sems.at[0, i, j], core_sems.at[1, i, j], sibling)

    def second_grad(j, carry):
        part_out[j] = dot(g_ref[j], c_ref[...], 0, 0).astype(BF16)
        over(1, j).start()
        return carry

    lax.fori_loop(0, CHUNKS, second_grad, 0)

    def second_sum(j, carry):
        over(1, j).wait()
        got_out[j] = (half(1, j, c)[...].astype(F32) + got_out[j].astype(F32)).astype(BF16)
        return carry

    lax.fori_loop(0, CHUNKS, second_sum, 0)
    pass_on, keep = (neighbour(x), 3 - neighbour(x)), (x, 3 - x)

    def pair_over(n):
        return remote(got_out.at[pass_on[n]], got2.at[n], pair_sems.at[0, n], pair_sems.at[1, n], (zh, neighbour(x), zl, y, c))

    for n in range(2):
        pair_over(n).start()

    def back(n, carry):
        r = TILES - 1 - n
        at = row_block(r)
        dx = jnp.zeros((STEP, D), F32)
        for j in range(CHUNKS):
            cw = dot(c_ref[at, :], full_out[j], 1, 1)
            dh = (d_ref[j, at, :].astype(F32) * cw).astype(BF16)
            d_ref[j, at, :] = dh
            dx = dx + dot(dh, full_in[j], 1, 1)
        x_send[at, :] = dx.astype(BF16)
        rows_ret.start_block(r)
        return carry

    lax.fori_loop(0, TILES, back, 0)

    def first_grad(n, carry):
        j, r = div(n, 3), rem(n, 3)
        part_in[j, row_block(r), :] = dot(xt_ref[row_block(r), :], d_ref[j]).astype(BF16)

        @pl.when(r == 2)
        def _():
            over(0, j).start()

        return carry

    lax.fori_loop(0, 3 * CHUNKS, first_grad, 0)

    def first_save(j):
        return pltpu.make_async_copy(got_in.at[j], dwin_out.at[j], save_sems.at[7])

    def first_sum(j, carry):
        over(0, j).wait()
        got_in[j] = (half(0, j, c)[...].astype(F32) + got_in[j].astype(F32)).astype(BF16)
        first_save(j).start()
        return carry

    lax.fori_loop(0, CHUNKS, first_sum, 0)
    heads.wait_send()
    heads_back.wait_send()
    weights.finish(0)
    weights.finish(1)
    for n in range(2):
        pair_over(n).wait()
        total_ref[n] = (got_out[keep[n]].astype(F32) + got2[n].astype(F32)).astype(BF16)
    last = pltpu.make_async_copy(total_ref, total_out, save_sems.at[6])
    last.start()
    for save in saves:
        save.wait()
    rows_y.wait()
    rows_ret.wait()
    last.wait()
    await_bytes(dwin_out, save_sems.at[7])


def front(tok, cot, gain1, w_qkv, w_o, gain2, gate, routes, w_in, w_out):
    buf = lambda *s: pltpu.VMEM(s, BF16)
    f32 = lambda *s: pltpu.VMEM(s, F32)
    outs = [
        ((BLOCKS, ROWS, 384), BF16),
        ((SLOTS, D), BF16),
        ((SLOTS, D), BF16),
        ((ROWS, D), F32),
        ((ROWS, D), BF16),
        ((ROWS, 128), F32),
        ((12, 64, ROWS), F32),
        ((12, 8, ROWS), F32),
        ((CHUNKS, D, 384), BF16),
        ((2, 384, D), BF16),
    ]
    return pl.pallas_call(
        front_body,
        out_shape=[jax.ShapeDtypeStruct(s, t) for s, t in outs],
        in_specs=[VMEM] * 3 + [ANY] * 2 + [VMEM] * 3 + [ANY] * 2,
        out_specs=[ANY] * len(outs),
        scratch_shapes=[
            buf(BLOCKS, ROWS, 384),
            f32(ROWS, D),
            buf(ROWS, D),
            f32(ROWS, 128),
            f32(12, 64, ROWS),
            f32(12, 8, ROWS),
            buf(2, 384, D),
            buf(D, SLOTS),
            buf(BLOCKS, ROWS, 384),
            buf(BLOCKS, ROWS, 128),
            buf(BLOCKS, ROWS, 128),
            buf(SLOTS, D),
            buf(SLOTS, D),
            buf(SLOTS, D),
            buf(SLOTS, D),
            buf(128, BLOCKS * ROWS),
            buf(CHUNKS, D, D),
            buf(CHUNKS, D, D),
            buf(CHUNKS, SLOTS, D),
            buf(CHUNKS, SLOTS, D),
            buf(CHUNKS, D, D),
            buf(CHUNKS, D, D),
            buf(CHUNKS, D, 384),
            buf(CHUNKS, 384, D),
            buf(2, 384, D),
            DMA((2, 2, 8)),
            DMA((4, 2)),
            DMA((6, 2, 4)),
            DMA((4,)),
            DMA((8,)),
            DMA((2, 2, 4)),
            DMA((2, 2)),
        ],
        compiler_params=remote_params(0, 63),
    )(tok, cot, gain1, w_qkv, w_o, gain2, gate, routes, w_in, w_out)


def back_body(ret_ref, y_ref, cot_ref, routes_ref, gates_ref, mid_ref, gain_ref, gate_w_ref, w_o_ref,
              send_ref, dmid_ref, gate_grad_ref, gain_grad_ref, out_ref):
    m1, m2, c1, c2 = choices(routes_ref[...])
    s1, s2 = chosen(c1), chosen(c2)
    g1, g2 = gates_ref[:, 0:1], gates_ref[:, 1:2]
    y = y_ref[...]
    c, y1, y2 = cot_ref[...].astype(F32), dot(s1, y), dot(s2, y)
    dl = g1 * g2 * jnp.sum(c * (y1 - y2), axis=1, keepdims=True)
    dlogits = (m1 - m2) * dl
    unit, inv = norm(mid_ref[...])
    high = dlogits.astype(BF16)
    low = (dlogits - high.astype(F32)).astype(BF16)
    gate_w = gate_w_ref[...]
    da2 = dot(s1 + s2, ret_ref[...]) + dot(high, gate_w) + dot(low, gate_w)
    dmid = c + norm_back(da2, row_of(gain_ref), unit, inv)
    dmid_ref[...] = dmid
    do = dot(dmid.astype(BF16), w_o_ref[...], 1, 1)
    for s in range(BLOCKS):
        send_ref[s] = pair_up(do, s).astype(BF16)

    def later():
        a2 = (unit * row_of(gain_ref)).astype(BF16)
        gate_grad_ref[...] = dot(high, a2, 0, 0) + dot(low, a2, 0, 0)
        gain_grad_ref[...] = jnp.sum(da2 * unit, axis=0, keepdims=True)
        out_ref[...] = (mid_ref[...] + (g1 * y1 + g2 * y2)).astype(BF16)

    return later


def axis_place(me, a):
    zh, x, zl, y, c = me
    return (x, y, 2 * zh + zl)[a]


def axis_peer(me, a, k):
    zh, x, zl, y, c = me
    p = rem(axis_place(me, a) + k, 4)
    if a == 0:
        return p, (zh, p, zl, y, c)
    if a == 1:
        return p, (zh, x, zl, p, c)
    return p, (div(p, 2), x, rem(p, 2), y, c)


def axis_partner(me, k):
    zh, x, zl, y, c = me
    along_z = div(k, 4)
    dz = rem(k + 1, 4) * along_z
    z = rem(2 * zh + zl + dz, 4)
    return div(z, 2), x, rem(z, 2), rem(y + k * (1 - along_z), 4), c


def multiple(n, w):
    return pl.ds(pl.multiple_of(n * w, w), w)


PEERS = (1, 2, 3)


class GroupSum:
    def __init__(self, me, g, axes, out, bufs, sems):
        self.me, self.g, self.axes, self.out, self.sems = me, g, axes, out, sems.at[g]
        self.s0, self.r0, self.a0, self.r1, self.a1, self.s2, self.r2, self.r3, self.whole = [b.at[g] for b in bufs]
        self.place = [axis_place(me, a) for a in axes]
        self.c = me[4]

    def copy(self, stage, k, src, dst):
        if stage in (0, 6):
            device = core_partner(self.me, 1)
        else:
            device = axis_peer(self.me, self.axes[(0, 0, 1, 2, 1, 0)[stage]], jnp.int32(k))[1]
        return remote(src, dst, self.sems.at[stage, 0, k], self.sems.at[stage, 1, k], device)

    def peer(self, t, k):
        return axis_peer(self.me, self.axes[t], jnp.int32(k))[0]

    def swap(self):
        return self.copy(0, 0, self.s0, self.r0)

    def scatter1(self, k):
        return self.copy(1, k, self.s0.at[multiple(self.peer(0, k), 192)], self.r1.at[k - 1])

    def scatter2(self, k):
        return self.copy(2, k, self.s2.at[multiple(self.peer(1, k), 48)], self.r2.at[k - 1])

    def share(self, k):
        mine = self.r3.at[self.place[2]]
        return self.copy(3, k, mine, mine)

    def block(self, rows):
        i, j = self.place[0], self.place[1]
        if rows == 48:
            return self.whole.at[multiple(4 * i + j, 48)]
        if rows == 192:
            return self.whole.at[multiple(i, 192)]
        return self.whole

    def gather(self, stage, k):
        ref = self.block((48, 192, 768)[stage - 4])
        if stage < 6:
            return self.copy(stage, k, ref, ref)
        lanes = pl.ds(pl.multiple_of(self.g * D + self.c * 384, 128), 384)
        return self.copy(stage, k, ref, self.out.at[:, lanes])

    def save(self):
        lanes = pl.ds(pl.multiple_of(self.g * D + self.c * 384, 128), 384)
        return pltpu.make_async_copy(self.whole, self.out.at[:, lanes], self.sems.at[6, 0, 1])

    def begin(self, grad):
        self.s0[...] = grad(1 - self.c).astype(BF16)
        self.swap().start()
        self.a0[...] = grad(self.c)

    def step1(self):
        self.swap().wait()
        self.a0[...] += self.r0[...].astype(F32)
        self.s0[...] = self.a0[...].astype(BF16)
        for k in PEERS:
            self.scatter1(k).start()

    def step2(self):
        for k in PEERS:
            self.scatter1(k).wait_recv()
        mine = self.a0[multiple(self.place[0], 192), :]
        for k in PEERS:
            mine = mine + self.r1[k - 1].astype(F32)
        self.a1[...] = mine
        self.s2[...] = mine.astype(BF16)
        for k in PEERS:
            self.scatter2(k).start()

    def step3(self):
        for k in PEERS:
            self.scatter2(k).wait_recv()
        mine = self.a1[multiple(self.place[1], 48), :]
        for k in PEERS:
            mine = mine + self.r2[k - 1].astype(F32)
        self.r3[self.place[2]] = mine.astype(BF16)
        for k in PEERS:
            self.share(k).start()

    def step4(self):
        for k in PEERS:
            p = axis_peer(self.me, self.axes[2], jnp.int32(k))[0]
            self.copy(3, 4 - k, self.r3.at[p], self.r3.at[p]).wait_recv()
        total = (self.r3[0].astype(F32) + self.r3[1].astype(F32)) + (
            self.r3[2].astype(F32) + self.r3[3].astype(F32)
        )
        self.block(48)[...] = total.astype(BF16)
        for k in PEERS:
            self.gather(4, k).start()

    def step5(self):
        for k in PEERS:
            self.gather(4, k).wait_recv()
        for k in PEERS:
            self.gather(5, k).start()

    def step6(self):
        for k in PEERS:
            self.gather(5, k).wait_recv()
        self.gather(6, 0).start()
        self.save().start()

    def finish(self):
        self.gather(6, 0).wait()
        self.save().wait()
        for k in PEERS:
            self.scatter1(k).wait_send()
            self.scatter2(k).wait_send()
            self.share(k).wait_send()
            self.gather(4, k).wait_send()
            self.gather(5, k).wait_send()


class SmallSum:
    def __init__(self, me, mine, over, slots, out, sems):
        self.me, self.mine, self.over, self.slots, self.out, self.sems = me, mine, over, slots, out, sems

    def half(self, ref, n):
        return ref.at[:, half_rows(n)]

    def swap(self):
        return remote(self.over.at[0], self.over.at[1], self.sems.at[0, 0], self.sems.at[1, 0], core_partner(self.me, 1))

    def share(self, a, k):
        n = 3 * a + k
        mine = self.slots.at[a, axis_place(self.me, a)]
        return remote(mine, mine, self.sems.at[0, n], self.sems.at[1, n], axis_peer(self.me, a, jnp.int32(k))[1])

    def join(self):
        mine = self.half(self.out, self.me[4])
        return remote(mine, mine, self.sems.at[0, 10], self.sems.at[1, 10], core_partner(self.me, 1))

    def begin(self):
        self.over[0] = self.half(self.mine, 1 - self.me[4])[...].astype(BF16)
        self.swap().start()

    def step(self, a):
        if a == 0:
            self.swap().wait_recv()
            total = self.half(self.mine, self.me[4])[...] + self.over[1].astype(F32)
        else:
            for k in PEERS:
                self.share(a - 1, k).wait_recv()
            s = [self.slots[a - 1, p].astype(F32) for p in range(4)]
            total = (s[0] + s[1]) + (s[2] + s[3])
        if a < 3:
            self.slots[a, axis_place(self.me, a)] = total.astype(BF16)
            for k in PEERS:
                self.share(a, k).start()
        else:
            self.half(self.out, self.me[4])[...] = total.astype(BF16)
            self.join().start()

    def finish(self):
        self.join().wait()
        self.swap().wait_send()
        for a in range(3):
            for k in PEERS:
                self.share(a, k).wait_send()


class Collect:
    def __init__(self, me, dw, kept, got, total, fin, sems):
        self.me, self.dw, self.kept, self.got, self.fin, self.sems = me, dw, kept, got, fin, sems
        x = me[1]
        self.totals = (got, total)
        self.keep, self.pass_on = (x, 3 - x), (neighbour(x), 3 - neighbour(x))

    def second(self, j, at=slice(None)):
        zh, x, zl, y, c = self.me
        return remote(self.dw.at[self.pass_on[j], at], self.got.at[j, at], self.sems.at[0, 0, j], self.sems.at[1, 0, j],
                      (zh, neighbour(x), zl, y, c))

    def quarters(self, j):
        return [self.second(j, slice(192 * q, 192 * q + 192)) for q in range(4)]

    def third(self, i, j, n=None):
        zh, x, zl, y, c = self.me
        pair = div(x, 2)
        size = (D, 384)[i] // 2
        at = slice(None) if n is None else slice(n * size, n * size + size)
        src, dst = self.totals[i].at[j, at], self.fin[i].at[zh, at]
        copy = remote(src, dst, self.sems.at[2, i, j], self.sems.at[3, i, zh], (c, self.keep[j], zl, y, pair))
        local = pltpu.make_async_copy(src, dst, self.sems.at[3, i, zh])
        if j == 1:
            return copy, None, None
        return copy, local, jnp.logical_and(zh == c, pair == c)

    def load(self, j, sem):
        return pltpu.make_async_copy(self.dw.at[self.keep[j]], self.kept.at[j], sem)

    def add(self, j):
        self.second(j).wait_recv()
        self.got[j] = (self.kept[j].astype(F32) + self.got[j].astype(F32)).astype(BF16)

    def send(self, i, j, parts=(0, 1)):
        for n in parts:
            copy, local, own = self.third(i, j, n)
            if j == 1:
                copy.start()
            else:
                pl.when(own)(local.start)
                pl.when(jnp.logical_not(own))(copy.start)

    def finish(self):
        for j in range(2):
            self.second(j).wait_send()
        for i in range(2):
            for j in range(2):
                copy, _, own = self.third(i, j)
                if j == 1:
                    copy.wait_send()
                else:
                    pl.when(jnp.logical_not(own))(copy.wait_send)
            for b in range(2):
                await_bytes(self.fin[i].at[b], self.sems.at[3, i, b])


def rear_body(cot_ref, routes_ref, gain2_ref, gate_w_ref, tok_ref, gain1_ref,
              ret_in, gates_in, mid_in, att_in, w_o_in, qkv_in, ot_in, lse_in, w_qkv_in, y_in, dw_ref, total_ref,
              tok_grad_out, grads_out, early_ref, late_ref, out_out, fin_in, fin_out,
              ret_ref, gates_ref, mid_ref, att_ref, w_o_ref, qkv_ref, ot_ref, lse_ref, w_qkv_ref, y_ref, kept, out_ref, tok_grad_ref,
              dmid_ref, do_send, do_recv, dqkv_send, dqkv_recv, kt_ref, dk_ref, dv_ref, d_ref, datt_ref, got,
              s0, r0, a0, r1, a1, s2, r2, r3, whole, early, early_over, early_slots, late, late_over, late_slots,
              load_sems, save_sems, head_sems, collect_sems, group_sems, small_sems):
    me = coords()
    collect = Collect(me, dw_ref, kept, got, total_ref, (fin_in, fin_out), collect_sems)
    pairs = (
        (ret_in, ret_ref), (y_in, y_ref), (mid_in, mid_ref), (gates_in, gates_ref), (w_o_in, w_o_ref), (att_in, att_ref),
        (qkv_in, qkv_ref), (ot_in, ot_ref), (lse_in, lse_ref), (w_qkv_in, w_qkv_ref),
    )
    loads = [pltpu.make_async_copy(src, dst, load_sems.at[n]) for n, (src, dst) in enumerate(pairs)]
    loads += [collect.load(j, load_sems.at[10 + j]) for j in range(2)]
    for load in loads:
        load.start()
    _, greeted = hello((chip_partner, 16), (axis_partner, 7))
    heads = HeadSwap(me, do_send, do_recv, head_sems.at[0])
    heads_back = HeadSwap(me, dqkv_send, dqkv_recv, head_sems.at[1])
    bufs = (s0, r0, a0, r1, a1, s2, r2, r3, whole)
    orders = ((0, 1, 2), (1, 2, 0), (2, 0, 1), (1, 0, 2))
    groups = [GroupSum(me, g, orders[g], grads_out, bufs, group_sems) for g in range(4)]
    qkv_groups, o_group = groups[:3], groups[3]
    small = SmallSum(me, early, early_over, early_slots, early_ref, small_sems.at[0])
    small_late = SmallSum(me, late, late_over, late_slots, late_ref, small_sems.at[1])
    early[...] = jnp.zeros_like(early)
    late[...] = jnp.zeros_like(late)
    parts = [copy.start for j in range(2) for copy in collect.quarters(j)]

    def pump(n):
        for _ in range(min(n, len(parts))):
            parts.pop(0)()

    for load in loads[:5]:
        load.wait()
    enter(greeted)
    pump(2)
    collect.send(1, 0)
    later = back_body(ret_ref, y_ref, cot_ref, routes_ref, gates_ref, mid_ref, gain2_ref, gate_w_ref, w_o_ref,
                      do_send, dmid_ref, early.at[0:32], early.at[32:33], out_ref)
    heads.start()
    later()
    small.begin()
    datt_ref[...] = dmid_ref[...].astype(BF16)
    for load in loads[5:]:
        load.wait()
    o_group.begin(lambda n: dot(att_ref[...], datt_ref[:, half_rows(n)], 0, 0))
    saves = [pltpu.make_async_copy(out_ref, out_out, save_sems.at[0]), pltpu.make_async_copy(tok_grad_ref, tok_grad_out, save_sems.at[1])]
    saves[0].start()
    for t in range(BLOCKS):
        heads.arrived(t)
    small.step(0)
    o_group.step1()
    collect.send(1, 1)
    pump(2)

    attend_backward(rem(me[1], 2), qkv_ref, do_recv, ot_ref, lse_ref, dqkv_send, kt_ref, dk_ref, dv_ref,
                    lambda b: None, heads_back.leave, lambda pair: None)
    small.step(1)
    o_group.step2()
    pump(4)
    collect.add(0)
    collect.send(0, 0)
    unit, inv = norm(tok_ref[...].astype(F32))
    a1_rows = (unit * row_of(gain1_ref)).astype(BF16)
    for t in range(BLOCKS):
        heads_back.arrived(t)
    for part in range(3):
        tiles = unpair(
            [dqkv_recv[s, :, part * 128 : part * 128 + 128].astype(F32) for s in range(BLOCKS)]
        )
        for t in range(6):
            d_ref[part, :, 128 * t : 128 * t + 128] = tiles[t].astype(BF16)
        qkv_groups[part].begin(lambda n: dot(a1_rows, d_ref[part, :, half_rows(n)], 0, 0))
        if part:
            qkv_groups[part - 1].step1()
    small.step(2)
    o_group.step3()
    qkv_groups[2].step1()
    da1 = dot(d_ref[0], w_qkv_ref[:, 0:D], 1, 1)
    for part in (1, 2):
        da1 = da1 + dot(d_ref[part], w_qkv_ref[:, part * D : part * D + D], 1, 1)
    late[0:1] = jnp.sum(da1 * unit, axis=0, keepdims=True)
    small_late.begin()
    tok_grad_ref[...] = dmid_ref[...] + norm_back(da1, row_of(gain1_ref), unit, inv)
    saves[1].start()
    small.step(3)
    o_group.step4()
    small_late.step(0)
    for g in qkv_groups:
        g.step2()
    small_late.step(1)
    for g in qkv_groups:
        g.step3()
    collect.add(1)
    o_group.step5()
    small_late.step(2)
    for g in qkv_groups:
        g.step4()
    small_late.step(3)
    for g in qkv_groups:
        g.step5()
    collect.send(0, 1)
    o_group.step6()
    for g in qkv_groups:
        g.step6()
    small.finish()
    small_late.finish()
    heads.wait_send()
    heads_back.wait_send()
    collect.finish()
    for g in groups:
        g.finish()
    for save in saves:
        save.wait()


def rear(*args):
    buf = lambda *s: pltpu.VMEM(s, BF16)
    f32 = lambda *s: pltpu.VMEM(s, F32)
    return pl.pallas_call(
        rear_body,
        out_shape=[
            jax.ShapeDtypeStruct((ROWS, D), F32),
            jax.ShapeDtypeStruct((D, 4 * D), BF16),
            jax.ShapeDtypeStruct((48, D), BF16),
            jax.ShapeDtypeStruct((16, D), BF16),
            jax.ShapeDtypeStruct((ROWS, D), BF16),
            jax.ShapeDtypeStruct((2, D, 384), BF16),
            jax.ShapeDtypeStruct((2, 384, D), BF16),
        ],
        in_specs=[VMEM] * 6 + [ANY] * 12,
        out_specs=[ANY, ANY, VMEM, VMEM, ANY, ANY, ANY],
        scratch_shapes=[
            buf(SLOTS, D),
            f32(ROWS, 128),
            f32(ROWS, D),
            buf(ROWS, D),
            buf(D, D),
            buf(BLOCKS, ROWS, 384),
            f32(12, 64, ROWS),
            f32(12, 8, ROWS),
            buf(D, 3 * D),
            buf(SLOTS, D),
            buf(2, D, 384),
            buf(ROWS, D),
            f32(ROWS, D),
            f32(ROWS, D),
            buf(BLOCKS, ROWS, 128),
            buf(BLOCKS, ROWS, 128),
            buf(BLOCKS, ROWS, 384),
            buf(BLOCKS, ROWS, 384),
            buf(128, BLOCKS * ROWS),
            f32(BLOCKS * ROWS, 128),
            f32(BLOCKS * ROWS, 128),
            buf(3, ROWS, D),
            buf(ROWS, D),
            buf(2, D, 384),
            buf(4, D, 384),
            buf(4, D, 384),
            f32(4, D, 384),
            buf(4, 3, 192, 384),
            f32(4, 192, 384),
            buf(4, 192, 384),
            buf(4, 3, 48, 384),
            buf(4, 4, 48, 384),
            buf(4, D, 384),
            f32(48, D),
            buf(2, 48, 384),
            buf(3, 4, 48, 384),
            f32(16, D),
            buf(2, 16, 384),
            buf(3, 4, 16, 384),
            DMA((12,)),
            DMA((2,)),
            DMA((2, 2, 8)),
            DMA((4, 2, 2)),
            DMA((4, 7, 2, 4)),
            DMA((2, 2, 11)),
        ],
        compiler_params=remote_params(2),
    )(*args)


PIECES = 2


def results_body(frozen_ref, grads_ref, win_ref, wout_ref, tok_ref, out_ref, early_ref, late_ref,
                 qkv_grad, o_grad, win_grad, wout_grad, tok_grad, out, gain1_grad, gain2_grad, gate_grad):
    expert = (lax.axis_index("zl") * 4 + lax.axis_index("y")) * 4 + lax.axis_index("c") * 2
    qkv_grad[...] = grads_ref[:, : 3 * D].astype(F32)
    o_grad[...] = grads_ref[:, 3 * D :].astype(F32)
    for b in range(2):
        keep = (1 - frozen_ref[expert + b]).astype(F32)
        win_grad[b] = win_ref[b].astype(F32) * keep
        wout_grad[b] = wout_ref[b].astype(F32) * keep
    tok_grad[...] = tok_ref[...]
    out[...] = out_ref[...]

    @pl.when(pl.program_id(0) == 0)
    def _():
        gain1_grad[...] = late_ref[0:1].astype(F32).reshape(D)
        gain2_grad[...] = early_ref[32:33].astype(F32).reshape(D)
        gate = early_ref[0:32].astype(F32)
        for k in range(EXPERTS):
            gate_grad[k : k + 1] = gate[k : k + 1] * (1 - frozen_ref[k]).astype(F32)


def results(frozen, *args):
    n = PIECES
    whole = lambda *s: pl.BlockSpec(s, lambda i: (0,) * len(s))
    rows = lambda a, b: pl.BlockSpec((a // n, b), lambda i: (i, 0))
    slices = lambda a, b: pl.BlockSpec((2, a // n, b), lambda i: (0, i, 0))
    outs = [
        ((D, 3 * D), F32, rows(D, 3 * D)),
        ((D, D), F32, rows(D, D)),
        ((2, D, 384), F32, slices(D, 384)),
        ((2, 384, D), F32, slices(384, D)),
        ((ROWS, D), F32, rows(ROWS, D)),
        ((ROWS, D), BF16, rows(ROWS, D)),
        ((D,), F32, whole(D)),
        ((D,), F32, whole(D)),
        ((EXPERTS, D), F32, whole(EXPERTS, D)),
    ]
    return pl.pallas_call(
        results_body,
        grid=(n,),
        out_shape=[jax.ShapeDtypeStruct(s, t) for s, t, _ in outs],
        in_specs=[
            pl.BlockSpec(memory_space=pltpu.SMEM),
            rows(D, 4 * D),
            slices(D, 384),
            slices(384, D),
            rows(ROWS, D),
            rows(ROWS, D),
            whole(48, D),
            whole(16, D),
        ],
        out_specs=[m for _, _, m in outs],
        compiler_params=params(60),
    )(frozen, *args)


def on_device(tokens, cotangent, gain_first, w_qkv, w_o, gain_second, w_gate, w_in, w_out, routes, frozen):
    tok, cot, routes, gate_t = tokens[0], cotangent[0], routes[0].T, w_gate.T
    qkv, ret, y, mid, att, gates, ot, lse, dw_in, total_out = front(
        tok, cot, gain_first, w_qkv, w_o, gain_second, gate_t, routes, w_in, w_out
    )
    tok_grad, grads, early, late, out, w_in_grad, w_out_grad = rear(
        cot, routes, gain_second, gate_t, tok, gain_first, ret, gates, mid, att, w_o, qkv, ot, lse, w_qkv, y, dw_in, total_out
    )
    qkv_grad, o_grad, w_in_grad, w_out_grad, tok_grad, out, gain1_grad, gain2_grad, gate_grad = results(
        frozen, grads, w_in_grad, w_out_grad, tok_grad, out, early, late
    )
    return (
        out[None], tok_grad[None], gain1_grad, qkv_grad, o_grad, gain2_grad, gate_grad.T, w_in_grad, w_out_grad
    )


def solution(mesh):
    fine = Mesh(mesh.devices.reshape(2, 4, 2, 4, 2), ALL)
    seq, exp = ("zh", "x"), ("zl", "y", "c")
    rows, rest = P(exp, seq, None), P()
    in_specs = (rows, rows, rest, rest, rest, rest, rest, P(exp, None, seq), rows, rows, rest)
    out_specs = (rows, rows, rest, rest, rest, rest, rest, P(exp, None, seq), rows)
    return jax.shard_map(on_device, mesh=fine, in_specs=in_specs, out_specs=out_specs, check_vma=False)
```

```python
import functools
import math

import jax
import jax.numpy as jnp
from jax import lax
from jax.experimental import pallas as pl
from jax.experimental.pallas import tpu as pltpu
from jax.sharding import Mesh
from jax.sharding import PartitionSpec as P

D = 768
HEADS = 12
HEAD_DIM = 64
EXPERTS = 32
CAP = 32
ROWS = 256
BLOCKS = 8
FF = 3072
SLOTS = EXPERTS * CAP
EPS = 1e-5
SCALE = HEAD_DIM ** -0.5
LOG2E = math.log2(math.e)
BF16 = jnp.bfloat16
F32 = jnp.float32
NEG = -1e30

SEQ = ("zh", "x")
MESH = pl.DeviceIdType.MESH
ALL = ("zh", "x", "zl", "y", "c")


def dot(a, b, ca=1, cb=0):
    return lax.dot_general(a, b, (((ca,), (cb,)), ((), ())), preferred_element_type=F32)


def params(mb=56):
    return pltpu.CompilerParams(vmem_limit_bytes=mb * 2**20)


def vspec(n):
    return [pl.BlockSpec(memory_space=pltpu.VMEM)] * n


def call(body, outs, n_in, scratch=(), **kw):
    return pl.pallas_call(
        body,
        out_shape=[jax.ShapeDtypeStruct(s, t) for s, t in outs],
        in_specs=vspec(n_in),
        out_specs=vspec(len(outs)),
        scratch_shapes=list(scratch),
        compiler_params=params(),
        **kw,
    )


def norm(v):
    mean = jnp.mean(v, axis=-1, keepdims=True)
    centred = v - mean
    inv = lax.rsqrt(jnp.mean(centred * centred, axis=-1, keepdims=True) + EPS)
    return centred * inv, inv


def row_of(gain_ref):
    return gain_ref[...].reshape(1, D)


def norm_back(grad, gain, unit, inv):
    t = grad * gain
    m1 = jnp.mean(t, axis=-1, keepdims=True)
    m2 = jnp.mean(t * unit, axis=-1, keepdims=True)
    return inv * (t - m1 - unit * m2)


def lane_low():
    return lax.broadcasted_iota(jnp.int32, (1, 128), 1) < 64


def pair_up(wide, s):
    low = wide[:, 128 * (s // 2) : 128 * (s // 2) + 128]
    if s % 2:
        low = pltpu.roll(low, 64, 1)
    high = wide[:, 512 + 128 * (s // 4) : 640 + 128 * (s // 4)]
    if (s // 2) % 2 == 0:
        high = pltpu.roll(high, 64, 1)
    return jnp.where(lane_low(), low, high)


def unpair(tiles):
    out = []
    for t in range(4):
        out.append(
            jnp.where(lane_low(), tiles[2 * t], pltpu.roll(tiles[2 * t + 1], 64, 1))
        )
    for t in range(2):
        a = tiles[4 * t] + tiles[4 * t + 1]
        b = tiles[4 * t + 2] + tiles[4 * t + 3]
        out.append(jnp.where(lane_low(), pltpu.roll(a, 64, 1), b))
    return out


def project(tok_ref, gain_ref, part_weights, send_ref):
    unit, _ = norm(tok_ref[...].astype(F32))
    a1 = (unit * row_of(gain_ref)).astype(BF16)
    for part in range(3):
        wide = dot(a1, part_weights(part))
        for s in range(BLOCKS):
            send_ref[s, :, part * 128 : part * 128 + 128] = pair_up(wide, s).astype(
                BF16
            )


def unit_of(half, h, i):
    if h == 0:
        return 0, i, i + 1, i, i
    a, b = ((0, 1), (3, 2), (4, 5), (7, 6))[i]
    return 1, a + half * (b - a), 2 * i + 2, 2 * i, BLOCKS + i


def masked_scores(k, q, block, first, count):
    s = dot(k, q, 1, 1)
    start = first * ROWS
    tail = (count - first) * ROWS
    keys = lax.broadcasted_iota(jnp.int32, (tail, ROWS), 0) + start
    queries = lax.broadcasted_iota(jnp.int32, (tail, ROWS), 1) + block * ROWS
    end = jnp.where(keys <= queries, s[start:], NEG)
    return end if start == 0 else jnp.concatenate([s[:start], end], axis=0)


def head_mask(h):
    low = lane_low()
    return (low if h == 0 else jnp.logical_not(low)).astype(F32).astype(BF16)


def padded(h, t):
    zero = jnp.zeros_like(t)
    return jnp.concatenate([t, zero] if h == 0 else [zero, t], axis=0).T


def attend_forward(half, qkv_ref, o_ref, ot_ref, lse_ref, vt_ref, arrived, leave):
    c = SCALE * LOG2E
    for pair in range(BLOCKS // 2):
        for b in (2 * pair, 2 * pair + 1):
            arrived(b)
            vt_ref[:, b * ROWS : (b + 1) * ROWS] = qkv_ref[b, :, 256:384].T
            o_ref[b] = jnp.zeros((ROWS, 128), BF16)
        for unit in ((1, pair), (0, 2 * pair), (0, 2 * pair + 1)):
            h, block, count, first, u = unit_of(half, *unit)
            q = qkv_ref[block, :, 0:128] * head_mask(h)
            k = qkv_ref[0:count, :, 128:256].reshape(count * ROWS, 128)
            s = masked_scores(k, q, block, first, count)
            top = jnp.max(s, axis=0, keepdims=True)
            p = jnp.exp2((s - top) * c)
            total = jnp.sum(p, axis=0, keepdims=True)
            ot = dot(vt_ref[64 * h : 64 * h + 64, 0 : count * ROWS], p.astype(BF16))
            ot = ot / total
            ot_ref[u] = ot
            lse_ref[u] = jnp.broadcast_to(top * c + jnp.log2(total), (8, ROWS))
            o_ref[block] = (o_ref[block].astype(F32) + padded(h, ot)).astype(BF16)
        if pair % 2:
            leave(pair // 2)


def attend_backward(half, qkv_ref, do_ref, ot_ref, lse_ref, out_ref, kt_ref, dk_ref, dv_ref, arrived, leave, beside):
    c = SCALE * LOG2E
    for b in range(BLOCKS):
        kt_ref[:, b * ROWS : (b + 1) * ROWS] = qkv_ref[b, :, 128:256].T
        out_ref[b, :, 0:128] = jnp.zeros((ROWS, 128), BF16)
    dk_ref[...] = jnp.zeros_like(dk_ref)
    dv_ref[...] = jnp.zeros_like(dv_ref)

    def one(h, i):
        h, block, count, first, u = unit_of(half, h, i)
        rows = count * ROWS
        q = qkv_ref[block, :, 0:128] * head_mask(h)
        do = do_ref[block] * head_mask(h)
        dot_rows = do.astype(F32).T[64 * h : 64 * h + 64]
        delta = jnp.sum(dot_rows * ot_ref[u], axis=0, keepdims=True)
        lse = lse_ref[u][0:1]
        k = qkv_ref[0:count, :, 128:256].reshape(rows, 128)
        v = qkv_ref[0:count, :, 256:384].reshape(rows, 128)
        s = masked_scores(k, q, block, first, count)
        p = jnp.exp2(s * c - lse)
        dp = dot(v, do, 1, 1)
        ds = (p * (dp - delta)).astype(BF16)
        dv_ref[0:rows] += dot(p.astype(BF16), do)
        dk_ref[0:rows] += dot(ds, q)
        dqt = dot(kt_ref[64 * h : 64 * h + 64, 0:rows], ds) * SCALE
        out_ref[block, :, 0:128] = (
            out_ref[block, :, 0:128].astype(F32) + padded(h, dqt)
        ).astype(BF16)

    for pair in reversed(range(BLOCKS // 2)):
        b = 2 * pair + 1
        arrived(b)
        arrived(b - 1)
        one(1, pair)
        for b in (b, b - 1):
            one(0, b)
            at = slice(b * ROWS, (b + 1) * ROWS)
            out_ref[b, :, 128:256] = (dk_ref[at] * SCALE).astype(BF16)
            out_ref[b, :, 256:384] = dv_ref[at].astype(BF16)
        beside(pair)
        if pair % 2 == 0:
            leave(pair // 2)


def choices(routes):
    ids = lax.broadcasted_iota(jnp.int32, (ROWS, EXPERTS), 1).astype(F32)
    e1, e2 = [jnp.broadcast_to(routes[k : k + 1].astype(F32), (8, ROWS)).T[:, 0:1] for k in range(2)]
    m1, m2 = (e1 == ids).astype(F32), (e2 == ids).astype(F32)
    r = lax.broadcasted_iota(jnp.int32, (ROWS, ROWS), 0)
    k = lax.broadcasted_iota(jnp.int32, (ROWS, ROWS), 1)
    lower = (k < r).astype(F32).astype(BF16)
    earlier = dot(lower, (m1 + m2).astype(BF16))
    s1 = jnp.sum(earlier * m1, axis=1, keepdims=True)
    s2 = jnp.sum(earlier * m2, axis=1, keepdims=True)

    return m1, m2, e1 * CAP + s1, e2 * CAP + s2


def chosen(col):
    at = lax.broadcasted_iota(jnp.int32, (ROWS, SLOTS), 1).astype(F32)
    return (at == col).astype(F32).astype(BF16)


def chosen_t(col):
    row = jnp.broadcast_to(col, (ROWS, 128)).T[0:1]
    at = lax.broadcasted_iota(jnp.int32, (SLOTS, ROWS), 0).astype(F32)
    return (at == row).astype(F32).astype(BF16)


def deal_body(cot_ref, routes_ref, gates_ref, send_ref):
    _, _, c1, c2 = choices(routes_ref[...])
    c = cot_ref[...].astype(F32)
    first, second = (gates_ref[:, 0:1] * c).astype(BF16), (gates_ref[:, 1:2] * c).astype(BF16)
    send_ref[...] = (dot(chosen_t(c1), first) + dot(chosen_t(c2), second)).astype(BF16)


def middle_body(o_ref, tok_ref, w_o, gain_ref, gate_ref, routes_ref, mid_ref, att_ref, send_ref, gates_ref):
    tiles = unpair([o_ref[s].astype(F32) for s in range(BLOCKS)])
    o = jnp.concatenate([t.astype(BF16) for t in tiles], axis=1)
    att_ref[...] = o
    mid = tok_ref[...].astype(F32) + dot(o, w_o)
    mid_ref[...] = mid
    unit, _ = norm(mid)
    a2 = (unit * row_of(gain_ref)).astype(BF16)
    logits = dot(a2, gate_ref[...], 1, 1)
    m1, m2, c1, c2 = choices(routes_ref[...])
    l1 = jnp.sum(logits * m1, axis=1, keepdims=True)
    l2 = jnp.sum(logits * m2, axis=1, keepdims=True)
    top = jnp.maximum(l1, l2)
    x1, x2 = jnp.exp(l1 - top), jnp.exp(l2 - top)
    g1, g2 = x1 / (x1 + x2), x2 / (x1 + x2)
    lane = lax.broadcasted_iota(jnp.int32, (ROWS, 128), 1)
    gates_ref[...] = jnp.where(lane == 0, g1, g2)
    send_ref[...] = dot(chosen_t(c1) + chosen_t(c2), a2).astype(BF16)


def gelu_parts(h):
    t = pl.reciprocal(1.0 + (0.3275911 * 0.5**0.5) * jnp.abs(h), approx=True)
    e = jnp.exp2(h * h * (-0.5 * LOG2E))
    poly = t * (
        0.127414796
        + t * (-0.142248368 + t * (0.7107068705 + t * (-0.7265760135 + t * 0.5307027145)))
    )
    tail = poly * e
    phi = jnp.where(h >= 0, 1.0 - tail, tail)
    return h * phi, phi + h * e * (1.0 / math.sqrt(2.0 * math.pi))


def div(a, b):
    return lax.div(a, jnp.int32(b))


def rem(a, b):
    return lax.rem(a, jnp.int32(b))


def coords():
    return tuple(lax.axis_index(a) for a in ALL)


def near(x, pair):
    return x + rem(div(x, 2) + pair, 2) * (3 - 2 * x)


def neighbour(x):
    return x + 1 - 2 * rem(x, 2)


def expert_of(zh, x, zl, y):
    return 4 * (4 * zl + y) + 2 * div(x, 2) + zh


def remote(src, dst, send, recv, device):
    return pltpu.make_async_remote_copy(
        src_ref=src,
        dst_ref=dst,
        send_sem=send,
        recv_sem=recv,
        device_id=device,
        device_id_type=MESH,
    )


def await_bytes(ref, sem):
    pltpu.make_async_copy(ref, ref, sem).wait()


def chip_partner(me, k):
    zh, x, zl, y, c = me
    return (
        rem(zh + div(k, 8), 2),
        rem(x + rem(div(k, 2), 4), 4),
        zl,
        y,
        rem(c + rem(k, 2), 2),
    )


def core_partner(me, k):
    return me[:4] + (rem(me[4] + k, 2),)


def row_partner(me, k):
    zh, x, zl, y, c = me
    return (
        rem(zh + rem(div(k, 8), 2), 2),
        x + div(k, 16) * (3 - 2 * x),
        rem(zl + rem(div(k, 4), 2), 2),
        rem(y + rem(k, 4), 4),
        c,
    )


def head_partner(me, k):
    zh, x, zl, y, c = me
    t = rem(zh * 4 + x + k, 8)
    return t, (div(t, 4), rem(t, 4), zl, y, c)


def greet(me, partner, count):
    barrier = pltpu.get_barrier_semaphore()

    def one(k, carry):
        pl.semaphore_signal(
            barrier, inc=1, device_id=partner(me, k), device_id_type=MESH
        )
        return carry

    lax.fori_loop(1, count, one, 0)
    return count - 1


def hello(*groups):
    me = coords()
    return me, sum(greet(me, partner, count) for partner, count in groups)


def enter(total):
    pl.semaphore_wait(pltpu.get_barrier_semaphore(), total)


class HeadSwap:
    def __init__(self, me, send, recv, sems):
        self.me, self.send, self.recv, self.sems = me, send, recv, sems
        self.place = me[0] * 4 + me[1]

    def leave(self, half):
        s = self.place
        zh, x, zl, y, c = self.me
        for k in (2, 1, 3, 0):
            p = rem(x + k, 4)
            t = 4 * half + p
            away = remote(
                self.send.at[t], self.recv.at[s], self.sems.at[0, t], self.sems.at[1, s], (jnp.int32(half), p, zl, y, c)
            )
            if k:
                away.start()
            else:
                local = pltpu.make_async_copy(self.send.at[t], self.recv.at[t], self.sems.at[1, t])
                pl.when(zh == half)(local.start)
                pl.when(zh != half)(away.start)

    def start(self):
        s = self.place
        pltpu.make_async_copy(self.send.at[s], self.recv.at[s], self.sems.at[1, s]).start()
        for k in (2, 4, 6, 1, 3, 5, 7):
            t, device = head_partner(self.me, jnp.int32(k))
            remote(self.send.at[t], self.recv.at[s], self.sems.at[0, t], self.sems.at[1, s], device).start()

    def arrived(self, t):
        await_bytes(self.recv.at[t], self.sems.at[1, t])

    def wait_send(self):
        for k in range(1, 8):
            t, _ = head_partner(self.me, jnp.int32(k))
            await_bytes(self.send.at[t], self.sems.at[0, t])


class RowSwap:
    def __init__(self, me, send, recv, sems, back=False):
        self.me, self.send, self.recv, self.sems = me, send, recv, sems
        self.back = back

    def slot(self, kx, kz, ky):
        return 8 * rem(8 + ky - kz - 2 * kx, 4) + 4 * kx + kz

    def ends(self, k):
        zh, x, zl, y, c = self.me
        device = row_partner(self.me, k)
        kx, kz, ky = div(k, 16), rem(div(k, 4), 4), rem(k, 4)
        if self.back:
            src = self.slot(kx, kz, ky)
            dst = expert_of(zh, x, zl, y)
        else:
            src = expert_of(*device[:4])
            dst = self.slot(kx, kz, 4 - ky)
        rows = lambda n: pl.ds(pl.multiple_of(n * CAP, CAP), CAP)
        return self.send.at[rows(src)], self.recv.at[rows(dst)], device

    def start(self, first=0, last=32):
        if first == 0:
            src, dst, _ = self.ends(jnp.int32(0))
            pltpu.make_async_copy(src, dst, self.sems.at[1]).start()

        def one(k, carry):
            src, dst, device = self.ends(rem(9 * k, 32))
            remote(src, dst, self.sems.at[0], self.sems.at[1], device).start()
            return carry

        lax.fori_loop(max(first, 1), last, one, 0)

    def start_block(self, r):
        def one(n, carry):
            q = rem(3 * n, 8)
            kx, kz = div(q, 4), rem(q, 4)
            k = 16 * kx + 4 * kz + rem(r + kz + 2 * kx, 4)
            src, dst, device = self.ends(k)
            local = pltpu.make_async_copy(src, dst, self.sems.at[1])
            away = remote(src, dst, self.sems.at[0], self.sems.at[1], device)
            pl.when(k == 0)(local.start)
            pl.when(k != 0)(away.start)
            return carry

        lax.fori_loop(0, 8, one, 0)

    def wait_recv(self):
        await_bytes(self.recv, self.sems.at[1])

    def wait_send(self, first=0, last=31):
        await_bytes(self.send.at[pl.ds(0, (last - first) * CAP)], self.sems.at[0])

    def wait(self):
        self.wait_recv()
        self.wait_send()


def remote_params(n, mb=60):
    return pltpu.CompilerParams(
        vmem_limit_bytes=mb * 2**20, collective_id=n, has_side_effects=True
    )


VMEM = pl.BlockSpec(memory_space=pltpu.VMEM)
ANY = pl.BlockSpec(memory_space=pl.ANY)
DMA = pltpu.SemaphoreType.DMA


class Weights:
    def __init__(self, me, w_in, w_out, full_in, full_out, sems):
        self.me, self.refs, self.full, self.sems = me, (w_in, w_out), (full_in, full_out), sems

    def place(self, i, x, zh):
        at = pl.ds(pl.multiple_of(zh * 384, 128), 384)
        return self.full[0].at[x, :, at] if i == 0 else self.full[1].at[x, at, :]

    def first(self, i, b):
        zh, x, zl, y, c = self.me
        device = (jnp.int32(b), near(x, c), zl, y, zh)
        copy = remote(
            self.refs[i].at[b], self.place(i, x, zh), self.sems.at[0, i, b], self.sems.at[1, i, x], device
        )
        local = pltpu.make_async_copy(
            self.refs[i].at[b], self.place(i, x, zh), self.sems.at[1, i, x]
        )
        own = jnp.logical_and(
            jnp.logical_and(zh == b, div(x, 2) == c), zh == c
        )
        return copy, local, own

    def start(self, i):
        for b in range(2):
            copy, local, own = self.first(i, b)
            pl.when(own)(local.start)
            pl.when(jnp.logical_not(own))(copy.start)

    def forward(self, i, x, step):
        zh, me_x, zl, y, c = self.me
        piece = self.place(i, x, c)
        device = (zh, neighbour(me_x), zl, y, c) if step == 2 else (zh, me_x, zl, y, 1 - c)
        return remote(piece, piece, self.sems.at[2 * step - 2, i, x], self.sems.at[2 * step - 1, i, x], device)

    def sources(self, step):
        x = self.me[1]
        if step == 1:
            return x, 3 - x
        return neighbour(x), 3 - neighbour(x)

    def second(self, i):
        for x in self.sources(1):
            await_bytes(self.place(i, x, self.me[4]), self.sems.at[1, i, x])
            self.forward(i, x, 2).start()
            self.forward(i, x, 3).start()

    def third(self, i):
        for x in self.sources(2):
            self.forward(i, x, 2).wait_recv()
            self.forward(i, x, 3).start()

    def ready(self, i):
        for x in range(4):
            self.forward(i, jnp.int32(x), 3).wait_recv()

    def finish(self, i):
        for b in range(2):
            copy, _, own = self.first(i, b)
            pl.when(jnp.logical_not(own))(copy.wait_send)
        for x in self.sources(1):
            self.forward(i, x, 2).wait_send()
        for x in range(4):
            self.forward(i, jnp.int32(x), 3).wait_send()


STEP = 256
CHUNKS = 4
TILES = SLOTS // STEP


def row_block(r):
    return pl.ds(pl.multiple_of(r * STEP, STEP), STEP)


def half_rows(n):
    return pl.ds(pl.multiple_of(n * 384, 128), 384)


def front_body(tok_ref, cot_ref, gain1_ref, w_qkv_ref, w_o_ref, gain2_ref, gate_ref, routes_ref, w_in_ref, w_out_ref,
               qkv_out, ret_ref, y_ref, mid_out, att_out, gates_out, ot_out, lse_out, dwin_out, total_out,
               qkv_ref, mid_ref, att_ref, gates_ref, ot_ref, lse_ref, total_ref, xt_ref,
               qkv_send, o_send, o_recv, x_send, c_send, x_ref, c_ref, vt_ref, full_in, full_out, g_ref, d_ref,
               part_in, part_out, got_in, got_out, got2,
               head_sems, row_sems, weight_sems, load_sems, save_sems, core_sems, pair_sems):
    loads = [
        pltpu.make_async_copy(w_qkv_ref.at[:, p * D : p * D + D], g_ref.at[p, 0:D], load_sems.at[p]) for p in range(3)
    ] + [pltpu.make_async_copy(w_o_ref, g_ref.at[3, 0:D], load_sems.at[3])]
    me, greeted = hello((chip_partner, 16), (row_partner, 32))
    for load in loads:
        load.start()
    zh, x, zl, y, c = me
    weights = Weights(me, w_in_ref, w_out_ref, full_in, full_out, weight_sems)
    heads = HeadSwap(me, qkv_send, qkv_ref, head_sems.at[0])
    heads_back = HeadSwap(me, o_send, o_recv, head_sems.at[1])
    rows_c = RowSwap(me, c_send, c_ref, row_sems.at[0])
    rows_x = RowSwap(me, x_send, x_ref, row_sems.at[1])
    rows_ret = RowSwap(me, x_send, ret_ref, row_sems.at[2], back=True)
    rows_y = RowSwap(me, c_send, y_ref, row_sems.at[3], back=True)

    def part_weights(p):
        loads[p].wait()
        return g_ref[p, 0:D, :]

    project(tok_ref, gain1_ref, part_weights, qkv_send)
    enter(greeted)
    heads.start()
    weights.start(0)
    heads.arrived(0)
    heads.arrived(1)
    weights.start(1)
    attend_forward(
        rem(x, 2), qkv_ref, o_send, ot_ref, lse_ref, vt_ref,
        lambda b: heads.arrived(b) if b > 1 else None, heads_back.leave,
    )
    weights.second(0)
    for t in range(BLOCKS):
        heads_back.arrived(t)
    loads[3].wait()
    middle_body(o_recv, tok_ref, g_ref[3, 0:D, :], gain2_ref, gate_ref, routes_ref, mid_ref, att_ref, x_send, gates_ref)
    rows_x.start()
    saves = [
        pltpu.make_async_copy(src, dst, save_sems.at[n])
        for n, (src, dst) in enumerate(
            ((qkv_ref, qkv_out), (mid_ref, mid_out), (att_ref, att_out), (gates_ref, gates_out), (ot_ref, ot_out), (lse_ref, lse_out))
        )
    ]
    for save in saves:
        save.start()
    deal_body(cot_ref, routes_ref, gates_ref, c_send)
    weights.second(1)
    weights.third(0)
    rows_x.wait_send(0, 22)
    rows_c.start()
    weights.ready(0)
    rows_x.wait_recv()
    rows_x.wait_send(22, 31)

    def hidden(j):
        tiles = [slice(r * STEP, r * STEP + STEP) for r in range(TILES)]
        w = full_in[j]

        def after(at, h):
            g, d = gelu_parts(h)
            g_ref[j, at, :] = g.astype(BF16)
            d_ref[j, at, :] = d.astype(BF16)

        before = dot(x_ref[tiles[0], :], w)
        for r in range(1, TILES):
            h = dot(x_ref[tiles[r], :], w)
            after(tiles[r - 1], before)
            before = h
        after(tiles[-1], before)

    def hidden_loop(j, carry):
        @pl.when(j == CHUNKS - 1)
        def _():
            weights.third(1)

        hidden(j)
        return carry

    lax.fori_loop(0, CHUNKS, hidden_loop, 0)
    for r in range(TILES):
        xt_ref[:, r * STEP : (r + 1) * STEP] = x_ref[r * STEP : (r + 1) * STEP, :].T
    weights.ready(1)
    rows_c.wait()

    def produce(n, carry):
        r = TILES - 1 - n
        at = row_block(r)
        out = dot(g_ref[0, at, :], full_out[0])
        for j in range(1, CHUNKS):
            out = out + dot(g_ref[j, at, :], full_out[j])
        c_send[at, :] = out.astype(BF16)
        rows_y.start_block(r)
        return carry

    lax.fori_loop(0, TILES, produce, 0)

    sibling = core_partner(me, 1)

    def half(i, j, n):
        return part_in.at[j, :, half_rows(n)] if i == 0 else part_out.at[j, half_rows(n), :]

    def over(i, j):
        got = (got_in, got_out)[i]
        return remote(half(i, j, 1 - c), got.at[j], core_sems.at[0, i, j], core_sems.at[1, i, j], sibling)

    def second_grad(j, carry):
        part_out[j] = dot(g_ref[j], c_ref[...], 0, 0).astype(BF16)
        over(1, j).start()
        return carry

    lax.fori_loop(0, CHUNKS, second_grad, 0)

    def second_sum(j, carry):
        over(1, j).wait()
        got_out[j] = (half(1, j, c)[...].astype(F32) + got_out[j].astype(F32)).astype(BF16)
        return carry

    lax.fori_loop(0, CHUNKS, second_sum, 0)
    pass_on, keep = (neighbour(x), 3 - neighbour(x)), (x, 3 - x)

    def pair_over(n):
        return remote(got_out.at[pass_on[n]], got2.at[n], pair_sems.at[0, n], pair_sems.at[1, n], (zh, neighbour(x), zl, y, c))

    for n in range(2):
        pair_over(n).start()

    def back(n, carry):
        r = TILES - 1 - n
        at = row_block(r)
        dx = jnp.zeros((STEP, D), F32)
        for j in range(CHUNKS):
            cw = dot(c_ref[at, :], full_out[j], 1, 1)
            dh = (d_ref[j, at, :].astype(F32) * cw).astype(BF16)
            d_ref[j, at, :] = dh
            dx = dx + dot(dh, full_in[j], 1, 1)
        x_send[at, :] = dx.astype(BF16)
        rows_ret.start_block(r)
        return carry

    lax.fori_loop(0, TILES, back, 0)

    def first_grad(n, carry):
        j, r = div(n, 3), rem(n, 3)
        part_in[j, row_block(r), :] = dot(xt_ref[row_block(r), :], d_ref[j]).astype(BF16)

        @pl.when(r == 2)
        def _():
            over(0, j).start()

        return carry

    lax.fori_loop(0, 3 * CHUNKS, first_grad, 0)

    def first_save(j):
        return pltpu.make_async_copy(got_in.at[j], dwin_out.at[j], save_sems.at[7])

    def first_sum(j, carry):
        over(0, j).wait()
        got_in[j] = (half(0, j, c)[...].astype(F32) + got_in[j].astype(F32)).astype(BF16)
        first_save(j).start()
        return carry

    lax.fori_loop(0, CHUNKS, first_sum, 0)
    heads.wait_send()
    heads_back.wait_send()
    weights.finish(0)
    weights.finish(1)
    for n in range(2):
        pair_over(n).wait()
        total_ref[n] = (got_out[keep[n]].astype(F32) + got2[n].astype(F32)).astype(BF16)
    last = pltpu.make_async_copy(total_ref, total_out, save_sems.at[6])
    last.start()
    for save in saves:
        save.wait()
    rows_y.wait()
    rows_ret.wait()
    last.wait()
    await_bytes(dwin_out, save_sems.at[7])


def front(tok, cot, gain1, w_qkv, w_o, gain2, gate, routes, w_in, w_out):
    buf = lambda *s: pltpu.VMEM(s, BF16)
    f32 = lambda *s: pltpu.VMEM(s, F32)
    outs = [
        ((BLOCKS, ROWS, 384), BF16),
        ((SLOTS, D), BF16),
        ((SLOTS, D), BF16),
        ((ROWS, D), F32),
        ((ROWS, D), BF16),
        ((ROWS, 128), F32),
        ((12, 64, ROWS), F32),
        ((12, 8, ROWS), F32),
        ((CHUNKS, D, 384), BF16),
        ((2, 384, D), BF16),
    ]
    return pl.pallas_call(
        front_body,
        out_shape=[jax.ShapeDtypeStruct(s, t) for s, t in outs],
        in_specs=[VMEM] * 3 + [ANY] * 2 + [VMEM] * 3 + [ANY] * 2,
        out_specs=[ANY] * len(outs),
        scratch_shapes=[
            buf(BLOCKS, ROWS, 384),
            f32(ROWS, D),
            buf(ROWS, D),
            f32(ROWS, 128),
            f32(12, 64, ROWS),
            f32(12, 8, ROWS),
            buf(2, 384, D),
            buf(D, SLOTS),
            buf(BLOCKS, ROWS, 384),
            buf(BLOCKS, ROWS, 128),
            buf(BLOCKS, ROWS, 128),
            buf(SLOTS, D),
            buf(SLOTS, D),
            buf(SLOTS, D),
            buf(SLOTS, D),
            buf(128, BLOCKS * ROWS),
            buf(CHUNKS, D, D),
            buf(CHUNKS, D, D),
            buf(CHUNKS, SLOTS, D),
            buf(CHUNKS, SLOTS, D),
            buf(CHUNKS, D, D),
            buf(CHUNKS, D, D),
            buf(CHUNKS, D, 384),
            buf(CHUNKS, 384, D),
            buf(2, 384, D),
            DMA((2, 2, 8)),
            DMA((4, 2)),
            DMA((6, 2, 4)),
            DMA((4,)),
            DMA((8,)),
            DMA((2, 2, 4)),
            DMA((2, 2)),
        ],
        compiler_params=remote_params(0, 63),
    )(tok, cot, gain1, w_qkv, w_o, gain2, gate, routes, w_in, w_out)


def back_body(ret_ref, y_ref, cot_ref, routes_ref, gates_ref, mid_ref, gain_ref, gate_w_ref, w_o_ref,
              send_ref, dmid_ref, gate_grad_ref, gain_grad_ref, out_ref):
    m1, m2, c1, c2 = choices(routes_ref[...])
    s1, s2 = chosen(c1), chosen(c2)
    g1, g2 = gates_ref[:, 0:1], gates_ref[:, 1:2]
    y = y_ref[...]
    c, y1, y2 = cot_ref[...].astype(F32), dot(s1, y), dot(s2, y)
    dl = g1 * g2 * jnp.sum(c * (y1 - y2), axis=1, keepdims=True)
    dlogits = (m1 - m2) * dl
    unit, inv = norm(mid_ref[...])
    high = dlogits.astype(BF16)
    low = (dlogits - high.astype(F32)).astype(BF16)
    gate_w = gate_w_ref[...]
    da2 = dot(s1 + s2, ret_ref[...]) + dot(high, gate_w) + dot(low, gate_w)
    dmid = c + norm_back(da2, row_of(gain_ref), unit, inv)
    dmid_ref[...] = dmid
    do = dot(dmid.astype(BF16), w_o_ref[...], 1, 1)
    for s in range(BLOCKS):
        send_ref[s] = pair_up(do, s).astype(BF16)

    def later():
        a2 = (unit * row_of(gain_ref)).astype(BF16)
        gate_grad_ref[...] = dot(high, a2, 0, 0) + dot(low, a2, 0, 0)
        gain_grad_ref[...] = jnp.sum(da2 * unit, axis=0, keepdims=True)
        out_ref[...] = (mid_ref[...] + (g1 * y1 + g2 * y2)).astype(BF16)

    return later


def axis_place(me, a):
    zh, x, zl, y, c = me
    return (x, y, 2 * zh + zl)[a]


def axis_peer(me, a, k):
    zh, x, zl, y, c = me
    p = rem(axis_place(me, a) + k, 4)
    if a == 0:
        return p, (zh, p, zl, y, c)
    if a == 1:
        return p, (zh, x, zl, p, c)
    return p, (div(p, 2), x, rem(p, 2), y, c)


def axis_partner(me, k):
    zh, x, zl, y, c = me
    along_z = div(k, 4)
    dz = rem(k + 1, 4) * along_z
    z = rem(2 * zh + zl + dz, 4)
    return div(z, 2), x, rem(z, 2), rem(y + k * (1 - along_z), 4), c


def multiple(n, w):
    return pl.ds(pl.multiple_of(n * w, w), w)


PEERS = (1, 2, 3)


class GroupSum:
    def __init__(self, me, g, axes, out, bufs, sems):
        self.me, self.g, self.axes, self.out, self.sems = me, g, axes, out, sems.at[g]
        self.s0, self.r0, self.a0, self.r1, self.a1, self.s2, self.r2, self.r3, self.whole = [b.at[g] for b in bufs]
        self.place = [axis_place(me, a) for a in axes]
        self.c = me[4]

    def copy(self, stage, k, src, dst):
        if stage in (0, 6):
            device = core_partner(self.me, 1)
        else:
            device = axis_peer(self.me, self.axes[(0, 0, 1, 2, 1, 0)[stage]], jnp.int32(k))[1]
        return remote(src, dst, self.sems.at[stage, 0, k], self.sems.at[stage, 1, k], device)

    def peer(self, t, k):
        return axis_peer(self.me, self.axes[t], jnp.int32(k))[0]

    def swap(self):
        return self.copy(0, 0, self.s0, self.r0)

    def scatter1(self, k):
        return self.copy(1, k, self.s0.at[multiple(self.peer(0, k), 192)], self.r1.at[k - 1])

    def scatter2(self, k):
        return self.copy(2, k, self.s2.at[multiple(self.peer(1, k), 48)], self.r2.at[k - 1])

    def share(self, k):
        mine = self.r3.at[self.place[2]]
        return self.copy(3, k, mine, mine)

    def block(self, rows):
        i, j = self.place[0], self.place[1]
        if rows == 48:
            return self.whole.at[multiple(4 * i + j, 48)]
        if rows == 192:
            return self.whole.at[multiple(i, 192)]
        return self.whole

    def gather(self, stage, k):
        ref = self.block((48, 192, 768)[stage - 4])
        if stage < 6:
            return self.copy(stage, k, ref, ref)
        lanes = pl.ds(pl.multiple_of(self.g * D + self.c * 384, 128), 384)
        return self.copy(stage, k, ref, self.out.at[:, lanes])

    def save(self):
        lanes = pl.ds(pl.multiple_of(self.g * D + self.c * 384, 128), 384)
        return pltpu.make_async_copy(self.whole, self.out.at[:, lanes], self.sems.at[6, 0, 1])

    def begin(self, grad):
        self.s0[...] = grad(1 - self.c).astype(BF16)
        self.swap().start()
        self.a0[...] = grad(self.c)

    def step1(self):
        self.swap().wait()
        self.a0[...] += self.r0[...].astype(F32)
        self.s0[...] = self.a0[...].astype(BF16)
        for k in PEERS:
            self.scatter1(k).start()

    def step2(self):
        for k in PEERS:
            self.scatter1(k).wait_recv()
        mine = self.a0[multiple(self.place[0], 192), :]
        for k in PEERS:
            mine = mine + self.r1[k - 1].astype(F32)
        self.a1[...] = mine
        self.s2[...] = mine.astype(BF16)
        for k in PEERS:
            self.scatter2(k).start()

    def step3(self):
        for k in PEERS:
            self.scatter2(k).wait_recv()
        mine = self.a1[multiple(self.place[1], 48), :]
        for k in PEERS:
            mine = mine + self.r2[k - 1].astype(F32)
        self.r3[self.place[2]] = mine.astype(BF16)
        for k in PEERS:
            self.share(k).start()

    def step4(self):
        for k in PEERS:
            p = axis_peer(self.me, self.axes[2], jnp.int32(k))[0]
            self.copy(3, 4 - k, self.r3.at[p], self.r3.at[p]).wait_recv()
        total = (self.r3[0].astype(F32) + self.r3[1].astype(F32)) + (
            self.r3[2].astype(F32) + self.r3[3].astype(F32)
        )
        self.block(48)[...] = total.astype(BF16)
        for k in PEERS:
            self.gather(4, k).start()

    def step5(self):
        for k in PEERS:
            self.gather(4, k).wait_recv()
        for k in PEERS:
            self.gather(5, k).start()

    def step6(self):
        for k in PEERS:
            self.gather(5, k).wait_recv()
        self.gather(6, 0).start()
        self.save().start()

    def finish(self):
        self.gather(6, 0).wait()
        self.save().wait()
        for k in PEERS:
            self.scatter1(k).wait_send()
            self.scatter2(k).wait_send()
            self.share(k).wait_send()
            self.gather(4, k).wait_send()
            self.gather(5, k).wait_send()


class SmallSum:
    def __init__(self, me, mine, over, slots, out, sems):
        self.me, self.mine, self.over, self.slots, self.out, self.sems = me, mine, over, slots, out, sems

    def half(self, ref, n):
        return ref.at[:, half_rows(n)]

    def swap(self):
        return remote(self.over.at[0], self.over.at[1], self.sems.at[0, 0], self.sems.at[1, 0], core_partner(self.me, 1))

    def share(self, a, k):
        n = 3 * a + k
        mine = self.slots.at[a, axis_place(self.me, a)]
        return remote(mine, mine, self.sems.at[0, n], self.sems.at[1, n], axis_peer(self.me, a, jnp.int32(k))[1])

    def join(self):
        mine = self.half(self.out, self.me[4])
        return remote(mine, mine, self.sems.at[0, 10], self.sems.at[1, 10], core_partner(self.me, 1))

    def begin(self):
        self.over[0] = self.half(self.mine, 1 - self.me[4])[...].astype(BF16)
        self.swap().start()

    def step(self, a):
        if a == 0:
            self.swap().wait_recv()
            total = self.half(self.mine, self.me[4])[...] + self.over[1].astype(F32)
        else:
            for k in PEERS:
                self.share(a - 1, k).wait_recv()
            s = [self.slots[a - 1, p].astype(F32) for p in range(4)]
            total = (s[0] + s[1]) + (s[2] + s[3])
        if a < 3:
            self.slots[a, axis_place(self.me, a)] = total.astype(BF16)
            for k in PEERS:
                self.share(a, k).start()
        else:
            self.half(self.out, self.me[4])[...] = total.astype(BF16)
            self.join().start()

    def finish(self):
        self.join().wait()
        self.swap().wait_send()
        for a in range(3):
            for k in PEERS:
                self.share(a, k).wait_send()


class Collect:
    def __init__(self, me, dw, kept, got, total, fin, sems):
        self.me, self.dw, self.kept, self.got, self.fin, self.sems = me, dw, kept, got, fin, sems
        x = me[1]
        self.totals = (got, total)
        self.keep, self.pass_on = (x, 3 - x), (neighbour(x), 3 - neighbour(x))

    def second(self, j, at=slice(None)):
        zh, x, zl, y, c = self.me
        return remote(self.dw.at[self.pass_on[j], at], self.got.at[j, at], self.sems.at[0, 0, j], self.sems.at[1, 0, j],
                      (zh, neighbour(x), zl, y, c))

    def quarters(self, j):
        return [self.second(j, slice(192 * q, 192 * q + 192)) for q in range(4)]

    def third(self, i, j, n=None):
        zh, x, zl, y, c = self.me
        pair = div(x, 2)
        size = (D, 384)[i] // 2
        at = slice(None) if n is None else slice(n * size, n * size + size)
        src, dst = self.totals[i].at[j, at], self.fin[i].at[zh, at]
        copy = remote(src, dst, self.sems.at[2, i, j], self.sems.at[3, i, zh], (c, self.keep[j], zl, y, pair))
        local = pltpu.make_async_copy(src, dst, self.sems.at[3, i, zh])
        if j == 1:
            return copy, None, None
        return copy, local, jnp.logical_and(zh == c, pair == c)

    def load(self, j, sem):
        return pltpu.make_async_copy(self.dw.at[self.keep[j]], self.kept.at[j], sem)

    def add(self, j):
        self.second(j).wait_recv()
        self.got[j] = (self.kept[j].astype(F32) + self.got[j].astype(F32)).astype(BF16)

    def send(self, i, j, parts=(0, 1)):
        for n in parts:
            copy, local, own = self.third(i, j, n)
            if j == 1:
                copy.start()
            else:
                pl.when(own)(local.start)
                pl.when(jnp.logical_not(own))(copy.start)

    def finish(self):
        for j in range(2):
            self.second(j).wait_send()
        for i in range(2):
            for j in range(2):
                copy, _, own = self.third(i, j)
                if j == 1:
                    copy.wait_send()
                else:
                    pl.when(jnp.logical_not(own))(copy.wait_send)
            for b in range(2):
                await_bytes(self.fin[i].at[b], self.sems.at[3, i, b])


def rear_body(cot_ref, routes_ref, gain2_ref, gate_w_ref, tok_ref, gain1_ref,
              ret_in, gates_in, mid_in, att_in, w_o_in, qkv_in, ot_in, lse_in, w_qkv_in, y_in, dw_ref, total_ref,
              tok_grad_out, grads_out, early_ref, late_ref, out_out, fin_in, fin_out,
              ret_ref, gates_ref, mid_ref, att_ref, w_o_ref, qkv_ref, ot_ref, lse_ref, w_qkv_ref, y_ref, kept, out_ref, tok_grad_ref,
              dmid_ref, do_send, do_recv, dqkv_send, dqkv_recv, kt_ref, dk_ref, dv_ref, d_ref, datt_ref, got,
              s0, r0, a0, r1, a1, s2, r2, r3, whole, early, early_over, early_slots, late, late_over, late_slots,
              load_sems, save_sems, head_sems, collect_sems, group_sems, small_sems):
    me, greeted = hello((chip_partner, 16), (axis_partner, 7))
    collect = Collect(me, dw_ref, kept, got, total_ref, (fin_in, fin_out), collect_sems)
    pairs = (
        (ret_in, ret_ref), (y_in, y_ref), (mid_in, mid_ref), (gates_in, gates_ref), (w_o_in, w_o_ref), (att_in, att_ref),
        (qkv_in, qkv_ref), (ot_in, ot_ref), (lse_in, lse_ref), (w_qkv_in, w_qkv_ref),
    )
    loads = [pltpu.make_async_copy(src, dst, load_sems.at[n]) for n, (src, dst) in enumerate(pairs)]
    loads += [collect.load(j, load_sems.at[10 + j]) for j in range(2)]
    for load in loads:
        load.start()
    heads = HeadSwap(me, do_send, do_recv, head_sems.at[0])
    heads_back = HeadSwap(me, dqkv_send, dqkv_recv, head_sems.at[1])
    bufs = (s0, r0, a0, r1, a1, s2, r2, r3, whole)
    orders = ((1, 0, 2), (1, 2, 0), (2, 1, 0), (1, 0, 2))
    groups = [GroupSum(me, g, orders[g], grads_out, bufs, group_sems) for g in range(4)]
    qkv_groups, o_group = groups[:3], groups[3]
    small = SmallSum(me, early, early_over, early_slots, early_ref, small_sems.at[0])
    small_late = SmallSum(me, late, late_over, late_slots, late_ref, small_sems.at[1])
    early[...] = jnp.zeros_like(early)
    late[...] = jnp.zeros_like(late)
    parts = [copy.start for j in range(2) for copy in collect.quarters(j)]

    def pump(n):
        for _ in range(min(n, len(parts))):
            parts.pop(0)()

    for load in loads[:5]:
        load.wait()
    enter(greeted)
    pump(2)
    collect.send(1, 0)
    later = back_body(ret_ref, y_ref, cot_ref, routes_ref, gates_ref, mid_ref, gain2_ref, gate_w_ref, w_o_ref,
                      do_send, dmid_ref, early.at[0:32], early.at[32:33], out_ref)
    heads.start()
    later()
    small.begin()
    datt_ref[...] = dmid_ref[...].astype(BF16)
    for load in loads[5:]:
        load.wait()
    o_group.begin(lambda n: dot(att_ref[...], datt_ref[:, half_rows(n)], 0, 0))
    saves = [pltpu.make_async_copy(out_ref, out_out, save_sems.at[0]), pltpu.make_async_copy(tok_grad_ref, tok_grad_out, save_sems.at[1])]
    saves[0].start()
    for t in range(BLOCKS):
        heads.arrived(t)
    small.step(0)
    o_group.step1()
    pump(2)

    attend_backward(rem(me[1], 2), qkv_ref, do_recv, ot_ref, lse_ref, dqkv_send, kt_ref, dk_ref, dv_ref,
                    lambda b: None, heads_back.leave, lambda pair: None)
    small.step(1)
    o_group.step2()
    collect.send(1, 1)
    pump(4)
    collect.add(0)
    unit, inv = norm(tok_ref[...].astype(F32))
    a1_rows = (unit * row_of(gain1_ref)).astype(BF16)
    for t in range(BLOCKS):
        heads_back.arrived(t)
    for part in range(3):
        tiles = unpair(
            [dqkv_recv[s, :, part * 128 : part * 128 + 128].astype(F32) for s in range(BLOCKS)]
        )
        for t in range(6):
            d_ref[part, :, 128 * t : 128 * t + 128] = tiles[t].astype(BF16)
        qkv_groups[part].begin(lambda n: dot(a1_rows, d_ref[part, :, half_rows(n)], 0, 0))
        if part:
            qkv_groups[part - 1].step1()
    small.step(2)
    o_group.step3()
    qkv_groups[2].step1()
    collect.send(0, 0)
    da1 = dot(d_ref[0], w_qkv_ref[:, 0:D], 1, 1)
    for part in (1, 2):
        da1 = da1 + dot(d_ref[part], w_qkv_ref[:, part * D : part * D + D], 1, 1)
    late[0:1] = jnp.sum(da1 * unit, axis=0, keepdims=True)
    small_late.begin()
    tok_grad_ref[...] = dmid_ref[...] + norm_back(da1, row_of(gain1_ref), unit, inv)
    saves[1].start()
    small.step(3)
    o_group.step4()
    small_late.step(0)
    for g in qkv_groups:
        g.step2()
    small_late.step(1)
    for g in qkv_groups:
        g.step3()
    collect.add(1)
    o_group.step5()
    small_late.step(2)
    for g in qkv_groups:
        g.step4()
    small_late.step(3)
    for g in qkv_groups:
        g.step5()
    collect.send(0, 1)
    o_group.step6()
    for g in qkv_groups:
        g.step6()
    small.finish()
    small_late.finish()
    heads.wait_send()
    heads_back.wait_send()
    collect.finish()
    for g in groups:
        g.finish()
    for save in saves:
        save.wait()


def rear(*args):
    buf = lambda *s: pltpu.VMEM(s, BF16)
    f32 = lambda *s: pltpu.VMEM(s, F32)
    return pl.pallas_call(
        rear_body,
        out_shape=[
            jax.ShapeDtypeStruct((ROWS, D), F32),
            jax.ShapeDtypeStruct((D, 4 * D), BF16),
            jax.ShapeDtypeStruct((48, D), BF16),
            jax.ShapeDtypeStruct((16, D), BF16),
            jax.ShapeDtypeStruct((ROWS, D), BF16),
            jax.ShapeDtypeStruct((2, D, 384), BF16),
            jax.ShapeDtypeStruct((2, 384, D), BF16),
        ],
        in_specs=[VMEM] * 6 + [ANY] * 12,
        out_specs=[ANY, ANY, VMEM, VMEM, ANY, ANY, ANY],
        scratch_shapes=[
            buf(SLOTS, D),
            f32(ROWS, 128),
            f32(ROWS, D),
            buf(ROWS, D),
            buf(D, D),
            buf(BLOCKS, ROWS, 384),
            f32(12, 64, ROWS),
            f32(12, 8, ROWS),
            buf(D, 3 * D),
            buf(SLOTS, D),
            buf(2, D, 384),
            buf(ROWS, D),
            f32(ROWS, D),
            f32(ROWS, D),
            buf(BLOCKS, ROWS, 128),
            buf(BLOCKS, ROWS, 128),
            buf(BLOCKS, ROWS, 384),
            buf(BLOCKS, ROWS, 384),
            buf(128, BLOCKS * ROWS),
            f32(BLOCKS * ROWS, 128),
            f32(BLOCKS * ROWS, 128),
            buf(3, ROWS, D),
            buf(ROWS, D),
            buf(2, D, 384),
            buf(4, D, 384),
            buf(4, D, 384),
            f32(4, D, 384),
            buf(4, 3, 192, 384),
            f32(4, 192, 384),
            buf(4, 192, 384),
            buf(4, 3, 48, 384),
            buf(4, 4, 48, 384),
            buf(4, D, 384),
            f32(48, D),
            buf(2, 48, 384),
            buf(3, 4, 48, 384),
            f32(16, D),
            buf(2, 16, 384),
            buf(3, 4, 16, 384),
            DMA((12,)),
            DMA((2,)),
            DMA((2, 2, 8)),
            DMA((4, 2, 2)),
            DMA((4, 7, 2, 4)),
            DMA((2, 2, 11)),
        ],
        compiler_params=remote_params(2),
    )(*args)


PIECES = 2


def results_body(frozen_ref, grads_ref, win_ref, wout_ref, tok_ref, out_ref, early_ref, late_ref,
                 qkv_grad, o_grad, win_grad, wout_grad, tok_grad, out, gain1_grad, gain2_grad, gate_grad):
    expert = (lax.axis_index("zl") * 4 + lax.axis_index("y")) * 4 + lax.axis_index("c") * 2
    qkv_grad[...] = grads_ref[:, : 3 * D].astype(F32)
    o_grad[...] = grads_ref[:, 3 * D :].astype(F32)
    for b in range(2):
        keep = (1 - frozen_ref[expert + b]).astype(F32)
        win_grad[b] = win_ref[b].astype(F32) * keep
        wout_grad[b] = wout_ref[b].astype(F32) * keep
    tok_grad[...] = tok_ref[...]
    out[...] = out_ref[...]

    @pl.when(pl.program_id(0) == 0)
    def _():
        gain1_grad[...] = late_ref[0:1].astype(F32).reshape(D)
        gain2_grad[...] = early_ref[32:33].astype(F32).reshape(D)
        gate = early_ref[0:32].astype(F32)
        for k in range(EXPERTS):
            gate_grad[k : k + 1] = gate[k : k + 1] * (1 - frozen_ref[k]).astype(F32)


def results(frozen, *args):
    n = PIECES
    whole = lambda *s: pl.BlockSpec(s, lambda i: (0,) * len(s))
    rows = lambda a, b: pl.BlockSpec((a // n, b), lambda i: (i, 0))
    slices = lambda a, b: pl.BlockSpec((2, a // n, b), lambda i: (0, i, 0))
    outs = [
        ((D, 3 * D), F32, rows(D, 3 * D)),
        ((D, D), F32, rows(D, D)),
        ((2, D, 384), F32, slices(D, 384)),
        ((2, 384, D), F32, slices(384, D)),
        ((ROWS, D), F32, rows(ROWS, D)),
        ((ROWS, D), BF16, rows(ROWS, D)),
        ((D,), F32, whole(D)),
        ((D,), F32, whole(D)),
        ((EXPERTS, D), F32, whole(EXPERTS, D)),
    ]
    return pl.pallas_call(
        results_body,
        grid=(n,),
        out_shape=[jax.ShapeDtypeStruct(s, t) for s, t, _ in outs],
        in_specs=[
            pl.BlockSpec(memory_space=pltpu.SMEM),
            rows(D, 4 * D),
            slices(D, 384),
            slices(384, D),
            rows(ROWS, D),
            rows(ROWS, D),
            whole(48, D),
            whole(16, D),
        ],
        out_specs=[m for _, _, m in outs],
        compiler_params=params(60),
    )(frozen, *args)


def on_device(tokens, cotangent, gain_first, w_qkv, w_o, gain_second, w_gate, w_in, w_out, routes, frozen):
    tok, cot, routes, gate_t = tokens[0], cotangent[0], routes[0].T, w_gate.T
    qkv, ret, y, mid, att, gates, ot, lse, dw_in, total_out = front(
        tok, cot, gain_first, w_qkv, w_o, gain_second, gate_t, routes, w_in, w_out
    )
    tok_grad, grads, early, late, out, w_in_grad, w_out_grad = rear(
        cot, routes, gain_second, gate_t, tok, gain_first, ret, gates, mid, att, w_o, qkv, ot, lse, w_qkv, y, dw_in, total_out
    )
    qkv_grad, o_grad, w_in_grad, w_out_grad, tok_grad, out, gain1_grad, gain2_grad, gate_grad = results(
        frozen, grads, w_in_grad, w_out_grad, tok_grad, out, early, late
    )
    return (
        out[None], tok_grad[None], gain1_grad, qkv_grad, o_grad, gain2_grad, gate_grad.T, w_in_grad, w_out_grad
    )


def solution(mesh):
    fine = Mesh(mesh.devices.reshape(2, 4, 2, 4, 2), ALL)
    seq, exp = ("zh", "x"), ("zl", "y", "c")
    rows, rest = P(exp, seq, None), P()
    in_specs = (rows, rows, rest, rest, rest, rest, rest, P(exp, None, seq), rows, rows, rest)
    out_specs = (rows, rows, rest, rest, rest, rest, rest, P(exp, None, seq), rows)
    return jax.shard_map(on_device, mesh=fine, in_specs=in_specs, out_specs=out_specs, check_vma=False)
```
